32 devices in a mesh: dp: 8 (over z, x), tensor: 4 (over y, core).
Axes of the slice: x: 2, y: 2, z: 4, core: 2. Of those that a mesh axis runs over, the one named last changes fastest.
Arguments:
- inputs: bfloat16 [16384, 1536], P(('dp', 'tensor')), may hold values from -6 to 6
- cotangent: bfloat16 [16384, 1536], P(('dp', 'tensor')), may hold values from -6 to 6
- picture_start: int32 [16], P('dp'), may hold values from 0 to 768, as said below
- picture_length: int32 [16], P('dp'), may hold values from 256 to 512, as said below
- qkvg_weight: float32 [4, 1536, 1536], P(None, 'dp', 'tensor'), may hold values from -0.15625 to 0.15625
- forget_weight: float32 [1536, 24], P('dp', 'tensor'), may hold values from -0.15625 to 0.15625
- forget_bias: float32 [24], replicated, may hold values from 1 to 7
- out_weight: float32 [1536, 1536], P('tensor', 'dp'), may hold values from -0.875 to 0.875
- gate_up: float32 [2, 1536, 4096], P(None, 'dp', 'tensor'), may hold values from -0.15625 to 0.15625
- down_weight: float32 [4096, 1536], P('tensor', 'dp'), may hold values from -0.09375 to 0.09375
- attn_gain: float32 [1536], replicated, may hold values from 0.5 to 1.5
- feed_gain: float32 [1536], replicated, may hold values from 0.5 to 1.5
- qkvg_first: float32 [4, 1536, 1536], P(None, 'dp', 'tensor'), may hold values from -0.000119096316 to 0.000119096316
- qkvg_second: float32 [4, 1536, 1536], P(None, 'dp', 'tensor'), may hold values from 1.7257769e-09 to 6.8379835e-09
- forget_first: float32 [1536, 24], P('dp', 'tensor'), may hold values from -0.000119096316 to 0.000119096316
- forget_second: float32 [1536, 24], P('dp', 'tensor'), may hold values from 1.7257769e-09 to 6.8379835e-09
- bias_first: float32 [24], replicated, may hold values from -0.000119096316 to 0.000119096316
- bias_second: float32 [24], replicated, may hold values from 1.7257769e-09 to 6.8379835e-09
- out_first: float32 [1536, 1536], P('tensor', 'dp'), may hold values from -0.000119096316 to 0.000119096316
- out_second: float32 [1536, 1536], P('tensor', 'dp'), may hold values from 1.7257769e-09 to 6.8379835e-09
- gateup_first: float32 [2, 1536, 4096], P(None, 'dp', 'tensor'), may hold values from -0.000119096316 to 0.000119096316
- gateup_second: float32 [2, 1536, 4096], P(None, 'dp', 'tensor'), may hold values from 1.7257769e-09 to 6.8379835e-09
- down_first: float32 [4096, 1536], P('tensor', 'dp'), may hold values from -0.000119096316 to 0.000119096316
- down_second: float32 [4096, 1536], P('tensor', 'dp'), may hold values from 1.7257769e-09 to 6.8379835e-09
- attngain_first: float32 [1536], replicated, may hold values from -0.000119096316 to 0.000119096316
- attngain_second: float32 [1536], replicated, may hold values from 1.7257769e-09 to 6.8379835e-09
- feedgain_first: float32 [1536], replicated, may hold values from -0.000119096316 to 0.000119096316
- feedgain_second: float32 [1536], replicated, may hold values from 1.7257769e-09 to 6.8379835e-09
Outputs:
- outputs: float32 [16384, 1536], P(('dp', 'tensor'))
- input_grad: float32 [16384, 1536], P(('dp', 'tensor'))
- grad_norm: float32 [], replicated
- qkvg_update: float32 [4, 1536, 1536], P(None, 'dp', 'tensor')
- qkvg_mean: float32 [4, 1536, 1536], P(None, 'dp', 'tensor')
- qkvg_meansq: float32 [4, 1536, 1536], P(None, 'dp', 'tensor')
- forget_update: float32 [1536, 24], P('dp', 'tensor')
- forget_mean: float32 [1536, 24], P('dp', 'tensor')
- forget_meansq: float32 [1536, 24], P('dp', 'tensor')
- bias_update: float32 [24], replicated
- bias_mean: float32 [24], replicated
- bias_meansq: float32 [24], replicated
- out_update: float32 [1536, 1536], P('tensor', 'dp')
- out_mean: float32 [1536, 1536], P('tensor', 'dp')
- out_meansq: float32 [1536, 1536], P('tensor', 'dp')
- gateup_update: float32 [2, 1536, 4096], P(None, 'dp', 'tensor')
- gateup_mean: float32 [2, 1536, 4096], P(None, 'dp', 'tensor')
- gateup_meansq: float32 [2, 1536, 4096], P(None, 'dp', 'tensor')
- down_update: float32 [4096, 1536], P('tensor', 'dp')
- down_mean: float32 [4096, 1536], P('tensor', 'dp')
- down_meansq: float32 [4096, 1536], P('tensor', 'dp')
- attngain_update: float32 [1536], replicated
- attngain_mean: float32 [1536], replicated
- attngain_meansq: float32 [1536], replicated
- feedgain_update: float32 [1536], replicated
- feedgain_mean: float32 [1536], replicated
- feedgain_meansq: float32 [1536], replicated
The draws below stay inside these ranges and needn't reach their ends.
Inputs may be any that keep to these rules, and one draw needn't show every extreme that they name: `picture_start`: a multiple of 256; picture_start + picture_length <= 1024. `picture_length`: a multiple of 256.
All inputs are finite; a program needn't handle non-finite values.
Results may differ from the reference program's by a relative error of at most 0.029.
Values may be sent and summed in bfloat16 or wider, within the bound.
No kernel may reach another device: no remote copies, remote signals or barrier semaphores. Data moves between devices by JAX's collectives and lax.ppermute only.
A program may use at most 168 MiB of HBM per device.

```python
import math
from functools import reduce
import jax
import jax.numpy as jnp
from jax import lax

D = 1536
HEADS = 24
HEAD_DIM = 64
FF = 4096
LENGTH = 1024
PIECE = 256
HD = 1536
SEQS = 16
TOKENS = 16384
N_TENSOR = 4


def picture_blocks(key):
    key_len, key_pick, key_start = jax.random.split(jax.random.fold_in(key, 11), 3)
    pieces = jax.random.randint(key_len, (SEQS,), 1, 3)
    chosen = jax.random.randint(key_pick, (), 0, SEQS)
    order = jnp.arange(SEQS)
    latest = (chosen + 1) % SEQS
    earliest = (chosen + 2) % SEQS
    pieces = jnp.where(order == chosen, 2, pieces)
    pieces = jnp.where(order == latest, 1, pieces)
    free_room = LENGTH // PIECE - pieces
    offset = jax.random.randint(key_start, (SEQS,), 0, free_room + 1)
    offset = jnp.where(order == latest, free_room, offset)
    offset = jnp.where(order == earliest, 0, offset)
    return ((offset * PIECE).astype(jnp.int32), (pieces * PIECE).astype(jnp.int32))


def draw_picture_start(key, part):
    return picture_blocks(key)[0]


def draw_picture_length(key, part):
    return picture_blocks(key)[1]


def shard_levels(stream_key, shape, cuts, smallest, high):
    def one(axis_at, blocks):
        heights = jax.random.uniform(jax.random.fold_in(jax.random.fold_in(stream_key, 6), axis_at), (blocks,), jnp.float32, smallest / len(cuts), high / len(cuts))
        return jnp.repeat(jnp.exp(heights), shape[axis_at] // blocks).reshape((-1,) + (1,) * (len(shape) - axis_at - 1))

    factor_of = one(*cuts[0])
    for cut in cuts[1:]:
        factor_of = factor_of * one(*cut)
    return factor_of


def gaussian(stream_key, shape, spread, bound, cuts=(), held_as=jnp.bfloat16):
    loudness = shard_levels(stream_key, shape, cuts, -0.22, 0.18) if cuts else 1.0
    drawn = jax.random.normal(stream_key, shape, jnp.float32) * spread * loudness
    return jnp.minimum(jnp.maximum(drawn, -bound), bound).astype(held_as)


def setup_inputs(seed: int = 0) -> dict:
    seeds = jax.random.split(jax.random.key(seed), 29)
    return {
        "inputs": gaussian(seeds[0], (TOKENS, D), 1.0, 6.0, ((0, 32),)),
        "cotangent": gaussian(seeds[1], (TOKENS, D), 1.0, 6.0, ((0, 32),)),
        "picture_start": draw_picture_start(jax.random.fold_in(seeds[28], 71), 0),
        "picture_length": draw_picture_length(jax.random.fold_in(seeds[28], 71), 0),
        "qkvg_weight": gaussian(seeds[4], (4, D, HD), D ** -0.5, 0.15625, ((1, 8), (2, 4)), jnp.float32),
        "forget_weight": gaussian(seeds[5], (D, HEADS), D ** -0.5, 0.15625, ((0, 8), (1, 4)), jnp.float32),
        "forget_bias": jnp.clip(jax.random.uniform(seeds[6], (HEADS,), jnp.float32, 1.0, 7.0), 1.0, 7.0),
        "out_weight": gaussian(seeds[7], (HD, D), (HD // 32) ** -0.5, 0.875, ((0, 4), (1, 8)), jnp.float32),
        "gate_up": gaussian(seeds[8], (2, D, FF), D ** -0.5, 0.15625, ((1, 8), (2, 4)), jnp.float32),
        "down_weight": gaussian(seeds[9], (FF, D), FF ** -0.5, 0.09375, ((0, 4), (1, 8)), jnp.float32),
        "attn_gain": jnp.clip(1.0 + 0.1 * jax.random.normal(seeds[10], (D,), jnp.float32), 0.5, 1.5),
        "feed_gain": jnp.clip(1.0 + 0.1 * jax.random.normal(seeds[11], (D,), jnp.float32), 0.5, 1.5),
        "qkvg_first": gaussian(seeds[12], (4, D, HD), (0.11 * (D * (5 * HD + HEADS + 3 * FF) + 2 * D + HEADS) ** -0.5), 0.000119096316, ((1, 8), (2, 4)), jnp.float32),
        "qkvg_second": jnp.clip(jnp.exp(math.log(6.837983512752999e-09) - 1.3768156 * jax.random.uniform(seeds[13], (4, D, HD), jnp.float32) ** shard_levels(seeds[13], (4, D, HD), ((1, 8), (2, 4)), -0.2, 0.2)), 1.7257768547551677e-09, 6.837983512752999e-09),
        "forget_first": gaussian(seeds[14], (D, HEADS), (0.11 * (D * (5 * HD + HEADS + 3 * FF) + 2 * D + HEADS) ** -0.5), 0.000119096316, ((0, 8), (1, 4)), jnp.float32),
        "forget_second": jnp.clip(jnp.exp(math.log(6.837983512752999e-09) - 1.3768156 * jax.random.uniform(seeds[15], (D, HEADS), jnp.float32) ** shard_levels(seeds[15], (D, HEADS), ((0, 8), (1, 4)), -0.2, 0.2)), 1.7257768547551677e-09, 6.837983512752999e-09),
        "bias_first": gaussian(seeds[16], (HEADS,), (0.11 * (D * (5 * HD + HEADS + 3 * FF) + 2 * D + HEADS) ** -0.5), 0.000119096316, (), jnp.float32),
        "bias_second": jnp.clip(jnp.exp(jax.random.uniform(seeds[17], (HEADS,), jnp.float32, math.log(1.7257768547551677e-09), math.log(6.837983512752999e-09))), 1.7257768547551677e-09, 6.837983512752999e-09),
        "out_first": gaussian(seeds[18], (HD, D), (0.11 * (D * (5 * HD + HEADS + 3 * FF) + 2 * D + HEADS) ** -0.5), 0.000119096316, ((0, 4), (1, 8)), jnp.float32),
        "out_second": jnp.clip(jnp.exp(math.log(6.837983512752999e-09) - 1.3768156 * jax.random.uniform(seeds[19], (HD, D), jnp.float32) ** shard_levels(seeds[19], (HD, D), ((0, 4), (1, 8)), -0.2, 0.2)), 1.7257768547551677e-09, 6.837983512752999e-09),
        "gateup_first": gaussian(seeds[20], (2, D, FF), (0.11 * (D * (5 * HD + HEADS + 3 * FF) + 2 * D + HEADS) ** -0.5), 0.000119096316, ((1, 8), (2, 4)), jnp.float32),
        "gateup_second": jnp.clip(jnp.exp(math.log(6.837983512752999e-09) - 1.3768156 * jax.random.uniform(seeds[21], (2, D, FF), jnp.float32) ** shard_levels(seeds[21], (2, D, FF), ((1, 8), (2, 4)), -0.2, 0.2)), 1.7257768547551677e-09, 6.837983512752999e-09),
        "down_first": gaussian(seeds[22], (FF, D), (0.11 * (D * (5 * HD + HEADS + 3 * FF) + 2 * D + HEADS) ** -0.5), 0.000119096316, ((0, 4), (1, 8)), jnp.float32),
        "down_second": jnp.clip(jnp.exp(math.log(6.837983512752999e-09) - 1.3768156 * jax.random.uniform(seeds[23], (FF, D), jnp.float32) ** shard_levels(seeds[23], (FF, D), ((0, 4), (1, 8)), -0.2, 0.2)), 1.7257768547551677e-09, 6.837983512752999e-09),
        "attngain_first": gaussian(seeds[24], (D,), (0.11 * (D * (5 * HD + HEADS + 3 * FF) + 2 * D + HEADS) ** -0.5), 0.000119096316, (), jnp.float32),
        "attngain_second": jnp.clip(jnp.exp(jax.random.uniform(seeds[25], (D,), jnp.float32, math.log(1.7257768547551677e-09), math.log(6.837983512752999e-09))), 1.7257768547551677e-09, 6.837983512752999e-09),
        "feedgain_first": gaussian(seeds[26], (D,), (0.11 * (D * (5 * HD + HEADS + 3 * FF) + 2 * D + HEADS) ** -0.5), 0.000119096316, (), jnp.float32),
        "feedgain_second": jnp.clip(jnp.exp(jax.random.uniform(seeds[27], (D,), jnp.float32, math.log(1.7257768547551677e-09), math.log(6.837983512752999e-09))), 1.7257768547551677e-09, 6.837983512752999e-09),
    }


MASK_FILL = -1000000000.0
NORM_EPS = 1e-05
BETA_ONE = 0.9
BETA_TWO = 0.95
WEIGHT_DECAY = 0.1
ADAM_EPS = 1e-08
MAX_NORM = 1.0
STEP_COUNT = 10.0
HIGH_PREC = lax.Precision.HIGHEST

@jax.custom_vjp
def low(v):
    return lax.optimization_barrier(v.astype(jnp.bfloat16)).astype(jnp.float32)

@jax.custom_vjp
def low_back(v):
    return v

def low_keep(v):
    return (low(v), None)

def low_pass(kept, grad):
    return (grad,)

def back_keep(v):
    return (v, None)

def back_low(kept, grad):
    return (low(grad),)
low.defvjp(low_keep, low_pass)
low_back.defvjp(back_keep, back_low)

def rms_scale(values):
    return lax.rsqrt(lax.optimization_barrier(jnp.mean(values * values, axis=-1, keepdims=True)) + NORM_EPS)

def mask_layout(pic_first, pic_size):
    places = jnp.arange(LENGTH)
    causal = places[None, :] <= places[:, None]
    inside = (places >= pic_first) & (places < pic_first + pic_size)
    allowed = causal | inside[:, None] & inside[None, :]
    return (allowed, jnp.where(causal, 1.0, -1.0).astype(jnp.float32))

def attend_sequence(members):
    queries, key_rows, values, forget_pre, pic_first, pic_size = members
    decay_sum = jnp.cumsum(jax.nn.log_sigmoid(forget_pre), axis=0)
    allowed, orient = mask_layout(pic_first, pic_size)
    raw_scores = jnp.einsum('ihe,jhe->hij', queries, key_rows, precision=HIGH_PREC) * HEAD_DIM ** (-0.5)
    cumulative = decay_sum.T
    shifted = raw_scores + orient[None] * (cumulative[:, :, None] - cumulative[:, None, :])
    scores = low_back(jnp.where(allowed[None], shifted, MASK_FILL))
    probability = jax.nn.softmax(scores, axis=-1)
    return jnp.einsum('hij,jhe->ihe', low(probability), values, precision=HIGH_PREC)

def layer_forward(inputs_f, qkvg_weight, forget_weight, forget_bias, out_weight, gate_up, down_weight, attn_gain, feed_gain, picture_start, picture_length):
    qkvg_low = low(qkvg_weight)
    forget_low = low(forget_weight)
    out_low = low(out_weight)
    gate_low = low(gate_up)
    down_low = low(down_weight)
    heads_local = HEADS // N_TENSOR
    width_local = heads_local * HEAD_DIM
    hidden_local = FF // N_TENSOR
    split_shape = (SEQS, LENGTH, heads_local, HEAD_DIM)
    normed_one = low(inputs_f * rms_scale(inputs_f) * attn_gain)
    attn_parts = []
    for group_rank in range(N_TENSOR):
        mine = low_back(normed_one)
        first_col = group_rank * width_local
        head_first = group_rank * heads_local
        projected = jnp.einsum('td,kde->kte', mine, qkvg_low[:, :, first_col:first_col + width_local], precision=HIGH_PREC)
        queries = low_back(low(projected[0])).reshape(split_shape)
        key_rows = low_back(low(projected[1])).reshape(split_shape)
        values = low_back(low(projected[2])).reshape(split_shape)
        gate_pre = low_back(projected[3])
        forget_pre = low_back(jnp.dot(mine, forget_low[:, head_first:head_first + heads_local], precision=HIGH_PREC) + forget_bias[head_first:head_first + heads_local])
        mixture = lax.map(jax.checkpoint(attend_sequence), (queries, key_rows, values, forget_pre.reshape(SEQS, LENGTH, heads_local), picture_start, picture_length))
        core = low_back(mixture.reshape(TOKENS, width_local))
        gated = low(core * jax.nn.sigmoid(gate_pre))
        attn_parts.append(low(jnp.dot(gated, out_low[first_col:first_col + width_local], precision=HIGH_PREC)))
    middle = inputs_f + low_back(reduce(jnp.add, attn_parts))
    normed_two = low(middle * rms_scale(middle) * feed_gain)
    feed_parts = []
    for group_rank in range(N_TENSOR):
        mine = low_back(normed_two)
        first_col = group_rank * hidden_local
        gate_act = low_back(jnp.einsum('td,kdf->ktf', mine, gate_low[:, :, first_col:first_col + hidden_local], precision=HIGH_PREC))
        hidden = low(jax.nn.silu(gate_act[0]) * gate_act[1])
        feed_parts.append(low(jnp.dot(hidden, down_low[first_col:first_col + hidden_local], precision=HIGH_PREC)))
    return middle + low_back(reduce(jnp.add, feed_parts))

def adam_step(weight, gradient, first_old, second_old, clip_scale, decay_rate):
    learn_rate = 0.4 / D ** 0.5
    scaled = gradient * clip_scale
    first_new = BETA_ONE * first_old + (1.0 - BETA_ONE) * scaled
    second_new = BETA_TWO * second_old + (1.0 - BETA_TWO) * scaled * scaled
    update = first_new / (1.0 - BETA_ONE ** STEP_COUNT) / (jnp.sqrt(second_new / (1.0 - BETA_TWO ** STEP_COUNT)) + ADAM_EPS)
    return (-learn_rate * (update + decay_rate * weight), first_new, second_new)

def reference(inputs, cotangent, picture_start, picture_length, qkvg_weight, forget_weight, forget_bias, out_weight, gate_up, down_weight, attn_gain, feed_gain, qkvg_first, qkvg_second, forget_first, forget_second, bias_first, bias_second, out_first, out_second, gateup_first, gateup_second, down_first, down_second, attngain_first, attngain_second, feedgain_first, feedgain_second):

    def closed(inputs_f, qkvg_w, forget_w, bias_w, out_w, gate_w, down_w, gain_one, gain_two):
        return layer_forward(inputs_f, qkvg_w, forget_w, bias_w, out_w, gate_w, down_w, gain_one, gain_two, picture_start, picture_length)
    result, pullback = jax.vjp(closed, inputs.astype(jnp.float32), qkvg_weight, forget_weight, forget_bias, out_weight, gate_up, down_weight, attn_gain, feed_gain)
    gradients = pullback(cotangent.astype(jnp.float32))
    total = reduce(jnp.add, [jnp.sum(grad_item * grad_item) for grad_item in gradients[1:]])
    grad_norm = jnp.sqrt(total)
    clip_scale = jnp.minimum(1.0, MAX_NORM / (grad_norm + 1e-06))
    qkvg_update, qkvg_mean, qkvg_meansq = adam_step(qkvg_weight, gradients[1], qkvg_first, qkvg_second, clip_scale, WEIGHT_DECAY)
    forget_update, forget_mean, forget_meansq = adam_step(forget_weight, gradients[2], forget_first, forget_second, clip_scale, WEIGHT_DECAY)
    bias_update, bias_mean, bias_meansq = adam_step(forget_bias, gradients[3], bias_first, bias_second, clip_scale, 0.0)
    out_update, out_mean, out_meansq = adam_step(out_weight, gradients[4], out_first, out_second, clip_scale, WEIGHT_DECAY)
    gateup_update, gateup_mean, gateup_meansq = adam_step(gate_up, gradients[5], gateup_first, gateup_second, clip_scale, WEIGHT_DECAY)
    down_update, down_mean, down_meansq = adam_step(down_weight, gradients[6], down_first, down_second, clip_scale, WEIGHT_DECAY)
    attngain_update, attngain_mean, attngain_meansq = adam_step(attn_gain, gradients[7], attngain_first, attngain_second, clip_scale, 0.0)
    feedgain_update, feedgain_mean, feedgain_meansq = adam_step(feed_gain, gradients[8], feedgain_first, feedgain_second, clip_scale, 0.0)
    return (result, gradients[0], grad_norm, qkvg_update, qkvg_mean, qkvg_meansq, forget_update, forget_mean, forget_meansq, bias_update, bias_mean, bias_meansq, out_update, out_mean, out_meansq, gateup_update, gateup_mean, gateup_meansq, down_update, down_mean, down_meansq, attngain_update, attngain_mean, attngain_meansq, feedgain_update, feedgain_mean, feedgain_meansq)
```

```python
import functools

import jax
import jax.numpy as jnp
from jax import lax
from jax.experimental import pallas as pl
from jax.experimental.pallas import tpu as pltpu

HEAD_DIM = 64
PIECE = 256
LOG2E = 1.4426950408889634
LOW = jnp.bfloat16
F32 = jnp.float32
HIDE = -1e30
NT = (((1,), (1,)), ((), ()))
TN = (((0,), (0,)), ((), ()))


def mm(a, b, dims=(((1,), (0,)), ((), ()))):
    return lax.dot_general(a, b, dims, preferred_element_type=F32)


def split_three(x):
    hi = x.astype(LOW)
    rest = x - hi.astype(F32)
    mid = rest.astype(LOW)
    return hi, mid, (rest - mid.astype(F32)).astype(LOW)


def scan_rows(x, reverse):
    length = x.shape[1]
    row = lax.broadcasted_iota(jnp.int32, (PIECE, PIECE), 0)
    col = lax.broadcasted_iota(jnp.int32, (PIECE, PIECE), 1)
    tri = jnp.where(row >= col if reverse else row <= col, 1.0, 0.0).astype(LOW)
    count = length // PIECE
    out = [None] * count
    carry = None
    for b in reversed(range(count)) if reverse else range(count):
        part = x[:, b * PIECE:(b + 1) * PIECE]
        done = sum(mm(t, tri) for t in split_three(part))
        if carry is not None:
            done = done + carry
        out[b] = done
        carry = done[:, :1] if reverse else done[:, PIECE - 1:]
    return jnp.concatenate(out, axis=1)


def log_gate(zf):
    return jnp.minimum(zf, 0.0) - jnp.log1p(jnp.exp(-jnp.abs(zf)))


def attn_fwd_kernel(start, size, q_ref, k_ref, v_ref, zf_ref, o_ref, lse_ref, *, hb):
    s_at = pl.program_id(0)
    length, width = q_ref.shape
    count = length // PIECE
    first, extent = start[s_at], size[s_at]
    c_rows = scan_rows(log_gate(zf_ref[...]), False) * LOG2E
    c_cols = c_rows.T
    row = lax.broadcasted_iota(jnp.int32, (PIECE, PIECE), 0)
    col = lax.broadcasted_iota(jnp.int32, (PIECE, PIECE), 1)
    causal = col <= row
    lane = lax.broadcasted_iota(jnp.int32, (1, width), 1)
    mine = [(lane >= h * HEAD_DIM) & (lane < (h + 1) * HEAD_DIM) for h in range(hb)]
    spare = [((h + 1) % hb) * HEAD_DIM for h in range(hb)]
    if lse_ref.shape[0] > hb:
        lse_ref[...] = jnp.zeros(lse_ref.shape, F32)

    def block(i, wide):
        lo, hi = i * PIECE, (i + 1) * PIECE
        in_pic = (lo >= first) & (lo < first + extent)
        out, lse = None, None
        for h in range(hb):
            q = jnp.where(mine[h], q_ref[lo:hi, :], jnp.zeros((), LOW))
            c_row = c_rows[h:h + 1, :]
            c_col = c_cols[lo:hi, h:h + 1]
            base = c_row[:, lo:lo + 1]
            parts, spans = [], []
            if i:
                parts.append(mm(q, k_ref[0:lo, :], NT) + (base - c_row[:, :lo]))
                spans.append((0, lo))
            back = base - 2.0 * c_col
            other = jnp.where(in_pic, back + c_row[:, lo:hi], HIDE)
            parts.append(mm(q, k_ref[lo:hi, :], NT) + jnp.where(causal, base - c_row[:, lo:hi], other))
            spans.append((lo, hi))
            if wide:
                parts.append(mm(q, k_ref[hi:hi + PIECE, :], NT) + (back + c_row[:, hi:hi + PIECE]))
                spans.append((hi, hi + PIECE))
            peak = functools.reduce(jnp.maximum, [jnp.max(p, axis=1, keepdims=True) for p in parts])
            acc = None
            for p, (a, b) in zip(parts, spans):
                v = jnp.where(mine[h], v_ref[a:b, :], jnp.ones((), LOW))
                t = mm(jnp.exp2(p - peak).astype(LOW), v)
                acc = t if acc is None else acc + t
            total = acc[:, spare[h]:spare[h] + 1]
            o_h = acc / total
            l_h = jnp.broadcast_to(peak + jnp.log2(total), o_h.shape)
            out = o_h if out is None else jnp.where(mine[h], o_h, out)
            lse = l_h if lse is None else jnp.where(mine[h], l_h, lse)
        o_ref[lo:hi, :] = out
        turned = lse.T
        for h in range(hb):
            lse_ref[h:h + 1, lo:hi] = turned[h * HEAD_DIM:h * HEAD_DIM + 1, :]

    for i in range(count):
        if i + 1 < count:
            wide = (first == i * PIECE) & (extent > PIECE)
            pl.when(wide)(functools.partial(block, i, True))
            pl.when(jnp.logical_not(wide))(functools.partial(block, i, False))
        else:
            block(i, False)


def attn_bwd_kernel(start, size, q_ref, k_ref, v_ref, zf_ref, lse_ref, o_ref, do_ref,
                    dq_ref, dk_ref, dv_ref, dzf_ref, dk_acc, dv_acc, dc_acc, *, hb):
    s_at = pl.program_id(0)
    length, width = q_ref.shape
    count = length // PIECE
    first, extent = start[s_at], size[s_at]
    zf = zf_ref[...]
    c_rows = scan_rows(log_gate(zf), False) * LOG2E
    c_cols = c_rows.T
    row = lax.broadcasted_iota(jnp.int32, (PIECE, PIECE), 0)
    col = lax.broadcasted_iota(jnp.int32, (PIECE, PIECE), 1)
    causal = row <= col
    lane = lax.broadcasted_iota(jnp.int32, (1, width), 1)
    mine = [(lane >= h * HEAD_DIM) & (lane < (h + 1) * HEAD_DIM) for h in range(hb)]
    spare = [((h + 1) % hb) * HEAD_DIM for h in range(hb)]
    zero, one = jnp.zeros((), LOW), jnp.ones((), LOW)
    dk_acc[...] = jnp.zeros(dk_acc.shape, F32)
    dv_acc[...] = jnp.zeros(dv_acc.shape, F32)
    prod = do_ref[...].astype(F32) * o_ref[...].astype(F32)
    head_row = lax.broadcasted_iota(jnp.int32, (8, width), 0)
    head_lane = lax.broadcasted_iota(jnp.int32, (8, width), 1)
    pick = jnp.where((head_lane >= head_row * HEAD_DIM) & (head_lane < (head_row + 1) * HEAD_DIM), 1.0, 0.0).astype(LOW)
    p_hi = prod.astype(LOW)
    p_lo = (prod - p_hi.astype(F32)).astype(LOW)
    delta = mm(pick, p_hi, NT) + mm(pick, p_lo, NT)

    def block(i, wide):
        lo, hi = i * PIECE, (i + 1) * PIECE
        in_pic = (lo >= first) & (lo < first + extent)
        out = None
        for h in range(hb):
            q_all = q_ref[lo:hi, :]
            q = jnp.where(mine[h], q_all, zero)
            q_one = jnp.where(mine[h], q_all, one)
            do = jnp.where(mine[h], do_ref[lo:hi, :], zero)
            c_row = c_rows[h:h + 1, lo:hi]
            base = c_row[:, :1]
            lse = lse_ref[h:h + 1, lo:hi]
            dl = delta[h:h + 1, lo:hi]
            back = base - 2.0 * c_row - lse
            acc = None
            todo = ([(0, lo, 0)] if i else []) + [(lo, hi, 1)] + ([(hi, hi + PIECE, 2)] if wide else [])
            for a, b, kind in todo:
                c_col = c_cols[a:b, h:h + 1]
                st = mm(k_ref[a:b, :], q, NT)
                if kind == 0:
                    st = st + (base - c_col) - lse
                elif kind == 1:
                    other = jnp.where(in_pic, back + c_col, HIDE)
                    st = st + jnp.where(causal, (base - c_col) - lse, other)
                else:
                    st = st + (back + c_col)
                p = jnp.exp2(st)
                ds = p * (mm(v_ref[a:b, :], do, NT) - dl)
                ds = ds.astype(LOW)
                dv_acc[a:b, :] += mm(p.astype(LOW), do)
                k_one = jnp.where(mine[h], k_ref[a:b, :], one)
                if kind == 2:
                    q_one = jnp.where(mine[h], q_all, -one)
                    k_one = jnp.where(mine[h], k_ref[a:b, :], -one)
                dk_acc[h, a:b, :] += mm(ds, q_one)
                t = mm(ds, k_one, TN)
                acc = t if acc is None else acc + t
                if kind == 1:
                    def signs(ds=ds, lo=lo, hi=hi, h=h):
                        minus = jnp.where(causal, zero, ds)
                        m2 = jnp.where(mine[h], zero, jnp.full((), -2.0, LOW))
                        m2 = jnp.broadcast_to(m2, (PIECE, width))
                        dk_acc[h, lo:hi, :] += mm(minus, m2)
                        dc_acc[h] = mm(minus, m2, TN)
                    def none(h=h):
                        dc_acc[h] = jnp.zeros((PIECE, width), F32)
                    pl.when(in_pic)(signs)
                    pl.when(jnp.logical_not(in_pic))(none)
                    acc = acc + dc_acc[h]
            out = acc if out is None else jnp.where(mine[h], acc, out)
            dc_row = acc.T[spare[h]:spare[h] + 1, :]
            dzf_ref[h:h + 1, lo:hi] = dc_row
        dq_ref[lo:hi, :] = (out * HEAD_DIM ** -0.5).astype(LOW)

    if dzf_ref.shape[0] > hb:
        dzf_ref[...] = jnp.zeros(dzf_ref.shape, F32)
    for i in range(count):
        if i + 1 < count:
            wide = (first == i * PIECE) & (extent > PIECE)
            pl.when(wide)(functools.partial(block, i, True))
            pl.when(jnp.logical_not(wide))(functools.partial(block, i, False))
        else:
            block(i, False)
    dv_ref[...] = dv_acc[...].astype(LOW)
    dk = dk_acc[0]
    for h in range(1, hb):
        dk = jnp.where(mine[h], dk_acc[h], dk)
    dk_ref[...] = (dk * (1.0 / LOG2E)).astype(LOW)
    for h in range(hb):
        turned = dk_acc[h].T
        dzf_ref[h:h + 1, :] -= turned[spare[h]:spare[h] + 1, :]
    dlog = scan_rows(dzf_ref[...], True)
    dzf_ref[...] = (dlog * jax.nn.sigmoid(-zf)).astype(LOW).astype(F32)


def attn_calls(q_like, seqs, heads):
    width = heads * HEAD_DIM
    hb = 2 if heads % 2 == 0 else heads
    return hb, heads // hb, hb * HEAD_DIM, width


def attend(start, size, qkv, zf, seqs):
    tokens, width3 = qkv.shape
    width, length = width3 // 3, tokens // seqs
    heads = width // HEAD_DIM
    hb, pairs, bw, _ = attn_calls(qkv, seqs, heads)
    col = lambda off: pl.BlockSpec((length, bw), lambda s, p, *_: (s, off * pairs + p))
    rows = pl.BlockSpec((None, None, 8, length), lambda s, p, *_: (s, p, 0, 0))
    if bw % 128:
        three, cols = [qkv[:, j * width:(j + 1) * width] for j in range(3)], [col(0)] * 3
    else:
        three, cols = [qkv] * 3, [col(0), col(1), col(2)]
    return pl.pallas_call(
        functools.partial(attn_fwd_kernel, hb=hb),
        grid_spec=pltpu.PrefetchScalarGridSpec(
            num_scalar_prefetch=2,
            grid=(seqs, pairs),
            in_specs=cols + [rows],
            out_specs=[col(0), rows],
        ),
        out_shape=[
            jax.ShapeDtypeStruct((tokens, width), F32),
            jax.ShapeDtypeStruct((seqs, pairs, 8, length), F32),
        ],
        compiler_params=pltpu.CompilerParams(vmem_limit_bytes=50 * 2**20),
        cost_estimate=pl.CostEstimate(flops=2 * 2 * 256 * length * length * seqs * heads * 5 // 8, bytes_accessed=tokens * width * 10, transcendentals=length * length * seqs * heads),
        name="attend",
    )(start, size, *three, zf)


def attend_back(start, size, qkv, zf, lse, core, up, seqs):
    tokens, width3 = qkv.shape
    width, length = width3 // 3, tokens // seqs
    heads = width // HEAD_DIM
    hb, pairs, bw, _ = attn_calls(qkv, seqs, heads)
    col = lambda off: pl.BlockSpec((length, bw), lambda s, p, *_: (s, off * pairs + p))
    rows = pl.BlockSpec((None, None, 8, length), lambda s, p, *_: (s, p, 0, 0))
    if bw % 128:
        three, cols = [qkv[:, j * width:(j + 1) * width] for j in range(3)], [col(0)] * 3
    else:
        three, cols = [qkv] * 3, [col(0), col(1), col(2)]
    return pl.pallas_call(
        functools.partial(attn_bwd_kernel, hb=hb),
        grid_spec=pltpu.PrefetchScalarGridSpec(
            num_scalar_prefetch=2,
            grid=(seqs, pairs),
            in_specs=cols + [rows, rows, col(0), col(0)],
            out_specs=[col(0), col(0), col(0), rows],
            scratch_shapes=[
                pltpu.VMEM((hb, length, bw), F32),
                pltpu.VMEM((length, bw), F32),
                pltpu.VMEM((hb, PIECE, bw), F32),
            ],
        ),
        out_shape=[jax.ShapeDtypeStruct((tokens, width), LOW)] * 3
        + [jax.ShapeDtypeStruct((seqs, pairs, 8, length), F32)],
        compiler_params=pltpu.CompilerParams(vmem_limit_bytes=50 * 2**20),
        cost_estimate=pl.CostEstimate(flops=5 * 2 * 256 * length * length * seqs * heads * 5 // 8, bytes_accessed=tokens * width * 20, transcendentals=length * length * seqs * heads),
        name="attend_back",
    )(start, size, *three, zf, lse, core, up)


from jax.sharding import PartitionSpec as P

NORM_EPS = 1e-05
BETA_ONE = 0.9
BETA_TWO = 0.95
WEIGHT_DECAY = 0.1
ADAM_EPS = 1e-08
MAX_NORM = 1.0
STEP_COUNT = 10.0


def rms_scale(values):
    return lax.rsqrt(jnp.mean(values * values, axis=-1, keepdims=True) + NORM_EPS)


def norm_back(gradient, values, inv_scale, gain_row):
    normed = values * inv_scale
    scaled = gradient * gain_row
    backward = inv_scale * (scaled - normed * jnp.mean(scaled * normed, axis=-1, keepdims=True))
    return (backward, jnp.sum(gradient * normed, axis=0))


def adam_step(weight, gradient, first_old, second_old, clip_scale, decay_rate, width):
    learn_rate = 0.4 / width**0.5
    scaled = gradient * clip_scale
    first_new = BETA_ONE * first_old + (1.0 - BETA_ONE) * scaled
    second_new = BETA_TWO * second_old + (1.0 - BETA_TWO) * scaled * scaled
    update = (
        first_new
        / (1.0 - BETA_ONE**STEP_COUNT)
        / (jnp.sqrt(second_new / (1.0 - BETA_TWO**STEP_COUNT)) + ADAM_EPS)
    )
    return (-learn_rate * (update + decay_rate * weight), first_new, second_new)


def after(x, *done):
    return lax.optimization_barrier((x,) + done)[0]


class Team:
    def __init__(self, axis, size):
        self.axis, self.size, self.me = axis, size, lax.axis_index(axis)

    def turn(self, x, k):
        return lax.ppermute(x, self.axis, [(i, (i + k) % self.size) for i in range(self.size)])

    def add(self, x):
        parts = jnp.stack([self.turn(x, k) if k else x for k in range(self.size)])
        order = lax.rem(self.me + self.size - jnp.arange(self.size, dtype=jnp.int32), self.size)
        return jnp.sum(jnp.take(parts, order, axis=0), axis=0)


class Ring:
    def __init__(self, axis, size):
        self.axis, self.size = axis, size
        if size == 8:
            self.table = list(range(0, size, 2)) + list(range(size - 1, 0, -2))
        else:
            self.table = list(range(size))
        spot = [self.table.index(i) for i in range(size)]
        me = lax.axis_index(axis)
        mine = jnp.asarray(spot, jnp.int32)[me]
        steps = jnp.arange(size, dtype=jnp.int32)
        self.ahead = jnp.asarray(self.table, jnp.int32)[lax.rem(mine + steps, size)]

    def step(self, x, way):
        n = self.size
        return lax.ppermute(x, self.axis, [(self.table[r], self.table[(r + way) % n]) for r in range(n)])

    def gather(self, x, way):
        n = self.size
        blocks = {0: x}
        a = b = x
        for k in range(1, n // 2 + 1):
            a = self.step(a, way)
            blocks[-k * way % n] = a
            if k <= (n - 1) // 2:
                b = self.step(b, -way)
                blocks[k * way % n] = b
        return [blocks[k] for k in range(n)]

    def reduce(self, x, way):
        n = self.size

        def block(k):
            return lax.dynamic_index_in_dim(x, self.ahead[k % n], 0, keepdims=False)

        arrived = []
        for w, far in ((way, n // 2), (-way, (n - 1) // 2)):
            moving = block(w * far)
            for k in range(far - 1, -1, -1):
                moving = self.step(moving, w)
                if k:
                    moving = (moving.astype(F32) + block(w * k).astype(F32)).astype(LOW)
            arrived.append(moving)
        return sum(m.astype(F32) for m in arrived) + block(0).astype(F32)


def place_kernel(where, *refs, rows, tail):
    count = (len(refs) - (3 if tail else 2))
    out, sem = refs[count], refs[-1]
    copies = []
    for i in range(count):
        at = pl.multiple_of(where[i] * rows, rows)
        copies.append(pltpu.make_async_copy(refs[i].at[pl.ds(0, rows), :], out.at[pl.ds(at, rows), :], sem.at[i]))
        if tail:
            at = pl.multiple_of(where[i] * tail, tail)
            copies.append(
                pltpu.make_async_copy(
                    refs[i].at[pl.ds(rows, tail), :], refs[count + 1].at[pl.ds(at, tail), :], sem.at[count + i]
                )
            )
    for copy in copies:
        copy.start()
    for copy in copies:
        copy.wait()


def place(blocks, where, tail=0):
    rows, n = blocks[0].shape
    rows -= tail
    count = len(blocks)
    shapes = [jax.ShapeDtypeStruct((count * r, n), blocks[0].dtype) for r in (rows, tail) if r]
    out = pl.pallas_call(
        functools.partial(place_kernel, rows=rows, tail=tail),
        in_specs=[pl.BlockSpec(memory_space=pltpu.SMEM)] + [pl.BlockSpec(memory_space=pl.ANY)] * count,
        out_specs=[pl.BlockSpec(memory_space=pltpu.VMEM)] * len(shapes),
        out_shape=shapes,
        scratch_shapes=[pltpu.SemaphoreType.DMA((2 * count,))],
        compiler_params=pltpu.CompilerParams(vmem_limit_bytes=40 * 2**20),
        cost_estimate=pl.CostEstimate(flops=0, bytes_accessed=4 * count * rows * n, transcendentals=0),
        name="place",
    )(where, *blocks)
    return out if tail else out[0]


def make_body(dp, tn):
    def body(
        inputs, cotangent, picture_start, picture_length,
        qkvg_weight, forget_weight, forget_bias, out_weight, gate_up, down_weight,
        attn_gain, feed_gain,
        qkvg_first, qkvg_second, forget_first, forget_second, bias_first, bias_second,
        out_first, out_second, gateup_first, gateup_second, down_first, down_second,
        attngain_first, attngain_second, feedgain_first, feedgain_second,
    ):
        dims = inputs.shape[1]
        local, rank_rows, width = inputs.shape[0], qkvg_weight.shape[1], qkvg_weight.shape[2]
        hidden_size = gate_up.shape[2]
        heads = forget_weight.shape[1]
        seqs = picture_start.shape[0]
        rows_group = local * tn
        length = rows_group // seqs
        data = Ring("dp", dp)
        rank = lax.axis_index("tensor")
        paired = tn == 4 and local * 2 == length
        core, side = lax.rem(rank, 2), lax.div(rank, 2)
        rows_each = dims // dp

        def swap(x, bit):
            return lax.ppermute(x, "tensor", [(i, i ^ bit) for i in range(tn)])

        def join(a, b):
            return jnp.where(core == 0, jnp.concatenate([a, b]), jnp.concatenate([b, a]))

        def half(p, which):
            return lax.dynamic_slice_in_dim(p, which * local, local, 0)

        def gather_rows(x):
            if not paired:
                return [lax.all_gather(x, "tensor", axis=0, tiled=True)]
            far = swap(x, 2)
            near = swap(x, 1)
            return [join(x, near), join(far, swap(far, 1))]

        def spread_far(part):
            if not paired:
                return lax.psum_scatter(part, "tensor", scatter_dimension=0, tiled=True)
            both = half(part, core).astype(F32) + swap(half(part, 1 - core), 1).astype(F32)
            return swap(both.astype(LOW), 2)

        def spread_near(back, part):
            if not paired:
                return back.astype(F32)
            near = half(part, core).astype(F32) + swap(half(part, 1 - core), 1).astype(F32)
            return near + back.astype(F32)

        if paired:
            order = [side, 1 - side]
            starts = [lax.dynamic_slice_in_dim(picture_start, o, 1) for o in order]
            sizes = [lax.dynamic_slice_in_dim(picture_length, o, 1) for o in order]
            seqs_each = 1
        else:
            starts, sizes, seqs_each = [picture_start], [picture_length], seqs
        chunks = len(starts)
        hb = 2 if heads % 2 == 0 else heads
        pairs = heads // hb

        def to_heads(z):
            z = z.reshape(pairs, hb, seqs_each, length).transpose(2, 0, 1, 3)
            return jnp.pad(z, ((0, 0), (0, 0), (0, 8 - hb), (0, 0)))

        def from_heads(z):
            return z[:, :, :hb].transpose(1, 2, 0, 3).reshape(heads, seqs_each * length)

        def flat(w):
            return w.transpose(1, 0, 2).reshape(w.shape[1], -1).astype(LOW)

        inputs_f = inputs.astype(F32)
        scale_one = rms_scale(inputs_f)
        normed_one = (inputs_f * scale_one * attn_gain).astype(LOW)
        tail = 16
        forget_row = forget_weight.T.astype(LOW).reshape(1, heads * rows_each)
        forget_row = jnp.pad(forget_row, ((0, tail - 1), (0, 3 * width - heads * rows_each)))
        blocks = data.gather(jnp.concatenate([flat(qkvg_weight[:3]), forget_row]), 1)
        w_qkv, w_forget = place(blocks, data.ahead, tail)
        w_forget = w_forget.reshape(dp, tail, -1)[:, 0, :heads * rows_each]
        w_forget = w_forget.reshape(dp, heads, rows_each).transpose(1, 0, 2).reshape(heads, dims)
        rows_one = gather_rows(normed_one)
        gate_out = jnp.concatenate([qkvg_weight[3].astype(LOW), out_weight.T.astype(LOW)], axis=1)
        blocks = data.gather(after(gate_out, w_qkv), -1)
        w_gate_out = place(blocks, data.ahead)
        w_gate, w_out = w_gate_out[:, :width], w_gate_out[:, width:]
        w_up = place(data.gather(after(flat(gate_up), w_qkv), 1), data.ahead)
        w_down = place(data.gather(after(down_weight.T.astype(LOW), w_gate_out), -1), data.ahead)
        feed_grad = gather_rows(after(cotangent, *rows_one))

        head_first = rank * heads
        bias_local = lax.dynamic_slice_in_dim(forget_bias, head_first, heads)
        col_scale = jnp.where(jnp.arange(3 * width) < width, HEAD_DIM**-0.5 * LOG2E, 1.0).astype(F32)

        last = ()
        qkv, zf, attended, gate_sig, gated = ([None] * chunks for _ in range(5))
        for i in range(chunks):
            r = after(rows_one[i], *last)
            qkv[i] = (mm(r, w_qkv) * col_scale).astype(LOW)
            zf[i] = to_heads(mm(w_forget, r, NT) + bias_local[:, None])
            last = (qkv[i], zf[i])
        parts = [None] * chunks
        back = None
        for i in reversed(range(chunks)):
            attended[i] = attend(starts[i], sizes[i], after(qkv[i], *last), zf[i], seqs_each)
            gate_sig[i] = jax.nn.sigmoid(mm(after(rows_one[i], attended[i][0]), w_gate))
            gated[i] = (attended[i][0] * gate_sig[i]).astype(LOW)
            parts[i] = mm(gated[i], w_out, NT).astype(LOW)
            last = (parts[i],)
            if back is None:
                back = spread_far(parts[i])
        middle = inputs_f + spread_near(back, parts[0])
        scale_two = rms_scale(middle)
        normed_two = (middle * scale_two * feed_gain).astype(LOW)
        rows_two = gather_rows(normed_two)

        hidden, grad_act = [None] * chunks, [None] * chunks
        last, back = (), None
        for i in range(chunks):
            act = mm(after(rows_two[i], *last), w_up)
            a, b = act[:, :hidden_size], act[:, hidden_size:]
            sig = jax.nn.sigmoid(a)
            silu = a * sig
            hidden[i] = (silu * b).astype(LOW)
            grad_hidden = mm(feed_grad[i], w_down)
            grad_gate = grad_hidden * b * sig * (1.0 + a * (1.0 - sig))
            grad_act[i] = jnp.concatenate([grad_gate, grad_hidden * silu], axis=1).astype(LOW)
            last = (grad_act[i],)
        back = spread_far(mm(grad_act[-1], w_up, NT).astype(LOW))
        own = mm(grad_act[0], w_up, NT).astype(LOW)
        grad_down = sum(mm(after(y, own), h, TN) for y, h in zip(feed_grad, hidden)).astype(LOW)
        shard_down = data.reduce(grad_down.reshape(dp, rows_each, -1), 1)
        grad_up = sum(mm(after(r, grad_down), g, TN) for r, g in zip(rows_two, grad_act)).astype(LOW)
        shard_up = data.reduce(after(grad_up, shard_down).reshape(dp, rows_each, -1), -1)
        grad_two = spread_near(back, own)
        grad_middle, gain_two_grad = norm_back(grad_two, middle, scale_two, feed_gain)
        grad_middle = grad_middle + cotangent.astype(F32)
        attn_grad = gather_rows(grad_middle.astype(LOW))
        out_back = spread_far(mm(after(hidden[-1], grad_up), w_down, NT).astype(LOW))
        outputs = middle + spread_near(out_back, mm(hidden[0], w_down, NT).astype(LOW))

        grad_gatepre, grad_proj, grad_zf = ([None] * chunks for _ in range(3))
        last = (grad_up,)
        for i in range(chunks):
            grad_core = mm(after(attn_grad[i], *last), w_out)
            up_stream = (grad_core * gate_sig[i]).astype(LOW)
            grad_gatepre[i] = (grad_core * attended[i][0] * gate_sig[i] * (1.0 - gate_sig[i])).astype(LOW)
            dq, dk, dv, dz = attend_back(
                starts[i], sizes[i], qkv[i], zf[i], attended[i][1], attended[i][0], up_stream, seqs_each
            )
            grad_proj[i] = jnp.concatenate([dq, dk, dv], axis=1)
            grad_zf[i] = from_heads(dz).astype(LOW)
            last = (dq,)
        grad_out = sum(mm(y, g, TN) for y, g in zip(attn_grad, gated)).astype(LOW)
        grad_gate_w = sum(mm(r, g, TN) for r, g in zip(rows_one, grad_gatepre)).astype(LOW)
        grad_go = jnp.concatenate([grad_gate_w, grad_out], axis=1)
        shard_go = data.reduce(grad_go.reshape(dp, rows_each, -1), 1)
        shard_gate, shard_out = shard_go[:, :width], shard_go[:, width:]
        grad_qkv = sum(mm(r, g, TN) for r, g in zip(rows_one, grad_proj)).astype(LOW)
        grad_forget = sum(mm(z, r) for r, z in zip(rows_one, grad_zf)).astype(LOW)
        grad_forget = grad_forget.reshape(heads, dp, rows_each).transpose(1, 0, 2).reshape(dp, 1, heads * rows_each)
        grad_forget = jnp.pad(grad_forget, ((0, 0), (0, tail - 1), (0, 3 * width - heads * rows_each)))
        packed = jnp.concatenate([grad_qkv.reshape(dp, rows_each, -1), grad_forget], axis=1)
        shard_qkv = data.reduce(packed, -1)
        shard_forget = shard_qkv[rows_each, :heads * rows_each].reshape(heads, rows_each).T
        shard_qkv = shard_qkv[:rows_each]
        bias_local_grad = sum(jnp.sum(z.astype(F32), axis=1) for z in grad_zf)
        terms = [None] * chunks
        back, last = None, (grad_qkv,)
        for i in reversed(range(chunks)):
            t = mm(after(grad_proj[i], *last), w_qkv, NT) + mm(grad_gatepre[i], w_gate, NT)
            terms[i] = (t + mm(grad_zf[i], w_forget, TN)).astype(LOW)
            last = (terms[i],)
            if back is None:
                back = spread_far(terms[i])
        grad_one = spread_near(back, terms[0])
        grad_inputs, gain_one_grad = norm_back(grad_one, inputs_f, scale_one, attn_gain)
        input_grad = grad_inputs + grad_middle

        bias_full = lax.dynamic_update_slice(jnp.zeros(forget_bias.shape, F32), bias_local_grad, (head_first,))
        shards = (shard_qkv, shard_gate, shard_forget, shard_out, shard_up, shard_down)
        square = sum(jnp.sum(s * s) for s in shards)
        pad = 128 - forget_bias.shape[0] - 1
        packed = jnp.concatenate([gain_one_grad, gain_two_grad, bias_full, square[None], jnp.zeros((pad,), F32)])
        packed = Team("dp", dp).add(Team("tensor", tn).add(packed.reshape(-1, 128))).reshape(-1)
        gain_one_sum, gain_two_sum = packed[:dims], packed[dims:2 * dims]
        bias_sum = packed[2 * dims:2 * dims + forget_bias.shape[0]]
        total = (
            packed[2 * dims + forget_bias.shape[0]]
            + jnp.sum(gain_one_sum * gain_one_sum)
            + jnp.sum(gain_two_sum * gain_two_sum)
            + jnp.sum(bias_sum * bias_sum)
        )
        grad_norm = jnp.sqrt(total)
        clip_scale = jnp.minimum(1.0, MAX_NORM / (grad_norm + 1e-06))

        def unflat(s, parts):
            return s.reshape(s.shape[0], parts, -1).transpose(1, 0, 2)

        def adam(weight, gradient, first_old, second_old, decay):
            return adam_step(weight, gradient, first_old, second_old, clip_scale, decay, dims)

        grad_attn = unflat(jnp.concatenate([shard_qkv, shard_gate], axis=1), 4)
        return (
            (outputs, input_grad, grad_norm)
            + adam(qkvg_weight, grad_attn, qkvg_first, qkvg_second, WEIGHT_DECAY)
            + adam(forget_weight, shard_forget, forget_first, forget_second, WEIGHT_DECAY)
            + adam(forget_bias, bias_sum, bias_first, bias_second, 0.0)
            + adam(out_weight, shard_out.T, out_first, out_second, WEIGHT_DECAY)
            + adam(gate_up, unflat(shard_up, 2), gateup_first, gateup_second, WEIGHT_DECAY)
            + adam(down_weight, shard_down.T, down_first, down_second, WEIGHT_DECAY)
            + adam(attn_gain, gain_one_sum, attngain_first, attngain_second, 0.0)
            + adam(feed_gain, gain_two_sum, feedgain_first, feedgain_second, 0.0)
        )

    return body


def solution(mesh):
    tokens = P(("dp", "tensor"), None)
    stack, tall, wide = P(None, "dp", "tensor"), P("dp", "tensor"), P("tensor", "dp")
    return jax.shard_map(
        make_body(mesh.shape["dp"], mesh.shape["tensor"]),
        mesh=mesh,
        in_specs=(tokens, tokens, P("dp"), P("dp"), stack, tall, P(), wide, stack, wide, P(), P())
        + (stack, stack, tall, tall, P(), P(), wide, wide, stack, stack, wide, wide, P(), P(), P(), P()),
        out_specs=(tokens, tokens, P())
        + (stack,) * 3 + (tall,) * 3 + (P(),) * 3 + (wide,) * 3 + (stack,) * 3 + (wide,) * 3 + (P(),) * 6,
        check_vma=False,
    )
```

```python
import functools

import jax
import jax.numpy as jnp
from jax import lax
from jax.experimental import pallas as pl
from jax.experimental.pallas import tpu as pltpu

HEAD_DIM = 64
PIECE = 256
LOG2E = 1.4426950408889634
LOW = jnp.bfloat16
F32 = jnp.float32
HIDE = -1e30
NT = (((1,), (1,)), ((), ()))
TN = (((0,), (0,)), ((), ()))


def mm(a, b, dims=(((1,), (0,)), ((), ()))):
    return lax.dot_general(a, b, dims, preferred_element_type=F32)


COST_SHARE = 1.0


def cost(flops, moved):
    return pl.CostEstimate(flops=int(flops * COST_SHARE), bytes_accessed=int(moved * COST_SHARE), transcendentals=0)


def split_three(x):
    hi = x.astype(LOW)
    rest = x - hi.astype(F32)
    mid = rest.astype(LOW)
    return hi, mid, (rest - mid.astype(F32)).astype(LOW)


def scan_rows(x, reverse):
    length = x.shape[1]
    row = lax.broadcasted_iota(jnp.int32, (PIECE, PIECE), 0)
    col = lax.broadcasted_iota(jnp.int32, (PIECE, PIECE), 1)
    tri = jnp.where(row >= col if reverse else row <= col, 1.0, 0.0).astype(LOW)
    count = length // PIECE
    out = [None] * count
    carry = None
    for b in reversed(range(count)) if reverse else range(count):
        part = x[:, b * PIECE:(b + 1) * PIECE]
        done = sum(mm(t, tri) for t in split_three(part))
        if carry is not None:
            done = done + carry
        out[b] = done
        carry = done[:, :1] if reverse else done[:, PIECE - 1:]
    return jnp.concatenate(out, axis=1)


def log_gate(zf):
    return jnp.minimum(zf, 0.0) - jnp.log1p(jnp.exp(-jnp.abs(zf)))


def attn_fwd_kernel(start, size, q_ref, k_ref, v_ref, zf_ref, o_ref, lse_ref, *, hb):
    s_at = pl.program_id(0)
    length, width = q_ref.shape
    count = length // PIECE
    first, extent = start[s_at], size[s_at]
    c_rows = scan_rows(log_gate(zf_ref[...]), False) * LOG2E
    c_cols = c_rows.T
    row = lax.broadcasted_iota(jnp.int32, (PIECE, PIECE), 0)
    col = lax.broadcasted_iota(jnp.int32, (PIECE, PIECE), 1)
    causal = col <= row
    lane = lax.broadcasted_iota(jnp.int32, (1, width), 1)
    mine = [(lane >= h * HEAD_DIM) & (lane < (h + 1) * HEAD_DIM) for h in range(hb)]
    spare = [((h + 1) % hb) * HEAD_DIM for h in range(hb)]
    if lse_ref.shape[0] > hb:
        lse_ref[...] = jnp.zeros(lse_ref.shape, F32)

    def block(i, wide):
        lo, hi = i * PIECE, (i + 1) * PIECE
        in_pic = (lo >= first) & (lo < first + extent)
        out, lse = None, None
        for h in range(hb):
            q = jnp.where(mine[h], q_ref[lo:hi, :], jnp.zeros((), LOW))
            c_row = c_rows[h:h + 1, :]
            c_col = c_cols[lo:hi, h:h + 1]
            base = c_row[:, lo:lo + 1]
            parts, spans = [], []
            if i:
                parts.append(mm(q, k_ref[0:lo, :], NT) + (base - c_row[:, :lo]))
                spans.append((0, lo))
            back = base - 2.0 * c_col
            other = jnp.where(in_pic, back + c_row[:, lo:hi], HIDE)
            parts.append(mm(q, k_ref[lo:hi, :], NT) + jnp.where(causal, base - c_row[:, lo:hi], other))
            spans.append((lo, hi))
            if wide:
                parts.append(mm(q, k_ref[hi:hi + PIECE, :], NT) + (back + c_row[:, hi:hi + PIECE]))
                spans.append((hi, hi + PIECE))
            peak = functools.reduce(jnp.maximum, [jnp.max(p, axis=1, keepdims=True) for p in parts])
            acc = None
            for p, (a, b) in zip(parts, spans):
                v = jnp.where(mine[h], v_ref[a:b, :], jnp.ones((), LOW))
                t = mm(jnp.exp2(p - peak).astype(LOW), v)
                acc = t if acc is None else acc + t
            total = acc[:, spare[h]:spare[h] + 1]
            o_h = acc / total
            l_h = jnp.broadcast_to(peak + jnp.log2(total), o_h.shape)
            out = o_h if out is None else jnp.where(mine[h], o_h, out)
            lse = l_h if lse is None else jnp.where(mine[h], l_h, lse)
        o_ref[lo:hi, :] = out
        turned = lse.T
        for h in range(hb):
            lse_ref[h:h + 1, lo:hi] = turned[h * HEAD_DIM:h * HEAD_DIM + 1, :]

    for i in range(count):
        if i + 1 < count:
            wide = (first == i * PIECE) & (extent > PIECE)
            pl.when(wide)(functools.partial(block, i, True))
            pl.when(jnp.logical_not(wide))(functools.partial(block, i, False))
        else:
            block(i, False)


def attn_bwd_kernel(start, size, q_ref, k_ref, v_ref, zf_ref, lse_ref, o_ref, do_ref,
                    dq_ref, dk_ref, dv_ref, dzf_ref, dk_acc, dv_acc, dc_acc, *, hb):
    s_at = pl.program_id(0)
    length, width = q_ref.shape
    count = length // PIECE
    first, extent = start[s_at], size[s_at]
    zf = zf_ref[...]
    c_rows = scan_rows(log_gate(zf), False) * LOG2E
    c_cols = c_rows.T
    row = lax.broadcasted_iota(jnp.int32, (PIECE, PIECE), 0)
    col = lax.broadcasted_iota(jnp.int32, (PIECE, PIECE), 1)
    causal = row <= col
    lane = lax.broadcasted_iota(jnp.int32, (1, width), 1)
    mine = [(lane >= h * HEAD_DIM) & (lane < (h + 1) * HEAD_DIM) for h in range(hb)]
    spare = [((h + 1) % hb) * HEAD_DIM for h in range(hb)]
    zero, one = jnp.zeros((), LOW), jnp.ones((), LOW)
    dk_acc[...] = jnp.zeros(dk_acc.shape, F32)
    dv_acc[...] = jnp.zeros(dv_acc.shape, F32)
    prod = do_ref[...].astype(F32) * o_ref[...].astype(F32)
    head_row = lax.broadcasted_iota(jnp.int32, (8, width), 0)
    head_lane = lax.broadcasted_iota(jnp.int32, (8, width), 1)
    pick = jnp.where((head_lane >= head_row * HEAD_DIM) & (head_lane < (head_row + 1) * HEAD_DIM), 1.0, 0.0).astype(LOW)
    p_hi = prod.astype(LOW)
    p_lo = (prod - p_hi.astype(F32)).astype(LOW)
    delta = mm(pick, p_hi, NT) + mm(pick, p_lo, NT)

    def block(i, wide):
        lo, hi = i * PIECE, (i + 1) * PIECE
        in_pic = (lo >= first) & (lo < first + extent)
        out = None
        for h in range(hb):
            q_all = q_ref[lo:hi, :]
            q = jnp.where(mine[h], q_all, zero)
            q_one = jnp.where(mine[h], q_all, one)
            do = jnp.where(mine[h], do_ref[lo:hi, :], zero)
            c_row = c_rows[h:h + 1, lo:hi]
            base = c_row[:, :1]
            lse = lse_ref[h:h + 1, lo:hi]
            dl = delta[h:h + 1, lo:hi]
            back = base - 2.0 * c_row - lse
            acc = None
            todo = ([(0, lo, 0)] if i else []) + [(lo, hi, 1)] + ([(hi, hi + PIECE, 2)] if wide else [])
            for a, b, kind in todo:
                c_col = c_cols[a:b, h:h + 1]
                st = mm(k_ref[a:b, :], q, NT)
                if kind == 0:
                    st = st + (base - c_col) - lse
                elif kind == 1:
                    other = jnp.where(in_pic, back + c_col, HIDE)
                    st = st + jnp.where(causal, (base - c_col) - lse, other)
                else:
                    st = st + (back + c_col)
                p = jnp.exp2(st)
                ds = p * (mm(v_ref[a:b, :], do, NT) - dl)
                ds = ds.astype(LOW)
                dv_acc[a:b, :] += mm(p.astype(LOW), do)
                k_one = jnp.where(mine[h], k_ref[a:b, :], one)
                if kind == 2:
                    q_one = jnp.where(mine[h], q_all, -one)
                    k_one = jnp.where(mine[h], k_ref[a:b, :], -one)
                dk_acc[h, a:b, :] += mm(ds, q_one)
                t = mm(ds, k_one, TN)
                acc = t if acc is None else acc + t
                if kind == 1:
                    def signs(ds=ds, lo=lo, hi=hi, h=h):
                        minus = jnp.where(causal, zero, ds)
                        m2 = jnp.where(mine[h], zero, jnp.full((), -2.0, LOW))
                        m2 = jnp.broadcast_to(m2, (PIECE, width))
                        dk_acc[h, lo:hi, :] += mm(minus, m2)
                        dc_acc[h] = mm(minus, m2, TN)
                    def none(h=h):
                        dc_acc[h] = jnp.zeros((PIECE, width), F32)
                    pl.when(in_pic)(signs)
                    pl.when(jnp.logical_not(in_pic))(none)
                    acc = acc + dc_acc[h]
            out = acc if out is None else jnp.where(mine[h], acc, out)
            dc_row = acc.T[spare[h]:spare[h] + 1, :]
            dzf_ref[h:h + 1, lo:hi] = dc_row
        dq_ref[lo:hi, :] = (out * HEAD_DIM ** -0.5).astype(LOW)

    if dzf_ref.shape[0] > hb:
        dzf_ref[...] = jnp.zeros(dzf_ref.shape, F32)
    for i in range(count):
        if i + 1 < count:
            wide = (first == i * PIECE) & (extent > PIECE)
            pl.when(wide)(functools.partial(block, i, True))
            pl.when(jnp.logical_not(wide))(functools.partial(block, i, False))
        else:
            block(i, False)
    dv_ref[...] = dv_acc[...].astype(LOW)
    dk = dk_acc[0]
    for h in range(1, hb):
        dk = jnp.where(mine[h], dk_acc[h], dk)
    dk_ref[...] = (dk * (1.0 / LOG2E)).astype(LOW)
    for h in range(hb):
        turned = dk_acc[h].T
        dzf_ref[h:h + 1, :] -= turned[spare[h]:spare[h] + 1, :]
    dlog = scan_rows(dzf_ref[...], True)
    dzf_ref[...] = (dlog * jax.nn.sigmoid(-zf)).astype(LOW).astype(F32)


def head_shapes(width):
    heads = width // HEAD_DIM
    hb = 2 if heads % 2 == 0 else heads
    return hb, heads // hb, hb * HEAD_DIM


def head_specs(qkv, seqs, first=0):
    tokens, width = qkv.shape[0], qkv.shape[1] // 3
    hb, pairs, bw = head_shapes(width)
    length = tokens // seqs

    def col(off):
        return pl.BlockSpec((length, bw), lambda s, p, *_: (s, off + p))

    def rows(off):
        return pl.BlockSpec((None, 8, length), lambda s, p, *_: (off + p, 0, s))

    if bw % 128:
        three, cols = [qkv[:, j * width:(j + 1) * width] for j in range(3)], [col(first)] * 3
    else:
        three, cols = [qkv] * 3, [col(j * pairs + first) for j in range(3)]
    return three, cols, col, rows


def attend(start, size, qkv, zf, seqs):
    tokens, width = qkv.shape[0], qkv.shape[1] // 3
    hb, pairs, bw = head_shapes(width)
    three, cols, col, rows = head_specs(qkv, seqs)
    work = tokens * tokens // seqs * width // HEAD_DIM
    return pl.pallas_call(
        functools.partial(attn_fwd_kernel, hb=hb),
        grid_spec=pltpu.PrefetchScalarGridSpec(
            num_scalar_prefetch=2,
            grid=(seqs, pairs),
            in_specs=cols + [rows(0)],
            out_specs=[col(0), rows(0)],
        ),
        out_shape=[
            jax.ShapeDtypeStruct((tokens, width), F32),
            jax.ShapeDtypeStruct((pairs, 8, tokens), F32),
        ],
        compiler_params=pltpu.CompilerParams(vmem_limit_bytes=40 * 2**20),
        cost_estimate=cost(1600 * work, tokens * width * 10),
        name="attend",
    )(start, size, *three, zf)


def attend_back(start, size, qkv, zf, lse, core, up, seqs, first, count):
    tokens, width = qkv.shape[0], qkv.shape[1] // 3
    hb, pairs, bw = head_shapes(width)
    length = tokens // seqs
    three, cols, col, rows = head_specs(qkv, seqs, first)
    work = tokens * tokens // seqs * hb * count
    return pl.pallas_call(
        functools.partial(attn_bwd_kernel, hb=hb),
        grid_spec=pltpu.PrefetchScalarGridSpec(
            num_scalar_prefetch=2,
            grid=(seqs, count),
            in_specs=cols + [rows(first), rows(first), col(first), col(first)],
            out_specs=[col(0)] * 3 + [rows(0)],
            scratch_shapes=[
                pltpu.VMEM((hb, length, bw), F32),
                pltpu.VMEM((length, bw), F32),
                pltpu.VMEM((hb, PIECE, bw), F32),
            ],
        ),
        out_shape=[jax.ShapeDtypeStruct((tokens, count * bw), LOW)] * 3
        + [jax.ShapeDtypeStruct((count, 8, tokens), F32)],
        compiler_params=pltpu.CompilerParams(vmem_limit_bytes=40 * 2**20),
        cost_estimate=cost(2600 * work, tokens * count * bw * 20),
        name="attend_back",
    )(start, size, *three, zf, lse, core, up)


BLOCK = 256


class Pieces:
    def __init__(self, half, count, rows):
        self.half, self.count, self.rows = half, count, rows
        self.block = min(BLOCK, rows)
        self.each = rows // self.block
        self.steps = count * self.each

    def first(self, p):
        return (self.count - 1 - p) * self.each

    def inside(self, p, i):
        return jnp.clip(i - self.first(p), 0, self.each - 1)

    def active(self, p, i):
        return (i >= self.first(p)) & (i < self.first(p) + self.each)

    def own_spec(self, p, n):
        return pl.BlockSpec((self.block, n), lambda i, *_: (self.inside(p, i), 0))

    def own_specs(self, n):
        return [self.own_spec(p, n) for p in range(self.count)]

    def true_at(self, i, half):
        return half[self.count - 1 - lax.div(i, self.each)] * self.each + lax.rem(i, self.each)

    def true_spec(self, n):
        return pl.BlockSpec((self.block, n), lambda i, half: (self.true_at(i, half), 0))

    def lane_spec(self, lead):
        return pl.BlockSpec(lead + (self.block,), lambda i, half: (0,) * len(lead) + (self.true_at(i, half),))

    def flat_spec(self, n):
        return pl.BlockSpec(
            (self.block, n),
            lambda i, *_: ((self.count - 1 - lax.div(i, self.each)) * self.each + lax.rem(i, self.each), 0),
        )

    def pick(self, refs, i):
        x = refs[0][...]
        for p in range(1, self.count):
            x = jnp.where(self.active(p, i), refs[p][...], x)
        return x

    def put(self, refs, i, value):
        for p in range(self.count):
            def write(p=p):
                refs[p][...] = value
            pl.when(self.active(p, i))(write)

    def shapes(self, n, dtype=LOW):
        return [jax.ShapeDtypeStruct((self.rows, n), dtype)] * self.count

    def all_rows(self):
        return self.count * self.rows

    def call(self, kernel, name, ins, in_specs, out_shapes, out_specs, flops):
        moved = sum(x.size * x.dtype.itemsize for x in ins) + sum(s.size * s.dtype.itemsize for s in out_shapes)
        return pl.pallas_call(
            kernel,
            grid_spec=pltpu.PrefetchScalarGridSpec(
                num_scalar_prefetch=1, grid=(self.steps,), in_specs=in_specs, out_specs=out_specs
            ),
            out_shape=out_shapes,
            compiler_params=pltpu.CompilerParams(vmem_limit_bytes=48 * 2**20),
            cost_estimate=cost(flops * 3 // 2, moved),
            name=name,
        )(self.half, *ins)


def whole(rows, n, at=0):
    return pl.BlockSpec((rows, n), lambda *_: (0, at), pipeline_mode=pl.Buffered(1))


def project(pc, xs, w, wf, bias):
    dims, width = w.shape[0], w.shape[1] // 3
    pairs = wf.shape[0] // 8

    def kernel(half, *refs):
        i = pl.program_id(0)
        w_ref, wf_ref, bias_ref, qkv_ref, zf_ref = refs[pc.count:]
        x = pc.pick(refs[:pc.count], i)
        q = mm(x, w_ref[:, :width]) * (HEAD_DIM**-0.5 * LOG2E)
        qkv_ref[:, :width] = q.astype(LOW)
        qkv_ref[:, width:] = mm(x, w_ref[:, width:]).astype(LOW)
        z = mm(wf_ref[...], x, NT) + bias_ref[...]
        for p in range(pairs):
            zf_ref[p] = z[8 * p:8 * p + 8, :]

    rows = pc.all_rows()
    return pc.call(
        kernel, "project",
        list(xs) + [w, wf, bias],
        pc.own_specs(dims) + [whole(dims, 3 * width), whole(8 * pairs, dims), whole(8 * pairs, 1)],
        [jax.ShapeDtypeStruct((rows, 3 * width), LOW), jax.ShapeDtypeStruct((pairs, 8, rows), F32)],
        [pc.true_spec(3 * width), pc.lane_spec((pairs, 8))],
        6 * rows * dims * width,
    )


def close(pc, xs, core, w_gate, w_out):
    dims, width = w_out.shape

    def kernel(half, *refs):
        i = pl.program_id(0)
        core_ref, wg_ref, w_ref, sig_ref, gated_ref = refs[pc.count:pc.count + 5]
        sig = jax.nn.sigmoid(mm(pc.pick(refs[:pc.count], i), wg_ref[...]))
        sig_ref[...] = sig
        g = (core_ref[...] * sig).astype(LOW)
        gated_ref[...] = g
        pc.put(refs[pc.count + 5:], i, mm(g, w_ref[...], NT).astype(LOW))

    rows = pc.all_rows()
    out = pc.call(
        kernel, "close",
        list(xs) + [core, w_gate, w_out],
        pc.own_specs(dims) + [pc.true_spec(width), whole(dims, width), whole(dims, width)],
        [jax.ShapeDtypeStruct((rows, width), F32), jax.ShapeDtypeStruct((rows, width), LOW)] + pc.shapes(dims),
        [pc.true_spec(width), pc.flat_spec(width)] + pc.own_specs(dims),
        4 * rows * dims * width,
    )
    return out[0], out[1], out[2:]


def feed(pc, xs, ys, w):
    dims, hidden = w.shape[0], w.shape[1] // 3
    n = pc.count

    def kernel(half, *refs):
        i = pl.program_id(0)
        w_ref, hidden_ref, grad_ref = refs[2 * n:2 * n + 3]
        x, y = pc.pick(refs[:n], i), pc.pick(refs[n:2 * n], i)
        a = mm(x, w_ref[:, :hidden])
        sig = jax.nn.sigmoid(a)
        silu = a * sig
        b = mm(x, w_ref[:, hidden:2 * hidden])
        hidden_ref[...] = (silu * b).astype(LOW)
        gh = mm(y, w_ref[:, 2 * hidden:])
        grad_ref[:, :hidden] = (gh * b * sig * (1.0 + a * (1.0 - sig))).astype(LOW)
        grad_ref[:, hidden:] = (gh * silu).astype(LOW)
        pc.put(refs[2 * n + 3:], i, mm(grad_ref[...], w_ref[:, :2 * hidden], NT).astype(LOW))

    rows = pc.all_rows()
    out = pc.call(
        kernel, "feed",
        list(xs) + list(ys) + [w],
        pc.own_specs(dims) * 2 + [whole(dims, 3 * hidden)],
        [jax.ShapeDtypeStruct((rows, hidden), LOW), jax.ShapeDtypeStruct((rows, 2 * hidden), LOW)] + pc.shapes(dims),
        [pc.flat_spec(hidden), pc.flat_spec(2 * hidden)] + pc.own_specs(dims),
        10 * rows * dims * hidden,
    )
    return out[0], out[1], out[2:]


def feed_out(pc, hidden, w):
    dims, n = w.shape[0], w.shape[1] // 3

    def kernel(half, hidden_ref, w_ref, *parts):
        pc.put(parts, pl.program_id(0), mm(hidden_ref[...], w_ref[...], NT).astype(LOW))

    return pc.call(
        kernel, "feed_out", [hidden, w], [pc.flat_spec(n), whole(dims, n, 2)],
        pc.shapes(dims), pc.own_specs(dims), 2 * pc.all_rows() * dims * n,
    )


def open_back(pc, ys, w_out, core, sig):
    dims, width = w_out.shape

    def kernel(half, *refs):
        w_ref, core_ref, sig_ref, up_ref, gate_ref = refs[pc.count:]
        g = mm(pc.pick(refs[:pc.count], pl.program_id(0)), w_ref[...])
        s = sig_ref[...]
        up_ref[...] = (g * s).astype(LOW)
        gate_ref[...] = (g * core_ref[...] * s * (1.0 - s)).astype(LOW)

    rows = pc.all_rows()
    return pc.call(
        kernel, "open_back",
        list(ys) + [w_out, core, sig],
        pc.own_specs(dims) + [whole(dims, width), pc.true_spec(width), pc.true_spec(width)],
        [jax.ShapeDtypeStruct((rows, width), LOW)] * 2,
        [pc.true_spec(width)] * 2,
        2 * rows * dims * width,
    )


def project_back(pc, grads, dz, w_qkv, w_gate, wf):
    dims = w_qkv.shape[0]
    pairs = dz.shape[0]
    n = len(grads)
    width = w_gate.shape[1]

    def kernel(half, *refs):
        dz_ref, w_ref, wg_ref, wf_ref = refs[n:n + 4]
        g = jnp.concatenate([r[...] for r in refs[:n - 1]], axis=1)
        total = mm(g, w_ref[...], NT) + mm(refs[n - 1][...], wg_ref[...], NT)
        z = jnp.concatenate([dz_ref[p] for p in range(pairs)], axis=0).astype(LOW)
        total = total + mm(z, wf_ref[...], TN)
        pc.put(refs[n + 4:], pl.program_id(0), total.astype(LOW))

    return pc.call(
        kernel, "project_back",
        list(grads) + [dz, w_qkv, w_gate, wf],
        [pc.true_spec(g.shape[1]) for g in grads]
        + [pc.lane_spec((pairs, 8)), whole(dims, 3 * width), whole(dims, width), whole(8 * pairs, dims)],
        pc.shapes(dims), pc.own_specs(dims), 8 * pc.all_rows() * dims * width,
    )


def weight_grads(pc, groups, name, step):
    dims = groups[0][0][0][0].shape[1]
    ins, specs, plan, at = [], [], [], 0
    flops = 0
    for group in groups:
        terms = []
        for lefts, (right, n, c), true in group:
            for p, left in enumerate(lefts):
                terms.append((len(ins), len(ins) + 1))
                ins += [left, right]
                specs.append(pl.BlockSpec((pc.rows, step), lambda i, *_: (0, i)))
                if true:
                    spec = pl.BlockSpec((pc.rows, n), lambda i, half, p=p, c=c: (half[p], c), pipeline_mode=pl.Buffered(1))
                else:
                    spec = pl.BlockSpec((pc.rows, n), lambda i, *_, p=p, c=c: (p, c), pipeline_mode=pl.Buffered(1))
                specs.append(spec)
                flops += 2 * pc.rows * dims * n
        plan.append((terms, at, n))
        at += n

    def kernel(half, *refs):
        out = refs[-1]
        for terms, at, n in plan:
            total = None
            for a, b in terms:
                t = mm(refs[a][...], refs[b][...], TN)
                total = t if total is None else total + t
            out[:, at:at + n] = total.astype(LOW)

    return pl.pallas_call(
        kernel,
        grid_spec=pltpu.PrefetchScalarGridSpec(
            num_scalar_prefetch=1, grid=(dims // step,), in_specs=specs,
            out_specs=pl.BlockSpec((step, at), lambda i, *_: (i, 0)),
        ),
        out_shape=jax.ShapeDtypeStruct((dims, at), LOW),
        compiler_params=pltpu.CompilerParams(vmem_limit_bytes=50 * 2**20),
        cost_estimate=cost(flops * 3 // 2, dims * at * 6),
        name=name,
    )(pc.half, *ins)


def project_grads(pc, chunks, size, tail, n):
    dims = chunks[0][0][0].shape[1]
    step = 384
    per = step // size
    cols = len(chunks[0][1])
    pairs = chunks[0][2].shape[0] if tail else 0
    ins, specs, plan = [], [], []
    for lefts, grads, dz in chunks:
        for p, left in enumerate(lefts):
            plan.append(len(ins))
            ins += [left] + [g for g, _ in grads]
            specs.append(pl.BlockSpec((pc.rows, step), lambda i, *_: (0, i)))
            for _, c in grads:
                specs.append(
                    pl.BlockSpec((pc.rows, n), lambda i, half, p=p, c=c: (half[p], c), pipeline_mode=pl.Buffered(1))
                )
            if tail:
                ins.append(dz)
                specs.append(pl.BlockSpec((pairs, 8, pc.rows), lambda i, half, p=p: (0, 0, half[p])))

    def kernel(half, *refs):
        out = refs[-1]
        for c in range(cols):
            total = None
            for at in plan:
                t = mm(refs[at][...], refs[at + 1 + c][...], TN)
                total = t if total is None else total + t
            total = total.astype(LOW)
            for b in range(per):
                out[b, :size, c * n:(c + 1) * n] = total[b * size:(b + 1) * size]
        if not tail:
            return
        total = None
        for at in plan:
            z = jnp.concatenate([refs[at + 1 + cols][p] for p in range(pairs)], axis=0).astype(LOW)
            t = mm(z, refs[at][...])
            total = t if total is None else total + t
        hb = tail_heads
        heads = [total[8 * p:8 * p + hb] for p in range(pairs)]
        heads.append(jnp.zeros((tail - hb * pairs, step), F32))
        total = jnp.concatenate(heads, axis=0)
        for b in range(per):
            row = total[:, b * size:(b + 1) * size]
            row = jnp.concatenate([row, jnp.zeros((tail, cols * n - size), F32)], axis=1)
            out[b, size:, :] = row.astype(LOW)

    tail_heads = head_shapes(n)[0]
    return pl.pallas_call(
        kernel,
        grid_spec=pltpu.PrefetchScalarGridSpec(
            num_scalar_prefetch=1, grid=(dims // step,), in_specs=specs,
            out_specs=pl.BlockSpec((per, size + tail, cols * n), lambda i, *_: (i, 0, 0)),
        ),
        out_shape=jax.ShapeDtypeStruct((dims // size, size + tail, cols * n), LOW),
        compiler_params=pltpu.CompilerParams(vmem_limit_bytes=50 * 2**20),
        cost_estimate=cost(12 * pc.rows * dims * cols * n, dims * cols * n * 6),
        name="project_grads",
    )(pc.half, *ins)


from jax.sharding import PartitionSpec as P

NORM_EPS = 1e-05
BETA_ONE = 0.9
BETA_TWO = 0.95
WEIGHT_DECAY = 0.1
ADAM_EPS = 1e-08
MAX_NORM = 1.0
STEP_COUNT = 10.0


def rms_scale(values):
    return lax.rsqrt(jnp.mean(values * values, axis=-1, keepdims=True) + NORM_EPS)


def norm_back(gradient, values, inv_scale, gain_row):
    normed = values * inv_scale
    scaled = gradient * gain_row
    backward = inv_scale * (scaled - normed * jnp.mean(scaled * normed, axis=-1, keepdims=True))
    return (backward, jnp.sum(gradient * normed, axis=0))


def adam_step(weight, gradient, first_old, second_old, clip_scale, decay_rate, width):
    learn_rate = 0.4 / width**0.5
    scaled = gradient * clip_scale
    first_new = BETA_ONE * first_old + (1.0 - BETA_ONE) * scaled
    second_new = BETA_TWO * second_old + (1.0 - BETA_TWO) * scaled * scaled
    update = (
        first_new
        / (1.0 - BETA_ONE**STEP_COUNT)
        / (jnp.sqrt(second_new / (1.0 - BETA_TWO**STEP_COUNT)) + ADAM_EPS)
    )
    return (-learn_rate * (update + decay_rate * weight), first_new, second_new)


def after(x, *done):
    return lax.optimization_barrier((x,) + done)[0]


def index(x, i, axis):
    return lax.dynamic_index_in_dim(x, i, axis, keepdims=False, allow_negative_indices=False)


class Ring:
    def __init__(self, axis, size):
        self.axis, self.size = axis, size
        if size == 8:
            self.table = list(range(0, size, 2)) + list(range(size - 1, 0, -2))
        else:
            self.table = list(range(size))
        spot = [self.table.index(i) for i in range(size)]
        ahead = [[self.table[(spot[i] + k) % size] for k in range(size)] for i in range(size)]
        self.ahead = index(jnp.asarray(ahead, jnp.int32), lax.axis_index(axis), 0)

    def step(self, x, way):
        n = self.size
        return lax.ppermute(x, self.axis, [(self.table[r], self.table[(r + way) % n]) for r in range(n)])

    def gather(self, x, way):
        return Gather(self, x, way)

    def reduce(self, x, way):
        return Reduce(self, x, way)


class Gather:
    def __init__(self, ring, x, way):
        self.ring, self.way, self.k = ring, way, 0
        self.blocks = {0: x}
        self.ends = [x, x]

    def step(self, *done):
        ring, n = self.ring, self.ring.size
        self.k += 1
        if self.k > 1 or done:
            self.ends = list(lax.optimization_barrier(tuple(self.ends) + done)[:2])
        self.ends[0] = ring.step(self.ends[0], self.way)
        self.blocks[-self.k * self.way % n] = self.ends[0]
        if self.k <= (n - 1) // 2:
            self.ends[1] = ring.step(self.ends[1], -self.way)
            self.blocks[self.k * self.way % n] = self.ends[1]
        return self.ends

    def all(self):
        while self.k < self.ring.size // 2:
            self.step()
        return [self.blocks[k] for k in range(self.ring.size)]


class Reduce:
    def __init__(self, ring, x, way):
        self.ring, self.x, self.k = ring, x, 0
        n = ring.size
        self.ways = ((way, n // 2), (-way, (n - 1) // 2))
        self.moving = [None, None]

    def block(self, k):
        return index(self.x, index(self.ring.ahead, k % self.ring.size, 0), 0)

    def step(self, *done):
        self.k += 1
        if self.k > 1:
            tied = lax.optimization_barrier(tuple(self.moving) + done)
            self.moving = list(tied[:2])
        for j, (way, far) in enumerate(self.ways):
            left = far - self.k + 1
            if left < 1:
                continue
            own = self.block(way * left)
            if self.k > 1:
                own = (self.moving[j].astype(F32) + own.astype(F32)).astype(LOW)
            self.moving[j] = self.ring.step(own, way)
        return self.moving

    def all(self):
        while self.k < self.ring.size // 2:
            self.step()
        return sum(m.astype(F32) for m in self.moving if m is not None) + self.block(0).astype(F32)


def sum_all(x, axis, size):
    bit = 1
    while bit < size:
        x = x + lax.ppermute(x, axis, [(i, i ^ bit) for i in range(size)])
        bit *= 2
    return x


def place_kernel(where, *refs, arrays, size, rows, tail):
    out, sem = refs[arrays], refs[-1]
    copies = []
    block = 0
    for ref in refs[:arrays]:
        for j in range(ref.shape[0] // size):
            spans = [(out, rows, j * size)] + ([(refs[arrays + 1], tail, j * size + rows)] if tail else [])
            for to, count, at in spans:
                to_at = pl.multiple_of(where[block] * count, count)
                copies.append(
                    pltpu.make_async_copy(
                        ref.at[pl.ds(at, count), :], to.at[pl.ds(to_at, count), :], sem.at[len(copies)]
                    )
                )
            block += 1
    for copy in copies:
        copy.start()
    for copy in copies:
        copy.wait()


def place(parts, where, size, tail=0):
    n = parts[0].shape[1]
    count = sum(p.shape[0] for p in parts) // size
    shapes = [jax.ShapeDtypeStruct((count * r, n), LOW) for r in (size - tail, tail) if r]
    out = pl.pallas_call(
        functools.partial(place_kernel, arrays=len(parts), size=size, rows=size - tail, tail=tail),
        in_specs=[pl.BlockSpec(memory_space=pltpu.SMEM)] + [pl.BlockSpec(memory_space=pl.ANY)] * len(parts),
        out_specs=[pl.BlockSpec(memory_space=pltpu.VMEM)] * len(shapes),
        out_shape=shapes,
        scratch_shapes=[pltpu.SemaphoreType.DMA((2 * count,))],
        compiler_params=pltpu.CompilerParams(vmem_limit_bytes=40 * 2**20),
        cost_estimate=cost(0, 4 * count * size * n),
        name="place",
    )(where, *parts)
    return out if tail else out[0]


def make_body(dp, tn):
    def body(
        inputs, cotangent, picture_start, picture_length,
        qkvg_weight, forget_weight, forget_bias, out_weight, gate_up, down_weight,
        attn_gain, feed_gain,
        qkvg_first, qkvg_second, forget_first, forget_second, bias_first, bias_second,
        out_first, out_second, gateup_first, gateup_second, down_first, down_second,
        attngain_first, attngain_second, feedgain_first, feedgain_second,
    ):
        dims = inputs.shape[1]
        local, rank_rows, width = inputs.shape[0], qkvg_weight.shape[1], qkvg_weight.shape[2]
        hidden_size = gate_up.shape[2]
        heads = forget_weight.shape[1]
        seqs = picture_start.shape[0]
        rows_group = local * tn
        length = rows_group // seqs
        data = Ring("dp", dp)
        rank = lax.axis_index("tensor")
        paired = tn == 4 and local * 2 == length
        core, side = lax.rem(rank, 2), lax.div(rank, 2)
        rows_each = dims // dp

        def swap(x, bit):
            return lax.ppermute(x, "tensor", [(i, i ^ bit) for i in range(tn)])

        def rows_start(x):
            if not paired:
                return [lax.all_gather(x, "tensor", axis=0, tiled=True)], None
            return [x, swap(x, 1)], swap(x, 2)

        def far(moved, *done):
            there = after(moved[1], *done) if done else moved[1]
            return [there, swap(there, 1)]

        def spread_far(parts, count=1):
            if not paired:
                return parts[0], [lax.psum_scatter(parts[0], "tensor", scatter_dimension=0, tiled=True)]
            both = (parts[0].astype(F32) + swap(parts[1], 1).astype(F32)).astype(LOW)
            came, size = [], local // count
            for k in range(count):
                came.append(swap(after(both[k * size:(k + 1) * size], *came[-1:]), 2))
            return both, came

        def spread_own(parts, *done):
            return [parts[0], swap(after(parts[1], *done), 1)] if paired else []

        def spread_sum(back, own):
            total = jnp.concatenate(back).astype(F32)
            for p in own:
                total = total + p.astype(F32)
            return total

        if paired:
            pc = Pieces(jnp.stack([core, 1 - core]).astype(jnp.int32), 2, local)
        else:
            pc = Pieces(jnp.zeros((1,), jnp.int32), 1, rows_group)

        if paired:
            order = [side, 1 - side]
            starts = [index(picture_start.reshape(2, 1), o, 0) for o in order]
            sizes = [index(picture_length.reshape(2, 1), o, 0) for o in order]
            seqs_each = 1
        else:
            starts, sizes, seqs_each = [picture_start], [picture_length], seqs
        chunks = len(starts)
        hb, pairs, _ = head_shapes(width)

        def flat(w):
            return w.transpose(1, 0, 2).reshape(w.shape[1], -1).astype(LOW)

        now = [()]

        def at(x):
            return after(x, *now[0])

        def done(*xs):
            now[0] = tuple(x for x in xs if x is not None)

        inputs_f = inputs.astype(F32)
        tail = 16
        forget_row = forget_weight.T.astype(LOW)
        forget_row = jnp.pad(forget_row, ((0, tail - heads), (0, 3 * width - rows_each)))
        pack = jnp.concatenate([flat(qkvg_weight[:3]), forget_row])
        ring_one = data.gather(pack, 1)
        ring_one.step()
        scale_one = rms_scale(inputs_f)
        normed_one = after((inputs_f * scale_one * attn_gain).astype(LOW), pack)
        low_go = jnp.concatenate([after(qkvg_weight[3], normed_one), out_weight.T], axis=1).astype(LOW)
        low_feed = jnp.concatenate([flat(after(gate_up, normed_one)), down_weight.T.astype(LOW)], axis=1)
        if paired:
            near, came = [normed_one, swap(normed_one, 1)], []
            for k in range(2):
                part = normed_one[k * local // 2:(k + 1) * local // 2]
                if k:
                    ring_one.step()
                    part = after(part, came[-1])
                    ring_one.step(came[-1])
                came.append(swap(part, 2))
            move_one = (near, jnp.concatenate(came))
        else:
            move_one = rows_start(normed_one)
        blocks = ring_one.all()
        w_qkv, w_tail = place([after(blocks[0], low_feed)] + blocks[1:], data.ahead, rows_each + tail, tail)
        w_forget = w_tail.reshape(dp, tail, -1)[:, :heads, :rows_each].transpose(1, 0, 2)
        w_forget = jnp.pad(w_forget.reshape(pairs, hb, dims), ((0, 0), (0, 8 - hb), (0, 0))).reshape(-1, dims)
        bias_local = index(forget_bias.reshape(tn, heads), rank, 0)
        bias_local = jnp.pad(bias_local.reshape(pairs, hb), ((0, 0), (0, 8 - hb))).reshape(-1, 1)
        w_feed = lax.all_gather(after(low_feed, blocks[-1], blocks[dp // 2]), "dp", axis=0, tiled=True)
        done(w_qkv)
        ring_go = data.gather(at(low_go), -1)
        ring_go.step()
        rows_one = [move_one[0]]
        if paired:
            rows_one.append(far(move_one))
        move_feed = rows_start(after(cotangent, rows_one[-1][0]))

        qkv, zf, attended, gate_sig, gated = ([None] * chunks for _ in range(5))
        for i in range(chunks):
            first = at(rows_one[i][0])
            qkv[i], zf[i] = project(pc, [first] + rows_one[i][1:], w_qkv, w_forget, bias_local)
            done(qkv[i])
        ring_go.step(qkv[-1])
        back, own = None, []
        feed_grad = [move_feed[0]]
        for i in reversed(range(chunks)):
            attended[i] = attend(starts[i], sizes[i], at(qkv[i]), zf[i], seqs_each)
            done(attended[i][0])
            ring_go.step(attended[i][0])
        w_go = place([at(ring_go.blocks[0])] + ring_go.all()[1:], data.ahead, rows_each)
        w_gate, w_out = w_go[:, :width], w_go[:, width:]
        if paired:
            feed_grad.append(far(move_feed))
        done(attended[0][0], w_go)
        for i in reversed(range(chunks)):
            gate_sig[i], gated[i], parts = close(
                pc, [at(rows_one[i][0])] + rows_one[i][1:], attended[i][0], w_gate, w_out
            )
            if back is None:
                sent, back = spread_far(parts)
                done(sent, feed_grad[-1][-1])
            else:
                own = spread_own(parts, back[0])
                done(gated[i], *own)
        middle = inputs_f + spread_sum(back, own)
        scale_two = rms_scale(middle)
        normed_two = (middle * scale_two * feed_gain).astype(LOW)
        move_two = rows_start(normed_two)

        hidden, grad_act, rows_two = ([None] * chunks for _ in range(3))
        done(w_feed)
        for i in range(chunks):
            rows_two[i] = far(move_two, *now[0]) if i else move_two[0]
            hidden[i], grad_act[i], parts = feed(
                pc, [at(rows_two[i][0])] + rows_two[i][1:], feed_grad[i], w_feed
            )
            done(hidden[i])
            if i == 0:
                own = spread_own(parts)
                done(hidden[i], *own)
            if i == chunks - 1:
                sent, back = spread_far(parts)
                done(sent)
        lefts = [[at(r[0])] + r[1:] for r in rows_two]
        groups = [
            [(r, (g, 2 * hidden_size, 0), False) for r, g in zip(lefts, grad_act)],
            [(y, (h, hidden_size, 0), False) for y, h in zip(feed_grad, hidden)],
        ]
        grad_feed = weight_grads(pc, groups, "grad_feed", 256)
        done(grad_feed)
        shard_feed = lax.psum_scatter(after(grad_feed, back[0]), "dp", scatter_dimension=0, tiled=True).astype(F32)
        shard_up, shard_down = shard_feed[:, :2 * hidden_size], shard_feed[:, 2 * hidden_size:]
        grad_two = spread_sum([after(back[0], grad_feed)], own)
        grad_middle, gain_two_grad = norm_back(grad_two, middle, scale_two, feed_gain)
        grad_middle = grad_middle + cotangent.astype(F32)
        grad_low = grad_middle.astype(LOW)
        done(grad_low)
        move_back = rows_start(grad_low)
        out_parts = [None] * chunks
        out_parts[-1] = feed_out(pc, at(hidden[-1]), w_feed)
        done(out_parts[-1][0])

        grad_gatepre, grad_proj, grad_zf, attn_grad = ([None] * chunks for _ in range(4))
        for i in range(chunks):
            attn_grad[i] = far(move_back, grad_proj[i - 1][0]) if i else move_back[0]
            up_stream, grad_gatepre[i] = open_back(
                pc, [at(attn_grad[i][0])] + attn_grad[i][1:], w_out, attended[i][0], gate_sig[i]
            )
            done(up_stream)
            if i == chunks - 1:
                groups = [
                    [([at(r[0])] + r[1:], (g, width, 0), True) for r, g in zip(rows_one, grad_gatepre)],
                    [(y, (g, width, 0), False) for y, g in zip(attn_grad, gated)],
                ]
                grad_go = weight_grads(pc, groups, "grad_gate_out", 512)
                done(grad_go)
                ring_go = data.reduce(grad_go.reshape(dp, rows_each, -1), 1)
                ring_go.step()
                sent, out_back = spread_far([after(p, attn_grad[i][-1]) for p in out_parts[-1]])
                done(grad_go, sent)
            *grad_proj[i], grad_zf[i] = attend_back(
                starts[i], sizes[i], qkv[i], zf[i], attended[i][1], attended[i][0], at(up_stream), seqs_each, 0, pairs
            )
            done(grad_proj[i][0])
            if i < chunks - 1:
                out_parts[i] = feed_out(pc, at(hidden[i]), w_feed)
                done(out_parts[i][0])
        ring_go.step(grad_proj[-1][0])
        bias_local_grad = sum(jnp.sum(z[:, :hb], axis=2).reshape(heads) for z in grad_zf)
        done(grad_proj[-1][0], *out_back)
        back, own = None, []
        for i in reversed(range(chunks)):
            g = list(grad_proj[i])
            parts = project_back(pc, [at(g[0])] + g[1:] + [grad_gatepre[i]], grad_zf[i], w_qkv, w_gate, w_forget)
            if back is None:
                sent, back = spread_far(parts, 2)
                done(sent)
            else:
                own = spread_own(parts, back[-1])
                done(parts[0], back[0])
        ring_go.step(back[0])
        packed = project_grads(
            pc,
            [([at(r[0])] + r[1:], [(x, 0) for x in g], z) for r, g, z in zip(rows_one, grad_proj, grad_zf)],
            rows_each, tail, width,
        )
        packed = after(packed, back[-1])
        ring_go.step(packed)
        ring_qkv = data.reduce(packed, -1)
        ring_qkv.step()
        outputs = middle + spread_sum(out_back, spread_own(out_parts[0]) if paired else [])
        shard_go = ring_go.all()
        shard_gate, shard_out = shard_go[:, :width], shard_go[:, width:]
        shard_qkv = ring_qkv.all()
        shard_forget = shard_qkv[rows_each:rows_each + heads, :rows_each].T
        shard_qkv = shard_qkv[:rows_each]
        grad_one = spread_sum(back, own)
        grad_inputs, gain_one_grad = norm_back(grad_one, inputs_f, scale_one, attn_gain)
        input_grad = grad_inputs + grad_middle

        bias_full = jnp.where(jnp.arange(tn)[:, None] == rank, bias_local_grad[None], 0.0).reshape(-1)
        owned = (shard_qkv, shard_gate, shard_forget, shard_out, shard_up, shard_down)
        square = sum(jnp.sum(s * s) for s in owned)
        pad = 128 - forget_bias.shape[0] - 1
        packed = jnp.concatenate([gain_one_grad, gain_two_grad, bias_full, square[None], jnp.zeros((pad,), F32)])
        packed = sum_all(sum_all(packed.reshape(-1, 128), "tensor", tn), "dp", dp).reshape(-1)
        gain_one_sum, gain_two_sum = packed[:dims], packed[dims:2 * dims]
        bias_sum = packed[2 * dims:2 * dims + forget_bias.shape[0]]
        total = (
            packed[2 * dims + forget_bias.shape[0]]
            + jnp.sum(gain_one_sum * gain_one_sum)
            + jnp.sum(gain_two_sum * gain_two_sum)
            + jnp.sum(bias_sum * bias_sum)
        )
        grad_norm = jnp.sqrt(total)
        clip_scale = jnp.minimum(1.0, MAX_NORM / (grad_norm + 1e-06))

        def unflat(s, parts):
            return s.reshape(s.shape[0], parts, -1).transpose(1, 0, 2)

        def adam(weight, gradient, first_old, second_old, decay):
            return adam_step(weight, gradient, first_old, second_old, clip_scale, decay, dims)

        grad_attn = unflat(jnp.concatenate([shard_qkv, shard_gate], axis=1), 4)
        return (
            (outputs, input_grad, grad_norm)
            + adam(qkvg_weight, grad_attn, qkvg_first, qkvg_second, WEIGHT_DECAY)
            + adam(forget_weight, shard_forget, forget_first, forget_second, WEIGHT_DECAY)
            + adam(forget_bias, bias_sum, bias_first, bias_second, 0.0)
            + adam(out_weight, shard_out.T, out_first, out_second, WEIGHT_DECAY)
            + adam(gate_up, unflat(shard_up, 2), gateup_first, gateup_second, WEIGHT_DECAY)
            + adam(down_weight, shard_down.T, down_first, down_second, WEIGHT_DECAY)
            + adam(attn_gain, gain_one_sum, attngain_first, attngain_second, 0.0)
            + adam(feed_gain, gain_two_sum, feedgain_first, feedgain_second, 0.0)
        )

    return body


def solution(mesh):
    tokens = P(("dp", "tensor"), None)
    stack, tall, wide = P(None, "dp", "tensor"), P("dp", "tensor"), P("tensor", "dp")
    return jax.shard_map(
        make_body(mesh.shape["dp"], mesh.shape["tensor"]),
        mesh=mesh,
        in_specs=(tokens, tokens, P("dp"), P("dp"), stack, tall, P(), wide, stack, wide, P(), P())
        + (stack, stack, tall, tall, P(), P(), wide, wide, stack, stack, wide, wide, P(), P(), P(), P()),
        out_specs=(tokens, tokens, P())
        + (stack,) * 3 + (tall,) * 3 + (P(),) * 3 + (wide,) * 3 + (stack,) * 3 + (wide,) * 3 + (P(),) * 6,
        check_vma=False,
    )
```

```python
import functools

import jax
import jax.numpy as jnp
from jax import lax
from jax.experimental import pallas as pl
from jax.experimental.pallas import tpu as pltpu

HEAD_DIM = 64
PIECE = 256
LOG2E = 1.4426950408889634
LOW = jnp.bfloat16
F32 = jnp.float32
HIDE = -1e30
NT = (((1,), (1,)), ((), ()))
TN = (((0,), (0,)), ((), ()))


def mm(a, b, dims=(((1,), (0,)), ((), ()))):
    return lax.dot_general(a, b, dims, preferred_element_type=F32)


COST_SHARE = 1.0


def cost(flops, moved):
    return pl.CostEstimate(flops=int(flops * COST_SHARE), bytes_accessed=int(moved * COST_SHARE), transcendentals=0)


def split_three(x):
    hi = x.astype(LOW)
    rest = x - hi.astype(F32)
    mid = rest.astype(LOW)
    return hi, mid, (rest - mid.astype(F32)).astype(LOW)


def scan_rows(x, reverse):
    length = x.shape[1]
    row = lax.broadcasted_iota(jnp.int32, (PIECE, PIECE), 0)
    col = lax.broadcasted_iota(jnp.int32, (PIECE, PIECE), 1)
    tri = jnp.where(row >= col if reverse else row <= col, 1.0, 0.0).astype(LOW)
    count = length // PIECE
    out = [None] * count
    carry = None
    for b in reversed(range(count)) if reverse else range(count):
        part = x[:, b * PIECE:(b + 1) * PIECE]
        done = sum(mm(t, tri) for t in split_three(part))
        if carry is not None:
            done = done + carry
        out[b] = done
        carry = done[:, :1] if reverse else done[:, PIECE - 1:]
    return jnp.concatenate(out, axis=1)


def log_gate(zf):
    return jnp.minimum(zf, 0.0) - jnp.log1p(jnp.exp(-jnp.abs(zf)))


def attn_fwd_kernel(start, size, q_ref, k_ref, v_ref, zf_ref, o_ref, lse_ref, *, hb):
    s_at = pl.program_id(0)
    length, width = q_ref.shape
    count = length // PIECE
    first, extent = start[s_at], size[s_at]
    c_rows = scan_rows(log_gate(zf_ref[...]), False) * LOG2E
    c_cols = c_rows.T
    row = lax.broadcasted_iota(jnp.int32, (PIECE, PIECE), 0)
    col = lax.broadcasted_iota(jnp.int32, (PIECE, PIECE), 1)
    causal = col <= row
    lane = lax.broadcasted_iota(jnp.int32, (1, width), 1)
    mine = [(lane >= h * HEAD_DIM) & (lane < (h + 1) * HEAD_DIM) for h in range(hb)]
    spare = [((h + 1) % hb) * HEAD_DIM for h in range(hb)]
    if lse_ref.shape[0] > hb:
        lse_ref[...] = jnp.zeros(lse_ref.shape, F32)

    def block(i, wide):
        lo, hi = i * PIECE, (i + 1) * PIECE
        in_pic = (lo >= first) & (lo < first + extent)
        out, lse = None, None
        for h in range(hb):
            q = jnp.where(mine[h], q_ref[lo:hi, :], jnp.zeros((), LOW))
            c_row = c_rows[h:h + 1, :]
            c_col = c_cols[lo:hi, h:h + 1]
            base = c_row[:, lo:lo + 1]
            parts, spans = [], []
            if i:
                parts.append(mm(q, k_ref[0:lo, :], NT) + (base - c_row[:, :lo]))
                spans.append((0, lo))
            back = base - 2.0 * c_col
            other = jnp.where(in_pic, back + c_row[:, lo:hi], HIDE)
            parts.append(mm(q, k_ref[lo:hi, :], NT) + jnp.where(causal, base - c_row[:, lo:hi], other))
            spans.append((lo, hi))
            if wide:
                parts.append(mm(q, k_ref[hi:hi + PIECE, :], NT) + (back + c_row[:, hi:hi + PIECE]))
                spans.append((hi, hi + PIECE))
            peak = functools.reduce(jnp.maximum, [jnp.max(p, axis=1, keepdims=True) for p in parts])
            acc = None
            for p, (a, b) in zip(parts, spans):
                v = jnp.where(mine[h], v_ref[a:b, :], jnp.ones((), LOW))
                t = mm(jnp.exp2(p - peak).astype(LOW), v)
                acc = t if acc is None else acc + t
            total = acc[:, spare[h]:spare[h] + 1]
            o_h = acc / total
            l_h = jnp.broadcast_to(peak + jnp.log2(total), o_h.shape)
            out = o_h if out is None else jnp.where(mine[h], o_h, out)
            lse = l_h if lse is None else jnp.where(mine[h], l_h, lse)
        o_ref[lo:hi, :] = out
        turned = lse.T
        for h in range(hb):
            lse_ref[h:h + 1, lo:hi] = turned[h * HEAD_DIM:h * HEAD_DIM + 1, :]

    for i in range(count):
        if i + 1 < count:
            wide = (first == i * PIECE) & (extent > PIECE)
            pl.when(wide)(functools.partial(block, i, True))
            pl.when(jnp.logical_not(wide))(functools.partial(block, i, False))
        else:
            block(i, False)


def attn_bwd_kernel(start, size, q_ref, k_ref, v_ref, zf_ref, lse_ref, o_ref, do_ref,
                    dq_ref, dk_ref, dv_ref, dzf_ref, dk_acc, dv_acc, dc_acc, *, hb):
    s_at = pl.program_id(0)
    length, width = q_ref.shape
    count = length // PIECE
    first, extent = start[s_at], size[s_at]
    zf = zf_ref[...]
    c_rows = scan_rows(log_gate(zf), False) * LOG2E
    c_cols = c_rows.T
    row = lax.broadcasted_iota(jnp.int32, (PIECE, PIECE), 0)
    col = lax.broadcasted_iota(jnp.int32, (PIECE, PIECE), 1)
    causal = row <= col
    lane = lax.broadcasted_iota(jnp.int32, (1, width), 1)
    mine = [(lane >= h * HEAD_DIM) & (lane < (h + 1) * HEAD_DIM) for h in range(hb)]
    spare = [((h + 1) % hb) * HEAD_DIM for h in range(hb)]
    zero, one = jnp.zeros((), LOW), jnp.ones((), LOW)
    dk_acc[...] = jnp.zeros(dk_acc.shape, F32)
    dv_acc[...] = jnp.zeros(dv_acc.shape, F32)
    prod = do_ref[...].astype(F32) * o_ref[...].astype(F32)
    head_row = lax.broadcasted_iota(jnp.int32, (8, width), 0)
    head_lane = lax.broadcasted_iota(jnp.int32, (8, width), 1)
    pick = jnp.where((head_lane >= head_row * HEAD_DIM) & (head_lane < (head_row + 1) * HEAD_DIM), 1.0, 0.0).astype(LOW)
    p_hi = prod.astype(LOW)
    p_lo = (prod - p_hi.astype(F32)).astype(LOW)
    delta = mm(pick, p_hi, NT) + mm(pick, p_lo, NT)

    def block(i, wide):
        lo, hi = i * PIECE, (i + 1) * PIECE
        in_pic = (lo >= first) & (lo < first + extent)
        out = None
        for h in range(hb):
            q_all = q_ref[lo:hi, :]
            q = jnp.where(mine[h], q_all, zero)
            q_one = jnp.where(mine[h], q_all, one)
            do = jnp.where(mine[h], do_ref[lo:hi, :], zero)
            c_row = c_rows[h:h + 1, lo:hi]
            base = c_row[:, :1]
            lse = lse_ref[h:h + 1, lo:hi]
            dl = delta[h:h + 1, lo:hi]
            back = base - 2.0 * c_row - lse
            acc = None
            todo = ([(0, lo, 0)] if i else []) + [(lo, hi, 1)] + ([(hi, hi + PIECE, 2)] if wide else [])
            for a, b, kind in todo:
                c_col = c_cols[a:b, h:h + 1]
                st = mm(k_ref[a:b, :], q, NT)
                if kind == 0:
                    st = st + (base - c_col) - lse
                elif kind == 1:
                    other = jnp.where(in_pic, back + c_col, HIDE)
                    st = st + jnp.where(causal, (base - c_col) - lse, other)
                else:
                    st = st + (back + c_col)
                p = jnp.exp2(st)
                ds = p * (mm(v_ref[a:b, :], do, NT) - dl)
                ds = ds.astype(LOW)
                dv_acc[a:b, :] += mm(p.astype(LOW), do)
                k_one = jnp.where(mine[h], k_ref[a:b, :], one)
                if kind == 2:
                    q_one = jnp.where(mine[h], q_all, -one)
                    k_one = jnp.where(mine[h], k_ref[a:b, :], -one)
                dk_acc[h, a:b, :] += mm(ds, q_one)
                t = mm(ds, k_one, TN)
                acc = t if acc is None else acc + t
                if kind == 1:
                    def signs(ds=ds, lo=lo, hi=hi, h=h):
                        minus = jnp.where(causal, zero, ds)
                        m2 = jnp.where(mine[h], zero, jnp.full((), -2.0, LOW))
                        m2 = jnp.broadcast_to(m2, (PIECE, width))
                        dk_acc[h, lo:hi, :] += mm(minus, m2)
                        dc_acc[h] = mm(minus, m2, TN)
                    def none(h=h):
                        dc_acc[h] = jnp.zeros((PIECE, width), F32)
                    pl.when(in_pic)(signs)
                    pl.when(jnp.logical_not(in_pic))(none)
                    acc = acc + dc_acc[h]
            out = acc if out is None else jnp.where(mine[h], acc, out)
            dc_row = acc.T[spare[h]:spare[h] + 1, :]
            dzf_ref[h:h + 1, lo:hi] = dc_row
        dq_ref[lo:hi, :] = (out * HEAD_DIM ** -0.5).astype(LOW)

    if dzf_ref.shape[0] > hb:
        dzf_ref[...] = jnp.zeros(dzf_ref.shape, F32)
    for i in range(count):
        if i + 1 < count:
            wide = (first == i * PIECE) & (extent > PIECE)
            pl.when(wide)(functools.partial(block, i, True))
            pl.when(jnp.logical_not(wide))(functools.partial(block, i, False))
        else:
            block(i, False)
    dv_ref[...] = dv_acc[...].astype(LOW)
    dk = dk_acc[0]
    for h in range(1, hb):
        dk = jnp.where(mine[h], dk_acc[h], dk)
    dk_ref[...] = (dk * (1.0 / LOG2E)).astype(LOW)
    for h in range(hb):
        turned = dk_acc[h].T
        dzf_ref[h:h + 1, :] -= turned[spare[h]:spare[h] + 1, :]
    dlog = scan_rows(dzf_ref[...], True)
    dzf_ref[...] = (dlog * jax.nn.sigmoid(-zf)).astype(LOW).astype(F32)


def head_shapes(width):
    heads = width // HEAD_DIM
    hb = 2 if heads % 2 == 0 else heads
    return hb, heads // hb, hb * HEAD_DIM


def head_specs(qkv, seqs, first=0):
    tokens, width = qkv.shape[0], qkv.shape[1] // 3
    hb, pairs, bw = head_shapes(width)
    length = tokens // seqs

    def col(off):
        return pl.BlockSpec((length, bw), lambda s, p, *_: (s, off + p))

    def rows(off):
        return pl.BlockSpec((None, 8, length), lambda s, p, *_: (off + p, 0, s))

    if bw % 128:
        three, cols = [qkv[:, j * width:(j + 1) * width] for j in range(3)], [col(first)] * 3
    else:
        three, cols = [qkv] * 3, [col(j * pairs + first) for j in range(3)]
    return three, cols, col, rows


def attend(start, size, qkv, zf, seqs):
    tokens, width = qkv.shape[0], qkv.shape[1] // 3
    hb, pairs, bw = head_shapes(width)
    three, cols, col, rows = head_specs(qkv, seqs)
    work = tokens * tokens // seqs * width // HEAD_DIM
    return pl.pallas_call(
        functools.partial(attn_fwd_kernel, hb=hb),
        grid_spec=pltpu.PrefetchScalarGridSpec(
            num_scalar_prefetch=2,
            grid=(seqs, pairs),
            in_specs=cols + [rows(0)],
            out_specs=[col(0), rows(0)],
        ),
        out_shape=[
            jax.ShapeDtypeStruct((tokens, width), F32),
            jax.ShapeDtypeStruct((pairs, 8, tokens), F32),
        ],
        compiler_params=pltpu.CompilerParams(vmem_limit_bytes=40 * 2**20),
        cost_estimate=cost(1600 * work, tokens * width * 10),
        name="attend",
    )(start, size, *three, zf)


def attend_back(start, size, qkv, zf, lse, core, up, seqs, first, count):
    tokens, width = qkv.shape[0], qkv.shape[1] // 3
    hb, pairs, bw = head_shapes(width)
    length = tokens // seqs
    three, cols, col, rows = head_specs(qkv, seqs, first)
    work = tokens * tokens // seqs * hb * count
    return pl.pallas_call(
        functools.partial(attn_bwd_kernel, hb=hb),
        grid_spec=pltpu.PrefetchScalarGridSpec(
            num_scalar_prefetch=2,
            grid=(seqs, count),
            in_specs=cols + [rows(first), rows(first), col(first), col(first)],
            out_specs=[col(0)] * 3 + [rows(0)],
            scratch_shapes=[
                pltpu.VMEM((hb, length, bw), F32),
                pltpu.VMEM((length, bw), F32),
                pltpu.VMEM((hb, PIECE, bw), F32),
            ],
        ),
        out_shape=[jax.ShapeDtypeStruct((tokens, count * bw), LOW)] * 3
        + [jax.ShapeDtypeStruct((count, 8, tokens), F32)],
        compiler_params=pltpu.CompilerParams(vmem_limit_bytes=40 * 2**20),
        cost_estimate=cost(2600 * work, tokens * count * bw * 20),
        name="attend_back",
    )(start, size, *three, zf, lse, core, up)


BLOCK = 256


class Pieces:
    def __init__(self, half, count, rows):
        self.half, self.count, self.rows = half, count, rows
        self.block = min(BLOCK, rows)
        self.each = rows // self.block
        self.steps = count * self.each

    def first(self, p):
        return (self.count - 1 - p) * self.each

    def inside(self, p, i):
        return jnp.clip(i - self.first(p), 0, self.each - 1)

    def active(self, p, i):
        return (i >= self.first(p)) & (i < self.first(p) + self.each)

    def own_spec(self, p, n):
        return pl.BlockSpec((self.block, n), lambda i, *_: (self.inside(p, i), 0))

    def own_specs(self, n):
        return [self.own_spec(p, n) for p in range(self.count)]

    def true_at(self, i, half):
        return half[self.count - 1 - lax.div(i, self.each)] * self.each + lax.rem(i, self.each)

    def true_spec(self, n):
        return pl.BlockSpec((self.block, n), lambda i, half: (self.true_at(i, half), 0))

    def lane_spec(self, lead):
        return pl.BlockSpec(lead + (self.block,), lambda i, half: (0,) * len(lead) + (self.true_at(i, half),))

    def flat_spec(self, n):
        return pl.BlockSpec(
            (self.block, n),
            lambda i, *_: ((self.count - 1 - lax.div(i, self.each)) * self.each + lax.rem(i, self.each), 0),
        )

    def pick(self, refs, i):
        x = refs[0][...]
        for p in range(1, self.count):
            x = jnp.where(self.active(p, i), refs[p][...], x)
        return x

    def put(self, refs, i, value):
        for p in range(self.count):
            def write(p=p):
                refs[p][...] = value
            pl.when(self.active(p, i))(write)

    def shapes(self, n, dtype=LOW):
        return [jax.ShapeDtypeStruct((self.rows, n), dtype)] * self.count

    def all_rows(self):
        return self.count * self.rows

    def call(self, kernel, name, ins, in_specs, out_shapes, out_specs, flops):
        moved = sum(x.size * x.dtype.itemsize for x in ins) + sum(s.size * s.dtype.itemsize for s in out_shapes)
        return pl.pallas_call(
            kernel,
            grid_spec=pltpu.PrefetchScalarGridSpec(
                num_scalar_prefetch=1, grid=(self.steps,), in_specs=in_specs, out_specs=out_specs
            ),
            out_shape=out_shapes,
            compiler_params=pltpu.CompilerParams(vmem_limit_bytes=48 * 2**20),
            cost_estimate=cost(flops * 3 // 2, moved),
            name=name,
        )(self.half, *ins)


def whole(rows, n, at=0):
    return pl.BlockSpec((rows, n), lambda *_: (0, at), pipeline_mode=pl.Buffered(1))


def project(pc, xs, w, wf, bias, width):
    dims = w.shape[0]
    pairs = wf.shape[0] // 8

    def kernel(half, *refs):
        i = pl.program_id(0)
        w_ref, wf_ref, bias_ref, qkv_ref, sig_ref, zf_ref = refs[pc.count:]
        x = pc.pick(refs[:pc.count], i)
        q = mm(x, w_ref[:, :width]) * (HEAD_DIM**-0.5 * LOG2E)
        qkv_ref[:, :width] = q.astype(LOW)
        qkv_ref[:, width:] = mm(x, w_ref[:, width:3 * width]).astype(LOW)
        sig_ref[...] = jax.nn.sigmoid(mm(x, w_ref[:, 3 * width:]))
        z = mm(wf_ref[...], x, NT) + bias_ref[...]
        for p in range(pairs):
            zf_ref[p] = z[8 * p:8 * p + 8, :]

    rows = pc.all_rows()
    return pc.call(
        kernel, "project",
        list(xs) + [w, wf, bias],
        pc.own_specs(dims) + [whole(dims, 4 * width), whole(8 * pairs, dims), whole(8 * pairs, 1)],
        [
            jax.ShapeDtypeStruct((rows, 3 * width), LOW),
            jax.ShapeDtypeStruct((rows, width), F32),
            jax.ShapeDtypeStruct((pairs, 8, rows), F32),
        ],
        [pc.true_spec(3 * width), pc.true_spec(width), pc.lane_spec((pairs, 8))],
        8 * rows * dims * width,
    )


def close(pc, core, sig, w_out):
    dims, width = w_out.shape

    def kernel(half, core_ref, sig_ref, w_ref, gated_ref, *parts):
        g = (core_ref[...] * sig_ref[...]).astype(LOW)
        gated_ref[...] = g
        pc.put(parts, pl.program_id(0), mm(g, w_ref[...], NT).astype(LOW))

    rows = pc.all_rows()
    out = pc.call(
        kernel, "close",
        [core, sig, w_out],
        [pc.true_spec(width), pc.true_spec(width), whole(dims, width)],
        [jax.ShapeDtypeStruct((rows, width), LOW)] + pc.shapes(dims),
        [pc.flat_spec(width)] + pc.own_specs(dims),
        2 * rows * dims * width,
    )
    return out[0], out[1:]


def feed(pc, xs, ys, w):
    dims, hidden = w.shape[0], w.shape[1] // 3
    n = pc.count

    def kernel(half, *refs):
        i = pl.program_id(0)
        w_ref, hidden_ref, grad_ref = refs[2 * n:2 * n + 3]
        x, y = pc.pick(refs[:n], i), pc.pick(refs[n:2 * n], i)
        a = mm(x, w_ref[:, :hidden])
        sig = jax.nn.sigmoid(a)
        silu = a * sig
        b = mm(x, w_ref[:, hidden:2 * hidden])
        hidden_ref[...] = (silu * b).astype(LOW)
        gh = mm(y, w_ref[:, 2 * hidden:])
        grad_ref[:, :hidden] = (gh * b * sig * (1.0 + a * (1.0 - sig))).astype(LOW)
        grad_ref[:, hidden:] = (gh * silu).astype(LOW)
        pc.put(refs[2 * n + 3:], i, mm(grad_ref[...], w_ref[:, :2 * hidden], NT).astype(LOW))

    rows = pc.all_rows()
    out = pc.call(
        kernel, "feed",
        list(xs) + list(ys) + [w],
        pc.own_specs(dims) * 2 + [whole(dims, 3 * hidden)],
        [jax.ShapeDtypeStruct((rows, hidden), LOW), jax.ShapeDtypeStruct((rows, 2 * hidden), LOW)] + pc.shapes(dims),
        [pc.flat_spec(hidden), pc.flat_spec(2 * hidden)] + pc.own_specs(dims),
        10 * rows * dims * hidden,
    )
    return out[0], out[1], out[2:]


def feed_out(pc, hidden, w):
    dims, n = w.shape[0], w.shape[1] // 3

    def kernel(half, hidden_ref, w_ref, *parts):
        pc.put(parts, pl.program_id(0), mm(hidden_ref[...], w_ref[...], NT).astype(LOW))

    return pc.call(
        kernel, "feed_out", [hidden, w], [pc.flat_spec(n), whole(dims, n, 2)],
        pc.shapes(dims), pc.own_specs(dims), 2 * pc.all_rows() * dims * n,
    )


def open_back(pc, ys, w_out, core, sig):
    dims, width = w_out.shape

    def kernel(half, *refs):
        w_ref, core_ref, sig_ref, up_ref, gate_ref = refs[pc.count:]
        g = mm(pc.pick(refs[:pc.count], pl.program_id(0)), w_ref[...])
        s = sig_ref[...]
        up_ref[...] = (g * s).astype(LOW)
        gate_ref[...] = (g * core_ref[...] * s * (1.0 - s)).astype(LOW)

    rows = pc.all_rows()
    return pc.call(
        kernel, "open_back",
        list(ys) + [w_out, core, sig],
        pc.own_specs(dims) + [whole(dims, width), pc.true_spec(width), pc.true_spec(width)],
        [jax.ShapeDtypeStruct((rows, width), LOW)] * 2,
        [pc.true_spec(width)] * 2,
        2 * rows * dims * width,
    )


def project_back(pc, grads, dz, w, wf, width):
    dims = w.shape[0]
    pairs = dz.shape[0]
    n = len(grads)

    def kernel(half, *refs):
        dz_ref, w_ref, wf_ref = refs[n:n + 3]
        g = jnp.concatenate([r[...] for r in refs[:n]], axis=1)
        total = mm(g, w_ref[...], NT)
        z = jnp.concatenate([dz_ref[p] for p in range(pairs)], axis=0).astype(LOW)
        total = total + mm(z, wf_ref[...], TN)
        pc.put(refs[n + 3:], pl.program_id(0), total.astype(LOW))

    return pc.call(
        kernel, "project_back",
        list(grads) + [dz, w, wf],
        [pc.true_spec(g.shape[1]) for g in grads]
        + [pc.lane_spec((pairs, 8)), whole(dims, 4 * width), whole(8 * pairs, dims)],
        pc.shapes(dims), pc.own_specs(dims), 8 * pc.all_rows() * dims * width,
    )


def weight_grads(pc, groups, name, step):
    dims = groups[0][0][0][0].shape[1]
    ins, specs, plan, at = [], [], [], 0
    flops = 0
    for group in groups:
        terms = []
        for lefts, (right, n, c), true in group:
            for p, left in enumerate(lefts):
                terms.append((len(ins), len(ins) + 1))
                ins += [left, right]
                specs.append(pl.BlockSpec((pc.rows, step), lambda i, *_: (0, i)))
                if true:
                    spec = pl.BlockSpec((pc.rows, n), lambda i, half, p=p, c=c: (half[p], c), pipeline_mode=pl.Buffered(1))
                else:
                    spec = pl.BlockSpec((pc.rows, n), lambda i, *_, p=p, c=c: (p, c), pipeline_mode=pl.Buffered(1))
                specs.append(spec)
                flops += 2 * pc.rows * dims * n
        plan.append((terms, at, n))
        at += n

    def kernel(half, *refs):
        out = refs[-1]
        for terms, at, n in plan:
            total = None
            for a, b in terms:
                t = mm(refs[a][...], refs[b][...], TN)
                total = t if total is None else total + t
            out[:, at:at + n] = total.astype(LOW)

    return pl.pallas_call(
        kernel,
        grid_spec=pltpu.PrefetchScalarGridSpec(
            num_scalar_prefetch=1, grid=(dims // step,), in_specs=specs,
            out_specs=pl.BlockSpec((step, at), lambda i, *_: (i, 0)),
        ),
        out_shape=jax.ShapeDtypeStruct((dims, at), LOW),
        compiler_params=pltpu.CompilerParams(vmem_limit_bytes=50 * 2**20),
        cost_estimate=cost(flops * 3 // 2, dims * at * 6),
        name=name,
    )(pc.half, *ins)


def project_grads(pc, chunks, size, tail, heads_each):
    dims = chunks[0][0][0].shape[1]
    step = 384
    per = step // size
    n = sum(g.shape[1] for g in chunks[0][1][0])
    cols = len(chunks[0][1])
    pairs = chunks[0][2].shape[0]
    ins, specs, plan = [], [], []
    for lefts, grads, dz in chunks:
        for p, left in enumerate(lefts):
            at, groups = len(ins), []
            ins.append(left)
            specs.append(pl.BlockSpec((pc.rows, step), lambda i, *_: (0, i)))
            for group in grads:
                groups.append(range(len(ins), len(ins) + len(group)))
                for g in group:
                    ins.append(g)
                    specs.append(
                        pl.BlockSpec(
                            (pc.rows, g.shape[1]), lambda i, half, p=p: (half[p], 0), pipeline_mode=pl.Buffered(1)
                        )
                    )
            plan.append((at, groups, len(ins)))
            ins.append(dz)
            specs.append(pl.BlockSpec((pairs, 8, pc.rows), lambda i, half, p=p: (0, 0, half[p])))

    def kernel(half, *refs):
        out = refs[-1]
        for c in range(cols):
            total = None
            for at, groups, _ in plan:
                right = [refs[j][...] for j in groups[c]]
                right = jnp.concatenate(right, axis=1) if len(right) > 1 else right[0]
                t = mm(refs[at][...], right, TN)
                total = t if total is None else total + t
            total = total.astype(LOW)
            for b in range(per):
                out[b, :size, c * n:(c + 1) * n] = total[b * size:(b + 1) * size]
        total = None
        for at, _, z_at in plan:
            z = jnp.concatenate([refs[z_at][p] for p in range(pairs)], axis=0).astype(LOW)
            t = mm(z, refs[at][...])
            total = t if total is None else total + t
        heads = [total[8 * p:8 * p + heads_each] for p in range(pairs)]
        heads.append(jnp.zeros((tail - heads_each * pairs, step), F32))
        total = jnp.concatenate(heads, axis=0)
        for b in range(per):
            row = total[:, b * size:(b + 1) * size]
            row = jnp.concatenate([row, jnp.zeros((tail, cols * n - size), F32)], axis=1)
            out[b, size:, :] = row.astype(LOW)

    return pl.pallas_call(
        kernel,
        grid_spec=pltpu.PrefetchScalarGridSpec(
            num_scalar_prefetch=1, grid=(dims // step,), in_specs=specs,
            out_specs=pl.BlockSpec((per, size + tail, cols * n), lambda i, *_: (i, 0, 0)),
        ),
        out_shape=jax.ShapeDtypeStruct((dims // size, size + tail, cols * n), LOW),
        compiler_params=pltpu.CompilerParams(vmem_limit_bytes=50 * 2**20),
        cost_estimate=cost(12 * pc.rows * dims * cols * n, dims * cols * n * 6),
        name="project_grads",
    )(pc.half, *ins)


from jax.sharding import PartitionSpec as P

NORM_EPS = 1e-05
BETA_ONE = 0.9
BETA_TWO = 0.95
WEIGHT_DECAY = 0.1
ADAM_EPS = 1e-08
MAX_NORM = 1.0
STEP_COUNT = 10.0


def rms_scale(values):
    return lax.rsqrt(jnp.mean(values * values, axis=-1, keepdims=True) + NORM_EPS)


def norm_back(gradient, values, inv_scale, gain_row):
    normed = values * inv_scale
    scaled = gradient * gain_row
    backward = inv_scale * (scaled - normed * jnp.mean(scaled * normed, axis=-1, keepdims=True))
    return (backward, jnp.sum(gradient * normed, axis=0))


def adam_step(weight, gradient, first_old, second_old, clip_scale, decay_rate, width):
    learn_rate = 0.4 / width**0.5
    scaled = gradient * clip_scale
    first_new = BETA_ONE * first_old + (1.0 - BETA_ONE) * scaled
    second_new = BETA_TWO * second_old + (1.0 - BETA_TWO) * scaled * scaled
    update = (
        first_new
        / (1.0 - BETA_ONE**STEP_COUNT)
        / (jnp.sqrt(second_new / (1.0 - BETA_TWO**STEP_COUNT)) + ADAM_EPS)
    )
    return (-learn_rate * (update + decay_rate * weight), first_new, second_new)


def after(x, *done):
    return lax.optimization_barrier((x,) + done)[0]


def index(x, i, axis):
    return lax.dynamic_index_in_dim(x, i, axis, keepdims=False, allow_negative_indices=False)


class Ring:
    def __init__(self, axis, size):
        self.axis, self.size = axis, size
        if size == 8:
            self.table = list(range(0, size, 2)) + list(range(size - 1, 0, -2))
        else:
            self.table = list(range(size))
        spot = [self.table.index(i) for i in range(size)]
        ahead = [[self.table[(spot[i] + k) % size] for k in range(size)] for i in range(size)]
        self.ahead = index(jnp.asarray(ahead, jnp.int32), lax.axis_index(axis), 0)

    def step(self, x, way):
        n = self.size
        return lax.ppermute(x, self.axis, [(self.table[r], self.table[(r + way) % n]) for r in range(n)])

    def gather(self, x, way):
        return Gather(self, x, way)

    def reduce(self, x, way):
        return Reduce(self, x, way)


class Gather:
    def __init__(self, ring, x, way):
        self.ring, self.way, self.k = ring, way, 0
        self.blocks = {0: x}
        self.ends = [x, x]

    def step(self, *done):
        ring, n = self.ring, self.ring.size
        self.k += 1
        if self.k > 1 or done:
            self.ends = list(lax.optimization_barrier(tuple(self.ends) + done)[:2])
        self.ends[0] = ring.step(self.ends[0], self.way)
        self.blocks[-self.k * self.way % n] = self.ends[0]
        if self.k <= (n - 1) // 2:
            self.ends[1] = ring.step(self.ends[1], -self.way)
            self.blocks[self.k * self.way % n] = self.ends[1]
        return self.ends

    def all(self):
        while self.k < self.ring.size // 2:
            self.step()
        return [self.blocks[k] for k in range(self.ring.size)]


class Reduce:
    def __init__(self, ring, x, way):
        self.ring, self.x, self.k = ring, x, 0
        n = ring.size
        self.ways = ((way, n // 2), (-way, (n - 1) // 2))
        self.moving = [None, None]

    def block(self, k):
        return index(self.x, index(self.ring.ahead, k % self.ring.size, 0), 0)

    def step(self, *done):
        self.k += 1
        if self.k > 1:
            tied = lax.optimization_barrier(tuple(self.moving) + done)
            self.moving = list(tied[:2])
        for j, (way, far) in enumerate(self.ways):
            left = far - self.k + 1
            if left < 1:
                continue
            own = self.block(way * left)
            if self.k > 1:
                own = (self.moving[j].astype(F32) + own.astype(F32)).astype(LOW)
            self.moving[j] = self.ring.step(own, way)
        return self.moving

    def all(self):
        while self.k < self.ring.size // 2:
            self.step()
        return sum(m.astype(F32) for m in self.moving if m is not None) + self.block(0).astype(F32)


def sum_all(x, axis, size):
    bit = 1
    while bit < size:
        x = x + lax.ppermute(x, axis, [(i, i ^ bit) for i in range(size)])
        bit *= 2
    return x


def place_kernel(where, *refs, arrays, size, rows, tail):
    out, sem = refs[arrays], refs[-1]
    copies = []
    block = 0
    for ref in refs[:arrays]:
        for j in range(ref.shape[0] // size):
            spans = [(out, rows, j * size)] + ([(refs[arrays + 1], tail, j * size + rows)] if tail else [])
            for to, count, at in spans:
                to_at = pl.multiple_of(where[block] * count, count)
                copies.append(
                    pltpu.make_async_copy(
                        ref.at[pl.ds(at, count), :], to.at[pl.ds(to_at, count), :], sem.at[len(copies)]
                    )
                )
            block += 1
    for copy in copies:
        copy.start()
    for copy in copies:
        copy.wait()


def place(parts, where, size, tail=0):
    n = parts[0].shape[1]
    count = sum(p.shape[0] for p in parts) // size
    shapes = [jax.ShapeDtypeStruct((count * r, n), LOW) for r in (size - tail, tail) if r]
    out = pl.pallas_call(
        functools.partial(place_kernel, arrays=len(parts), size=size, rows=size - tail, tail=tail),
        in_specs=[pl.BlockSpec(memory_space=pltpu.SMEM)] + [pl.BlockSpec(memory_space=pl.ANY)] * len(parts),
        out_specs=[pl.BlockSpec(memory_space=pltpu.VMEM)] * len(shapes),
        out_shape=shapes,
        scratch_shapes=[pltpu.SemaphoreType.DMA((2 * count,))],
        compiler_params=pltpu.CompilerParams(vmem_limit_bytes=40 * 2**20),
        cost_estimate=cost(0, 4 * count * size * n),
        name="place",
    )(where, *parts)
    return out if tail else out[0]


def make_body(dp, tn):
    def body(
        inputs, cotangent, picture_start, picture_length,
        qkvg_weight, forget_weight, forget_bias, out_weight, gate_up, down_weight,
        attn_gain, feed_gain,
        qkvg_first, qkvg_second, forget_first, forget_second, bias_first, bias_second,
        out_first, out_second, gateup_first, gateup_second, down_first, down_second,
        attngain_first, attngain_second, feedgain_first, feedgain_second,
    ):
        dims = inputs.shape[1]
        local, rank_rows, width = inputs.shape[0], qkvg_weight.shape[1], qkvg_weight.shape[2]
        hidden_size = gate_up.shape[2]
        heads = forget_weight.shape[1]
        seqs = picture_start.shape[0]
        rows_group = local * tn
        length = rows_group // seqs
        data = Ring("dp", dp)
        rank = lax.axis_index("tensor")
        paired = tn == 4 and local * 2 == length
        core, side = lax.rem(rank, 2), lax.div(rank, 2)
        rows_each = dims // dp

        def swap(x, bit):
            return lax.ppermute(x, "tensor", [(i, i ^ bit) for i in range(tn)])

        def rows_start(x):
            if not paired:
                return [lax.all_gather(x, "tensor", axis=0, tiled=True)], None
            return [x, swap(x, 1)], swap(x, 2)

        def far(moved, *done):
            there = after(moved[1], *done) if done else moved[1]
            return [there, swap(there, 1)]

        def spread_far(parts, count=1):
            if not paired:
                return parts[0], [lax.psum_scatter(parts[0], "tensor", scatter_dimension=0, tiled=True)]
            both = (parts[0].astype(F32) + swap(parts[1], 1).astype(F32)).astype(LOW)
            came, size = [], local // count
            for k in range(count):
                came.append(swap(after(both[k * size:(k + 1) * size], *came[-1:]), 2))
            return both, came

        def spread_own(parts, *done):
            return [parts[0], swap(after(parts[1], *done), 1)] if paired else []

        def spread_sum(back, own):
            total = jnp.concatenate(back).astype(F32)
            for p in own:
                total = total + p.astype(F32)
            return total

        if paired:
            pc = Pieces(jnp.stack([core, 1 - core]).astype(jnp.int32), 2, local)
        else:
            pc = Pieces(jnp.zeros((1,), jnp.int32), 1, rows_group)

        if paired:
            order = [side, 1 - side]
            starts = [index(picture_start.reshape(2, 1), o, 0) for o in order]
            sizes = [index(picture_length.reshape(2, 1), o, 0) for o in order]
            seqs_each = 1
        else:
            starts, sizes, seqs_each = [picture_start], [picture_length], seqs
        chunks = len(starts)
        hb, pairs, _ = head_shapes(width)

        def flat(w):
            return w.transpose(1, 0, 2).reshape(w.shape[1], -1).astype(LOW)

        now = [()]

        def at(x):
            return after(x, *now[0])

        def done(*xs):
            now[0] = tuple(x for x in xs if x is not None)

        inputs_f = inputs.astype(F32)
        tail = 16
        forget_row = forget_weight.T.astype(LOW)
        forget_row = jnp.pad(forget_row, ((0, tail - heads), (0, 5 * width - rows_each)))
        pack = jnp.concatenate([flat(qkvg_weight), out_weight.T.astype(LOW)], axis=1)
        pack = jnp.concatenate([pack, forget_row])
        ring_one = data.gather(pack, 1)
        ring_one.step()
        scale_one = rms_scale(inputs_f)
        normed_one = after((inputs_f * scale_one * attn_gain).astype(LOW), pack)
        low_feed = jnp.concatenate([flat(after(gate_up, normed_one)), down_weight.T.astype(LOW)], axis=1)
        if paired:
            near, came = [normed_one, swap(normed_one, 1)], []
            for k in range(2):
                part = normed_one[k * local // 2:(k + 1) * local // 2]
                if k:
                    ring_one.step()
                    part = after(part, came[-1])
                    ring_one.step(came[-1])
                came.append(swap(part, 2))
            move_one = (near, jnp.concatenate(came))
        else:
            move_one = rows_start(normed_one)
        while ring_one.k < dp // 2 - 1:
            ring_one.step()
        early = tuple(ring_one.ends)
        blocks = ring_one.all()
        w_one, w_tail = place([after(blocks[0], low_feed)] + blocks[1:], data.ahead, rows_each + tail, tail)
        w_out = w_one[:, 4 * width:]
        w_forget = w_tail.reshape(dp, tail, -1)[:, :heads, :rows_each].transpose(1, 0, 2)
        w_forget = jnp.pad(w_forget.reshape(pairs, hb, dims), ((0, 0), (0, 8 - hb), (0, 0))).reshape(-1, dims)
        bias_local = index(forget_bias.reshape(tn, heads), rank, 0)
        bias_local = jnp.pad(bias_local.reshape(pairs, hb), ((0, 0), (0, 8 - hb))).reshape(-1, 1)
        w_feed = lax.all_gather(after(low_feed, *early), "dp", axis=0, tiled=True)
        done(w_one)
        rows_one = [move_one[0]]
        if paired:
            rows_one.append(far(move_one))
        move_feed = rows_start(after(cotangent, rows_one[-1][0]))

        qkv, zf, attended, gate_sig, gated = ([None] * chunks for _ in range(5))
        for i in range(chunks):
            first = at(rows_one[i][0])
            qkv[i], gate_sig[i], zf[i] = project(pc, [first] + rows_one[i][1:], w_one, w_forget, bias_local, width)
            done(qkv[i])
        back, own = None, []
        feed_grad = [move_feed[0]]
        for i in reversed(range(chunks)):
            attended[i] = attend(starts[i], sizes[i], at(qkv[i]), zf[i], seqs_each)
            done(attended[i][0])
            gated[i], parts = close(pc, at(attended[i][0]), gate_sig[i], w_out)
            if back is None:
                sent, back = spread_far(parts)
                if paired:
                    feed_grad.append(far(move_feed))
                done(sent, feed_grad[-1][-1])
            else:
                own = spread_own(parts, back[0])
                done(gated[i], *own)
        middle = inputs_f + spread_sum(back, own)
        scale_two = rms_scale(middle)
        normed_two = (middle * scale_two * feed_gain).astype(LOW)
        move_two = rows_start(normed_two)

        hidden, grad_act, rows_two = ([None] * chunks for _ in range(3))
        done(w_feed)
        for i in range(chunks):
            rows_two[i] = far(move_two, *now[0]) if i else move_two[0]
            hidden[i], grad_act[i], parts = feed(
                pc, [at(rows_two[i][0])] + rows_two[i][1:], feed_grad[i], w_feed
            )
            done(hidden[i])
            if i == 0:
                own = spread_own(parts)
                done(hidden[i], *own)
            if i == chunks - 1:
                sent, back = spread_far(parts)
                done(sent)
        lefts = [[at(r[0])] + r[1:] for r in rows_two]
        groups = [
            [(r, (g, 2 * hidden_size, 0), False) for r, g in zip(lefts, grad_act)],
            [(y, (h, hidden_size, 0), False) for y, h in zip(feed_grad, hidden)],
        ]
        grad_feed = weight_grads(pc, groups, "grad_feed", 256)
        done(grad_feed)
        shard_feed = lax.psum_scatter(after(grad_feed, back[0]), "dp", scatter_dimension=0, tiled=True)
        grad_two = spread_sum([after(back[0], grad_feed)], own)
        grad_middle, gain_two_grad = norm_back(grad_two, middle, scale_two, feed_gain)
        grad_middle = grad_middle + cotangent.astype(F32)
        grad_low = grad_middle.astype(LOW)
        done(grad_low)
        move_back = rows_start(grad_low)
        out_parts = [None] * chunks
        out_parts[-1] = feed_out(pc, at(hidden[-1]), w_feed)
        done(out_parts[-1][0])

        grad_gatepre, grad_proj, grad_zf, attn_grad = ([None] * chunks for _ in range(4))
        for i in range(chunks):
            attn_grad[i] = far(move_back, grad_proj[i - 1][0]) if i else move_back[0]
            up_stream, grad_gatepre[i] = open_back(
                pc, [at(attn_grad[i][0])] + attn_grad[i][1:], w_out, attended[i][0], gate_sig[i]
            )
            done(up_stream)
            if i == chunks - 1:
                groups = [
                    [([at(r[0])] + r[1:], (g, width, 0), True) for r, g in zip(rows_one, grad_gatepre)],
                    [(y, (g, width, 0), False) for y, g in zip(attn_grad, gated)],
                ]
                grad_go = weight_grads(pc, groups, "grad_gate_out", 512)
                done(grad_go)
                ring_go = data.reduce(grad_go.reshape(dp, rows_each, -1), 1)
                ring_go.step()
                sent, out_back = spread_far([after(p, attn_grad[i][-1]) for p in out_parts[-1]])
                done(grad_go, sent)
            *grad_proj[i], grad_zf[i] = attend_back(
                starts[i], sizes[i], qkv[i], zf[i], attended[i][1], attended[i][0], at(up_stream), seqs_each, 0, pairs
            )
            grad_proj[i] = [[g] for g in grad_proj[i]]
            done(grad_proj[i][0][0])
            if i < chunks - 1:
                out_parts[i] = feed_out(pc, at(hidden[i]), w_feed)
                done(out_parts[i][0])

        def going():
            return [m for m in ring_go.moving if m is not None]

        bias_local_grad = sum(jnp.sum(z[:, :hb], axis=2).reshape(heads) for z in grad_zf)
        done(grad_proj[-1][0][0], *going(), *out_back)
        ring_go.step(grad_proj[-1][0][0])

        def rows_back(i):
            g = [x for group in grad_proj[i] for x in group]
            return project_back(pc, [at(g[0])] + g[1:] + [grad_gatepre[i]], grad_zf[i], w_one, w_forget, width)

        parts = rows_back(chunks - 1)
        sent, back = spread_far(parts, 2)
        done(sent)
        packed = project_grads(
            pc, [([at(r[0])] + r[1:], g, z) for r, g, z in zip(rows_one, grad_proj, grad_zf)], rows_each, tail, hb
        )
        packed = after(packed, back[0], *going())
        ring_go.step(packed)
        ring_qkv = data.reduce(packed, -1)
        ring_qkv.step()
        own = []
        if paired:
            done(packed)
            parts = rows_back(0)
            own = spread_own(parts, back[-1])
            outputs = after(middle, parts[0]) + spread_sum(out_back, spread_own(out_parts[0]))
            ring_qkv.step(parts[0], *going())
            ring_go.step(parts[0])
            shard_feed = after(shard_feed, outputs).astype(F32)
            square_feed = jnp.sum(shard_feed * shard_feed)
            ring_qkv.step(outputs, *going())
        else:
            outputs = middle + spread_sum(out_back, [])
            shard_feed = shard_feed.astype(F32)
            square_feed = jnp.sum(shard_feed * shard_feed)
        shard_up, shard_down = shard_feed[:, :2 * hidden_size], shard_feed[:, 2 * hidden_size:]
        grad_one = spread_sum(back, own)
        grad_inputs, gain_one_grad = norm_back(grad_one, inputs_f, scale_one, attn_gain)
        input_grad = grad_inputs + grad_middle
        while ring_go.k < dp // 2:
            ring_go.step()
        shard_go = ring_go.all()
        square_go = jnp.sum(shard_go * shard_go)
        ring_qkv.step(square_feed, gain_one_grad)
        shard_gate, shard_out = shard_go[:, :width], shard_go[:, width:]
        shard_qkv = ring_qkv.all()
        shard_forget = shard_qkv[rows_each:rows_each + heads, :rows_each].T
        shard_qkv = shard_qkv[:rows_each]
        bias_full = jnp.where(jnp.arange(tn)[:, None] == rank, bias_local_grad[None], 0.0).reshape(-1)
        square = square_feed + square_go + sum(jnp.sum(s * s) for s in (shard_qkv, shard_forget))
        pad = 128 - forget_bias.shape[0] - 1
        packed = jnp.concatenate([gain_one_grad, gain_two_grad, bias_full, square[None], jnp.zeros((pad,), F32)])
        packed = sum_all(sum_all(packed.reshape(-1, 128), "tensor", tn), "dp", dp).reshape(-1)
        gain_one_sum, gain_two_sum = packed[:dims], packed[dims:2 * dims]
        bias_sum = packed[2 * dims:2 * dims + forget_bias.shape[0]]
        total = (
            packed[2 * dims + forget_bias.shape[0]]
            + jnp.sum(gain_one_sum * gain_one_sum)
            + jnp.sum(gain_two_sum * gain_two_sum)
            + jnp.sum(bias_sum * bias_sum)
        )
        grad_norm = jnp.sqrt(total)
        clip_scale = jnp.minimum(1.0, MAX_NORM / (grad_norm + 1e-06))

        def unflat(s, parts):
            return s.reshape(s.shape[0], parts, -1).transpose(1, 0, 2)

        def adam(weight, gradient, first_old, second_old, decay):
            return adam_step(weight, gradient, first_old, second_old, clip_scale, decay, dims)

        grad_attn = unflat(jnp.concatenate([shard_qkv, shard_gate], axis=1), 4)
        return (
            (outputs, input_grad, grad_norm)
            + adam(qkvg_weight, grad_attn, qkvg_first, qkvg_second, WEIGHT_DECAY)
            + adam(forget_weight, shard_forget, forget_first, forget_second, WEIGHT_DECAY)
            + adam(forget_bias, bias_sum, bias_first, bias_second, 0.0)
            + adam(out_weight, shard_out.T, out_first, out_second, WEIGHT_DECAY)
            + adam(gate_up, unflat(shard_up, 2), gateup_first, gateup_second, WEIGHT_DECAY)
            + adam(down_weight, shard_down.T, down_first, down_second, WEIGHT_DECAY)
            + adam(attn_gain, gain_one_sum, attngain_first, attngain_second, 0.0)
            + adam(feed_gain, gain_two_sum, feedgain_first, feedgain_second, 0.0)
        )

    return body


def solution(mesh):
    tokens = P(("dp", "tensor"), None)
    stack, tall, wide = P(None, "dp", "tensor"), P("dp", "tensor"), P("tensor", "dp")
    return jax.shard_map(
        make_body(mesh.shape["dp"], mesh.shape["tensor"]),
        mesh=mesh,
        in_specs=(tokens, tokens, P("dp"), P("dp"), stack, tall, P(), wide, stack, wide, P(), P())
        + (stack, stack, tall, tall, P(), P(), wide, wide, stack, stack, wide, wide, P(), P(), P(), P()),
        out_specs=(tokens, tokens, P())
        + (stack,) * 3 + (tall,) * 3 + (P(),) * 3 + (wide,) * 3 + (stack,) * 3 + (wide,) * 3 + (P(),) * 6,
        check_vma=False,
    )
```

```python
import functools

import jax
import jax.numpy as jnp
from jax import lax
from jax.experimental import pallas as pl
from jax.experimental.pallas import tpu as pltpu

HEAD_DIM = 64
PIECE = 256
LOG2E = 1.4426950408889634
LOW = jnp.bfloat16
F32 = jnp.float32
HIDE = -1e30
NT = (((1,), (1,)), ((), ()))
TN = (((0,), (0,)), ((), ()))


def mm(a, b, dims=(((1,), (0,)), ((), ()))):
    return lax.dot_general(a, b, dims, preferred_element_type=F32)


COST_SHARE = 1.0


def cost(flops, moved):
    return pl.CostEstimate(flops=int(flops * COST_SHARE), bytes_accessed=int(moved * COST_SHARE), transcendentals=0)


def split_three(x):
    hi = x.astype(LOW)
    rest = x - hi.astype(F32)
    mid = rest.astype(LOW)
    return hi, mid, (rest - mid.astype(F32)).astype(LOW)


def scan_rows(x, reverse):
    length = x.shape[1]
    row = lax.broadcasted_iota(jnp.int32, (PIECE, PIECE), 0)
    col = lax.broadcasted_iota(jnp.int32, (PIECE, PIECE), 1)
    tri = jnp.where(row >= col if reverse else row <= col, 1.0, 0.0).astype(LOW)
    count = length // PIECE
    out = [None] * count
    carry = None
    for b in reversed(range(count)) if reverse else range(count):
        part = x[:, b * PIECE:(b + 1) * PIECE]
        done = sum(mm(t, tri) for t in split_three(part))
        if carry is not None:
            done = done + carry
        out[b] = done
        carry = done[:, :1] if reverse else done[:, PIECE - 1:]
    return jnp.concatenate(out, axis=1)


def log_gate(zf):
    return jnp.minimum(zf, 0.0) - jnp.log1p(jnp.exp(-jnp.abs(zf)))


def attn_fwd_kernel(start, size, q_ref, k_ref, v_ref, zf_ref, o_ref, lse_ref, *, hb):
    s_at = pl.program_id(0)
    length, width = q_ref.shape
    count = length // PIECE
    first, extent = start[s_at], size[s_at]
    c_rows = scan_rows(log_gate(zf_ref[...]), False) * LOG2E
    c_cols = c_rows.T
    row = lax.broadcasted_iota(jnp.int32, (PIECE, PIECE), 0)
    col = lax.broadcasted_iota(jnp.int32, (PIECE, PIECE), 1)
    causal = col <= row
    lane = lax.broadcasted_iota(jnp.int32, (1, width), 1)
    mine = [(lane >= h * HEAD_DIM) & (lane < (h + 1) * HEAD_DIM) for h in range(hb)]
    spare = [((h + 1) % hb) * HEAD_DIM for h in range(hb)]
    if lse_ref.shape[0] > hb:
        lse_ref[...] = jnp.zeros(lse_ref.shape, F32)

    def stack(rows):
        return jnp.concatenate([jnp.broadcast_to(r, (PIECE, r.shape[1])) for r in rows], axis=0)

    causal = jnp.concatenate([causal] * hb, axis=0)
    heads = range(hb)
    spans_of = [slice(h * PIECE, (h + 1) * PIECE) for h in heads]

    def block(i, wide):
        lo, hi = i * PIECE, (i + 1) * PIECE
        in_pic = (lo >= first) & (lo < first + extent)
        q_all = q_ref[lo:hi, :]
        q = jnp.concatenate([jnp.where(m, q_all, jnp.zeros((), LOW)) for m in mine], axis=0)
        c_row = [c_rows[h:h + 1, :] for h in heads]
        base = [c_row[h][:, lo:lo + 1] for h in heads]
        back = jnp.concatenate([base[h] - 2.0 * c_cols[lo:hi, h:h + 1] for h in heads], axis=0)
        parts, spans = [], []
        if i:
            parts.append(mm(q, k_ref[0:lo, :], NT) + stack([base[h] - c_row[h][:, :lo] for h in heads]))
            spans.append((0, lo))
        ahead = stack([base[h] - c_row[h][:, lo:hi] for h in heads])
        other = jnp.where(in_pic, back + stack([c_row[h][:, lo:hi] for h in heads]), HIDE)
        parts.append(mm(q, k_ref[lo:hi, :], NT) + jnp.where(causal, ahead, other))
        spans.append((lo, hi))
        if wide:
            more = stack([c_row[h][:, hi:hi + PIECE] for h in heads])
            parts.append(mm(q, k_ref[hi:hi + PIECE, :], NT) + (back + more))
            spans.append((hi, hi + PIECE))
        peak = functools.reduce(jnp.maximum, [jnp.max(p, axis=1, keepdims=True) for p in parts])
        acc = [None] * hb
        for p, (a, b) in zip(parts, spans):
            p = jnp.exp2(p - peak).astype(LOW)
            for h in heads:
                v = jnp.where(mine[h], v_ref[a:b, :], jnp.ones((), LOW))
                t = mm(p[spans_of[h]], v)
                acc[h] = t if acc[h] is None else acc[h] + t
        out, lse = None, None
        for h in heads:
            total = acc[h][:, spare[h]:spare[h] + 1]
            o_h = acc[h] / total
            l_h = jnp.broadcast_to(peak[spans_of[h]] + jnp.log2(total), o_h.shape)
            out = o_h if out is None else jnp.where(mine[h], o_h, out)
            lse = l_h if lse is None else jnp.where(mine[h], l_h, lse)
        o_ref[lo:hi, :] = out
        turned = lse.T
        for h in heads:
            lse_ref[h:h + 1, lo:hi] = turned[h * HEAD_DIM:h * HEAD_DIM + 1, :]

    for i in range(count):
        if i + 1 < count:
            wide = (first == i * PIECE) & (extent > PIECE)
            pl.when(wide)(functools.partial(block, i, True))
            pl.when(jnp.logical_not(wide))(functools.partial(block, i, False))
        else:
            block(i, False)


def attn_bwd_kernel(start, size, q_ref, k_ref, v_ref, zf_ref, lse_ref, o_ref, do_ref,
                    dq_ref, dk_ref, dv_ref, dzf_ref, dk_acc, dv_acc, dc_acc, *, hb):
    s_at = pl.program_id(0)
    length, width = q_ref.shape
    count = length // PIECE
    first, extent = start[s_at], size[s_at]
    zf = zf_ref[...]
    c_rows = scan_rows(log_gate(zf), False) * LOG2E
    c_cols = c_rows.T
    row = lax.broadcasted_iota(jnp.int32, (PIECE, PIECE), 0)
    col = lax.broadcasted_iota(jnp.int32, (PIECE, PIECE), 1)
    causal = row <= col
    lane = lax.broadcasted_iota(jnp.int32, (1, width), 1)
    mine = [(lane >= h * HEAD_DIM) & (lane < (h + 1) * HEAD_DIM) for h in range(hb)]
    spare = [((h + 1) % hb) * HEAD_DIM for h in range(hb)]
    zero, one = jnp.zeros((), LOW), jnp.ones((), LOW)
    dk_acc[...] = jnp.zeros(dk_acc.shape, F32)
    dv_acc[...] = jnp.zeros(dv_acc.shape, F32)
    prod = do_ref[...].astype(F32) * o_ref[...].astype(F32)
    head_row = lax.broadcasted_iota(jnp.int32, (8, width), 0)
    head_lane = lax.broadcasted_iota(jnp.int32, (8, width), 1)
    pick = jnp.where((head_lane >= head_row * HEAD_DIM) & (head_lane < (head_row + 1) * HEAD_DIM), 1.0, 0.0).astype(LOW)
    p_hi = prod.astype(LOW)
    p_lo = (prod - p_hi.astype(F32)).astype(LOW)
    delta = mm(pick, p_hi, NT) + mm(pick, p_lo, NT)

    heads = range(hb)
    parts_of = [slice(h * PIECE, (h + 1) * PIECE) for h in heads]
    causal_all = jnp.concatenate([causal] * hb, axis=1)

    def side(xs):
        return jnp.concatenate(xs, axis=1)

    def block(i, wide):
        lo, hi = i * PIECE, (i + 1) * PIECE
        in_pic = (lo >= first) & (lo < first + extent)
        q_all, do_all = q_ref[lo:hi, :], do_ref[lo:hi, :]
        q = jnp.concatenate([jnp.where(m, q_all, zero) for m in mine], axis=0)
        do = jnp.concatenate([jnp.where(m, do_all, zero) for m in mine], axis=0)
        c_row = [c_rows[h:h + 1, lo:hi] for h in heads]
        lse = side([lse_ref[h:h + 1, lo:hi] for h in heads])
        dl = side([delta[h:h + 1, lo:hi] for h in heads])
        base = side([jnp.broadcast_to(c[:, :1], (1, PIECE)) for c in c_row])
        ahead = base - lse
        back = ahead - 2.0 * side(c_row)
        acc = [None] * hb
        todo = ([(0, lo, 0)] if i else []) + [(lo, hi, 1)] + ([(hi, hi + PIECE, 2)] if wide else [])
        for a, b, kind in todo:
            c_col = side([jnp.broadcast_to(c_cols[a:b, h:h + 1], (b - a, PIECE)) for h in heads])
            st = mm(k_ref[a:b, :], q, NT)
            if kind == 0:
                st = st + (ahead - c_col)
            elif kind == 1:
                st = st + jnp.where(causal_all, ahead - c_col, jnp.where(in_pic, back + c_col, HIDE))
            else:
                st = st + (back + c_col)
            p = jnp.exp2(st)
            ds_all = (p * (mm(v_ref[a:b, :], do, NT) - dl)).astype(LOW)
            dv_acc[a:b, :] += mm(p.astype(LOW), do)
            mark = -one if kind == 2 else one
            for h in heads:
                ds = ds_all[:, parts_of[h]]
                dk_acc[h, a:b, :] += mm(ds, jnp.where(mine[h], q_all, mark))
                t = mm(ds, jnp.where(mine[h], k_ref[a:b, :], mark), TN)
                acc[h] = t if acc[h] is None else acc[h] + t
                if kind == 1:
                    def signs(ds=ds, h=h):
                        minus = jnp.where(causal, zero, ds)
                        m2 = jnp.where(mine[h], zero, jnp.full((), -2.0, LOW))
                        m2 = jnp.broadcast_to(m2, (PIECE, width))
                        dk_acc[h, lo:hi, :] += mm(minus, m2)
                        dc_acc[h] = mm(minus, m2, TN)
                    def none(h=h):
                        dc_acc[h] = jnp.zeros((PIECE, width), F32)
                    pl.when(in_pic)(signs)
                    pl.when(jnp.logical_not(in_pic))(none)
                    acc[h] = acc[h] + dc_acc[h]
        out = acc[0]
        for h in heads:
            out = jnp.where(mine[h], acc[h], out)
            dzf_ref[h:h + 1, lo:hi] = acc[h].T[spare[h]:spare[h] + 1, :]
        dq_ref[lo:hi, :] = (out * HEAD_DIM ** -0.5).astype(LOW)

    if dzf_ref.shape[0] > hb:
        dzf_ref[...] = jnp.zeros(dzf_ref.shape, F32)
    for i in range(count):
        if i + 1 < count:
            wide = (first == i * PIECE) & (extent > PIECE)
            pl.when(wide)(functools.partial(block, i, True))
            pl.when(jnp.logical_not(wide))(functools.partial(block, i, False))
        else:
            block(i, False)
    dv_ref[...] = dv_acc[...].astype(LOW)
    dk = dk_acc[0]
    for h in range(1, hb):
        dk = jnp.where(mine[h], dk_acc[h], dk)
    dk_ref[...] = (dk * (1.0 / LOG2E)).astype(LOW)
    for h in range(hb):
        turned = dk_acc[h].T
        dzf_ref[h:h + 1, :] -= turned[spare[h]:spare[h] + 1, :]
    dlog = scan_rows(dzf_ref[...], True)
    dzf_ref[...] = (dlog * jax.nn.sigmoid(-zf)).astype(LOW).astype(F32)


def head_shapes(width):
    heads = width // HEAD_DIM
    hb = 2 if heads % 2 == 0 else heads
    return hb, heads // hb, hb * HEAD_DIM


def head_specs(qkv, seqs, first=0):
    tokens, width = qkv.shape[0], qkv.shape[1] // 3
    hb, pairs, bw = head_shapes(width)
    length = tokens // seqs

    def col(off):
        return pl.BlockSpec((length, bw), lambda s, p, *_: (s, off + p))

    def rows(off):
        return pl.BlockSpec((None, 8, length), lambda s, p, *_: (off + p, 0, s))

    if bw % 128:
        three, cols = [qkv[:, j * width:(j + 1) * width] for j in range(3)], [col(first)] * 3
    else:
        three, cols = [qkv] * 3, [col(j * pairs + first) for j in range(3)]
    return three, cols, col, rows


def attend(start, size, qkv, zf, seqs):
    tokens, width = qkv.shape[0], qkv.shape[1] // 3
    hb, pairs, bw = head_shapes(width)
    three, cols, col, rows = head_specs(qkv, seqs)
    work = tokens * tokens // seqs * width // HEAD_DIM
    return pl.pallas_call(
        functools.partial(attn_fwd_kernel, hb=hb),
        grid_spec=pltpu.PrefetchScalarGridSpec(
            num_scalar_prefetch=2,
            grid=(seqs, pairs),
            in_specs=cols + [rows(0)],
            out_specs=[col(0), rows(0)],
        ),
        out_shape=[
            jax.ShapeDtypeStruct((tokens, width), F32),
            jax.ShapeDtypeStruct((pairs, 8, tokens), F32),
        ],
        compiler_params=pltpu.CompilerParams(vmem_limit_bytes=40 * 2**20),
        cost_estimate=cost(1600 * work, tokens * width * 10),
        name="attend",
    )(start, size, *three, zf)


def attend_back(start, size, qkv, zf, lse, core, up, seqs, first, count):
    tokens, width = qkv.shape[0], qkv.shape[1] // 3
    hb, pairs, bw = head_shapes(width)
    length = tokens // seqs
    three, cols, col, rows = head_specs(qkv, seqs, first)
    work = tokens * tokens // seqs * hb * count
    return pl.pallas_call(
        functools.partial(attn_bwd_kernel, hb=hb),
        grid_spec=pltpu.PrefetchScalarGridSpec(
            num_scalar_prefetch=2,
            grid=(seqs, count),
            in_specs=cols + [rows(first), rows(first), col(first), col(first)],
            out_specs=[col(0)] * 3 + [rows(0)],
            scratch_shapes=[
                pltpu.VMEM((hb, length, bw), F32),
                pltpu.VMEM((length, bw), F32),
                pltpu.VMEM((hb, PIECE, bw), F32),
            ],
        ),
        out_shape=[jax.ShapeDtypeStruct((tokens, count * bw), LOW)] * 3
        + [jax.ShapeDtypeStruct((count, 8, tokens), F32)],
        compiler_params=pltpu.CompilerParams(vmem_limit_bytes=40 * 2**20),
        cost_estimate=cost(2600 * work, tokens * count * bw * 20),
        name="attend_back",
    )(start, size, *three, zf, lse, core, up)


BLOCK = 256


class Pieces:
    def __init__(self, half, count, rows):
        self.half, self.count, self.rows = half, count, rows
        self.block = min(BLOCK, rows)
        self.each = rows // self.block
        self.steps = count * self.each

    def first(self, p):
        return (self.count - 1 - p) * self.each

    def inside(self, p, i):
        return jnp.clip(i - self.first(p), 0, self.each - 1)

    def active(self, p, i):
        return (i >= self.first(p)) & (i < self.first(p) + self.each)

    def own_spec(self, p, n):
        return pl.BlockSpec((self.block, n), lambda i, *_: (self.inside(p, i), 0))

    def own_specs(self, n):
        return [self.own_spec(p, n) for p in range(self.count)]

    def true_at(self, i, half):
        return half[self.count - 1 - lax.div(i, self.each)] * self.each + lax.rem(i, self.each)

    def true_spec(self, n):
        return pl.BlockSpec((self.block, n), lambda i, half: (self.true_at(i, half), 0))

    def lane_spec(self, lead):
        return pl.BlockSpec(lead + (self.block,), lambda i, half: (0,) * len(lead) + (self.true_at(i, half),))

    def flat_spec(self, n):
        return pl.BlockSpec(
            (self.block, n),
            lambda i, *_: ((self.count - 1 - lax.div(i, self.each)) * self.each + lax.rem(i, self.each), 0),
        )

    def pick(self, refs, i):
        x = refs[0][...]
        for p in range(1, self.count):
            x = jnp.where(self.active(p, i), refs[p][...], x)
        return x

    def put(self, refs, i, value):
        for p in range(self.count):
            def write(p=p):
                refs[p][...] = value
            pl.when(self.active(p, i))(write)

    def shapes(self, n, dtype=LOW):
        return [jax.ShapeDtypeStruct((self.rows, n), dtype)] * self.count

    def all_rows(self):
        return self.count * self.rows

    def call(self, kernel, name, ins, in_specs, out_shapes, out_specs, flops):
        moved = sum(x.size * x.dtype.itemsize for x in ins) + sum(s.size * s.dtype.itemsize for s in out_shapes)
        return pl.pallas_call(
            kernel,
            grid_spec=pltpu.PrefetchScalarGridSpec(
                num_scalar_prefetch=1, grid=(self.steps,), in_specs=in_specs, out_specs=out_specs
            ),
            out_shape=out_shapes,
            compiler_params=pltpu.CompilerParams(vmem_limit_bytes=48 * 2**20),
            cost_estimate=cost(flops * 3 // 2, moved),
            name=name,
        )(self.half, *ins)


def whole(rows, n, at=0):
    return pl.BlockSpec((rows, n), lambda *_: (0, at), pipeline_mode=pl.Buffered(1))


def project(pc, xs, w, wf, bias, width):
    dims = w.shape[0]
    pairs = wf.shape[0] // 8

    def kernel(half, *refs):
        i = pl.program_id(0)
        w_ref, wf_ref, bias_ref, qkv_ref, sig_ref, zf_ref = refs[pc.count:]
        x = pc.pick(refs[:pc.count], i)
        q = mm(x, w_ref[:, :width]) * (HEAD_DIM**-0.5 * LOG2E)
        qkv_ref[:, :width] = q.astype(LOW)
        qkv_ref[:, width:] = mm(x, w_ref[:, width:3 * width]).astype(LOW)
        sig_ref[...] = jax.nn.sigmoid(mm(x, w_ref[:, 3 * width:]))
        z = mm(wf_ref[...], x, NT) + bias_ref[...]
        for p in range(pairs):
            zf_ref[p] = z[8 * p:8 * p + 8, :]

    rows = pc.all_rows()
    return pc.call(
        kernel, "project",
        list(xs) + [w, wf, bias],
        pc.own_specs(dims) + [whole(dims, 4 * width), whole(8 * pairs, dims), whole(8 * pairs, 1)],
        [
            jax.ShapeDtypeStruct((rows, 3 * width), LOW),
            jax.ShapeDtypeStruct((rows, width), F32),
            jax.ShapeDtypeStruct((pairs, 8, rows), F32),
        ],
        [pc.true_spec(3 * width), pc.true_spec(width), pc.lane_spec((pairs, 8))],
        8 * rows * dims * width,
    )


def close(pc, core, sig, w_out):
    dims, width = w_out.shape

    def kernel(half, core_ref, sig_ref, w_ref, gated_ref, *parts):
        g = (core_ref[...] * sig_ref[...]).astype(LOW)
        gated_ref[...] = g
        pc.put(parts, pl.program_id(0), mm(g, w_ref[...], NT).astype(LOW))

    rows = pc.all_rows()
    out = pc.call(
        kernel, "close",
        [core, sig, w_out],
        [pc.true_spec(width), pc.true_spec(width), whole(dims, width)],
        [jax.ShapeDtypeStruct((rows, width), LOW)] + pc.shapes(dims),
        [pc.flat_spec(width)] + pc.own_specs(dims),
        2 * rows * dims * width,
    )
    return out[0], out[1:]


def feed(pc, xs, ys, w):
    dims, hidden = w.shape[0], w.shape[1] // 3
    n = pc.count

    def kernel(half, *refs):
        i = pl.program_id(0)
        w_ref, hidden_ref, grad_ref = refs[2 * n:2 * n + 3]
        x, y = pc.pick(refs[:n], i), pc.pick(refs[n:2 * n], i)
        a = mm(x, w_ref[:, :hidden])
        sig = jax.nn.sigmoid(a)
        silu = a * sig
        b = mm(x, w_ref[:, hidden:2 * hidden])
        hidden_ref[...] = (silu * b).astype(LOW)
        gh = mm(y, w_ref[:, 2 * hidden:])
        grad_ref[:, :hidden] = (gh * b * sig * (1.0 + a * (1.0 - sig))).astype(LOW)
        grad_ref[:, hidden:] = (gh * silu).astype(LOW)
        pc.put(refs[2 * n + 3:], i, mm(grad_ref[...], w_ref[:, :2 * hidden], NT).astype(LOW))

    rows = pc.all_rows()
    out = pc.call(
        kernel, "feed",
        list(xs) + list(ys) + [w],
        pc.own_specs(dims) * 2 + [whole(dims, 3 * hidden)],
        [jax.ShapeDtypeStruct((rows, hidden), LOW), jax.ShapeDtypeStruct((rows, 2 * hidden), LOW)] + pc.shapes(dims),
        [pc.flat_spec(hidden), pc.flat_spec(2 * hidden)] + pc.own_specs(dims),
        10 * rows * dims * hidden,
    )
    return out[0], out[1], out[2:]


def feed_out(pc, hidden, w):
    dims, n = w.shape[0], w.shape[1] // 3

    def kernel(half, hidden_ref, w_ref, *parts):
        pc.put(parts, pl.program_id(0), mm(hidden_ref[...], w_ref[...], NT).astype(LOW))

    return pc.call(
        kernel, "feed_out", [hidden, w], [pc.flat_spec(n), whole(dims, n, 2)],
        pc.shapes(dims), pc.own_specs(dims), 2 * pc.all_rows() * dims * n,
    )


def open_back(pc, ys, w_out, core, sig):
    dims, width = w_out.shape

    def kernel(half, *refs):
        w_ref, core_ref, sig_ref, up_ref, gate_ref = refs[pc.count:]
        g = mm(pc.pick(refs[:pc.count], pl.program_id(0)), w_ref[...])
        s = sig_ref[...]
        up_ref[...] = (g * s).astype(LOW)
        gate_ref[...] = (g * core_ref[...] * s * (1.0 - s)).astype(LOW)

    rows = pc.all_rows()
    return pc.call(
        kernel, "open_back",
        list(ys) + [w_out, core, sig],
        pc.own_specs(dims) + [whole(dims, width), pc.true_spec(width), pc.true_spec(width)],
        [jax.ShapeDtypeStruct((rows, width), LOW)] * 2,
        [pc.true_spec(width)] * 2,
        2 * rows * dims * width,
    )


def project_back(pc, grads, dz, w, wf, width):
    dims = w.shape[0]
    pairs = dz.shape[0]
    n = len(grads)

    def kernel(half, *refs):
        dz_ref, w_ref, wf_ref = refs[n:n + 3]
        g = jnp.concatenate([r[...] for r in refs[:n]], axis=1)
        total = mm(g, w_ref[...], NT)
        z = jnp.concatenate([dz_ref[p] for p in range(pairs)], axis=0).astype(LOW)
        total = total + mm(z, wf_ref[...], TN)
        pc.put(refs[n + 3:], pl.program_id(0), total.astype(LOW))

    return pc.call(
        kernel, "project_back",
        list(grads) + [dz, w, wf],
        [pc.true_spec(g.shape[1]) for g in grads]
        + [pc.lane_spec((pairs, 8)), whole(dims, 4 * width), whole(8 * pairs, dims)],
        pc.shapes(dims), pc.own_specs(dims), 8 * pc.all_rows() * dims * width,
    )


def weight_grads(pc, groups, name, step):
    dims = groups[0][0][0][0].shape[1]
    ins, specs, plan, at = [], [], [], 0
    flops = 0
    for group in groups:
        terms = []
        for lefts, (right, n, c), true in group:
            for p, left in enumerate(lefts):
                terms.append((len(ins), len(ins) + 1))
                ins += [left, right]
                specs.append(pl.BlockSpec((pc.rows, step), lambda i, *_: (0, i)))
                if true:
                    spec = pl.BlockSpec((pc.rows, n), lambda i, half, p=p, c=c: (half[p], c), pipeline_mode=pl.Buffered(1))
                else:
                    spec = pl.BlockSpec((pc.rows, n), lambda i, *_, p=p, c=c: (p, c), pipeline_mode=pl.Buffered(1))
                specs.append(spec)
                flops += 2 * pc.rows * dims * n
        plan.append((terms, at, n))
        at += n

    def kernel(half, *refs):
        out = refs[-1]
        for terms, at, n in plan:
            total = None
            for a, b in terms:
                t = mm(refs[a][...], refs[b][...], TN)
                total = t if total is None else total + t
            out[:, at:at + n] = total.astype(LOW)

    return pl.pallas_call(
        kernel,
        grid_spec=pltpu.PrefetchScalarGridSpec(
            num_scalar_prefetch=1, grid=(dims // step,), in_specs=specs,
            out_specs=pl.BlockSpec((step, at), lambda i, *_: (i, 0)),
        ),
        out_shape=jax.ShapeDtypeStruct((dims, at), LOW),
        compiler_params=pltpu.CompilerParams(vmem_limit_bytes=50 * 2**20),
        cost_estimate=cost(flops * 3 // 2, dims * at * 6),
        name=name,
    )(pc.half, *ins)


def project_grads(pc, chunks, size, tail, heads_each):
    dims = chunks[0][0][0].shape[1]
    step = 384
    per = step // size
    n = sum(g.shape[1] for g in chunks[0][1][0])
    cols = len(chunks[0][1])
    pairs = chunks[0][2].shape[0]
    ins, specs, plan = [], [], []
    for lefts, grads, dz in chunks:
        for p, left in enumerate(lefts):
            at, groups = len(ins), []
            ins.append(left)
            specs.append(pl.BlockSpec((pc.rows, step), lambda i, *_: (0, i)))
            for group in grads:
                groups.append(range(len(ins), len(ins) + len(group)))
                for g in group:
                    ins.append(g)
                    specs.append(
                        pl.BlockSpec(
                            (pc.rows, g.shape[1]), lambda i, half, p=p: (half[p], 0), pipeline_mode=pl.Buffered(1)
                        )
                    )
            plan.append((at, groups, len(ins)))
            ins.append(dz)
            specs.append(pl.BlockSpec((pairs, 8, pc.rows), lambda i, half, p=p: (0, 0, half[p])))

    def kernel(half, *refs):
        out = refs[-1]
        for c in range(cols):
            total = None
            for at, groups, _ in plan:
                right = [refs[j][...] for j in groups[c]]
                right = jnp.concatenate(right, axis=1) if len(right) > 1 else right[0]
                t = mm(refs[at][...], right, TN)
                total = t if total is None else total + t
            total = total.astype(LOW)
            for b in range(per):
                out[b, :size, c * n:(c + 1) * n] = total[b * size:(b + 1) * size]
        total = None
        for at, _, z_at in plan:
            z = jnp.concatenate([refs[z_at][p] for p in range(pairs)], axis=0).astype(LOW)
            t = mm(z, refs[at][...])
            total = t if total is None else total + t
        heads = [total[8 * p:8 * p + heads_each] for p in range(pairs)]
        heads.append(jnp.zeros((tail - heads_each * pairs, step), F32))
        total = jnp.concatenate(heads, axis=0)
        for b in range(per):
            row = total[:, b * size:(b + 1) * size]
            row = jnp.concatenate([row, jnp.zeros((tail, cols * n - size), F32)], axis=1)
            out[b, size:, :] = row.astype(LOW)

    return pl.pallas_call(
        kernel,
        grid_spec=pltpu.PrefetchScalarGridSpec(
            num_scalar_prefetch=1, grid=(dims // step,), in_specs=specs,
            out_specs=pl.BlockSpec((per, size + tail, cols * n), lambda i, *_: (i, 0, 0)),
        ),
        out_shape=jax.ShapeDtypeStruct((dims // size, size + tail, cols * n), LOW),
        compiler_params=pltpu.CompilerParams(vmem_limit_bytes=50 * 2**20),
        cost_estimate=cost(12 * pc.rows * dims * cols * n, dims * cols * n * 6),
        name="project_grads",
    )(pc.half, *ins)


from jax.sharding import PartitionSpec as P

NORM_EPS = 1e-05
BETA_ONE = 0.9
BETA_TWO = 0.95
WEIGHT_DECAY = 0.1
ADAM_EPS = 1e-08
MAX_NORM = 1.0
STEP_COUNT = 10.0


def rms_scale(values):
    return lax.rsqrt(jnp.mean(values * values, axis=-1, keepdims=True) + NORM_EPS)


def norm_back(gradient, values, inv_scale, gain_row):
    normed = values * inv_scale
    scaled = gradient * gain_row
    backward = inv_scale * (scaled - normed * jnp.mean(scaled * normed, axis=-1, keepdims=True))
    return (backward, jnp.sum(gradient * normed, axis=0))


def adam_step(weight, gradient, first_old, second_old, clip_scale, decay_rate, width):
    learn_rate = 0.4 / width**0.5
    scaled = gradient * clip_scale
    first_new = BETA_ONE * first_old + (1.0 - BETA_ONE) * scaled
    second_new = BETA_TWO * second_old + (1.0 - BETA_TWO) * scaled * scaled
    update = (
        first_new
        / (1.0 - BETA_ONE**STEP_COUNT)
        / (jnp.sqrt(second_new / (1.0 - BETA_TWO**STEP_COUNT)) + ADAM_EPS)
    )
    return (-learn_rate * (update + decay_rate * weight), first_new, second_new)


def after(x, *done):
    return lax.optimization_barrier((x,) + done)[0]


def index(x, i, axis):
    return lax.dynamic_index_in_dim(x, i, axis, keepdims=False, allow_negative_indices=False)


class Ring:
    def __init__(self, axis, size):
        self.axis, self.size = axis, size
        if size == 8:
            self.table = list(range(0, size, 2)) + list(range(size - 1, 0, -2))
        else:
            self.table = list(range(size))
        spot = [self.table.index(i) for i in range(size)]
        ahead = [[self.table[(spot[i] + k) % size] for k in range(size)] for i in range(size)]
        self.ahead = index(jnp.asarray(ahead, jnp.int32), lax.axis_index(axis), 0)

    def step(self, x, way):
        n = self.size
        return lax.ppermute(x, self.axis, [(self.table[r], self.table[(r + way) % n]) for r in range(n)])

    def gather(self, x, way):
        return Gather(self, x, way)

    def reduce(self, x, way):
        return Reduce(self, x, way)


class Gather:
    def __init__(self, ring, x, way):
        self.ring, self.way, self.k = ring, way, 0
        self.blocks = {0: x}
        self.ends = [x, x]

    def step(self, *done):
        ring, n = self.ring, self.ring.size
        self.k += 1
        if self.k > 1 or done:
            self.ends = list(lax.optimization_barrier(tuple(self.ends) + done)[:2])
        self.ends[0] = ring.step(self.ends[0], self.way)
        self.blocks[-self.k * self.way % n] = self.ends[0]
        if self.k <= (n - 1) // 2:
            self.ends[1] = ring.step(self.ends[1], -self.way)
            self.blocks[self.k * self.way % n] = self.ends[1]
        return self.ends

    def all(self):
        while self.k < self.ring.size // 2:
            self.step()
        return [self.blocks[k] for k in range(self.ring.size)]


class Reduce:
    def __init__(self, ring, x, way):
        self.ring, self.x, self.k = ring, x, 0
        n = ring.size
        self.ways = ((way, n // 2), (-way, (n - 1) // 2))
        self.moving = [None, None]

    def block(self, k):
        return index(self.x, index(self.ring.ahead, k % self.ring.size, 0), 0)

    def step(self, *done):
        self.k += 1
        if self.k > 1:
            tied = lax.optimization_barrier(tuple(self.moving) + done)
            self.moving = list(tied[:2])
        for j, (way, far) in enumerate(self.ways):
            left = far - self.k + 1
            if left < 1:
                continue
            own = self.block(way * left)
            if self.k > 1:
                own = (self.moving[j].astype(F32) + own.astype(F32)).astype(LOW)
            self.moving[j] = self.ring.step(own, way)
        return self.moving

    def all(self):
        while self.k < self.ring.size // 2:
            self.step()
        return sum(m.astype(F32) for m in self.moving if m is not None) + self.block(0).astype(F32)


def sum_all(x, axis, size):
    bit = 1
    while bit < size:
        x = x + lax.ppermute(x, axis, [(i, i ^ bit) for i in range(size)])
        bit *= 2
    return x


def place_kernel(where, *refs, arrays, size, rows, tail):
    out, sem = refs[arrays], refs[-1]
    copies = []
    block = 0
    for ref in refs[:arrays]:
        for j in range(ref.shape[0] // size):
            spans = [(out, rows, j * size)] + ([(refs[arrays + 1], tail, j * size + rows)] if tail else [])
            for to, count, at in spans:
                to_at = pl.multiple_of(where[block] * count, count)
                copies.append(
                    pltpu.make_async_copy(
                        ref.at[pl.ds(at, count), :], to.at[pl.ds(to_at, count), :], sem.at[len(copies)]
                    )
                )
            block += 1
    for copy in copies:
        copy.start()
    for copy in copies:
        copy.wait()


def place(parts, where, size, tail=0):
    n = parts[0].shape[1]
    count = sum(p.shape[0] for p in parts) // size
    shapes = [jax.ShapeDtypeStruct((count * r, n), LOW) for r in (size - tail, tail) if r]
    out = pl.pallas_call(
        functools.partial(place_kernel, arrays=len(parts), size=size, rows=size - tail, tail=tail),
        in_specs=[pl.BlockSpec(memory_space=pltpu.SMEM)] + [pl.BlockSpec(memory_space=pl.ANY)] * len(parts),
        out_specs=[pl.BlockSpec(memory_space=pltpu.VMEM)] * len(shapes),
        out_shape=shapes,
        scratch_shapes=[pltpu.SemaphoreType.DMA((2 * count,))],
        compiler_params=pltpu.CompilerParams(vmem_limit_bytes=40 * 2**20),
        cost_estimate=cost(0, 4 * count * size * n),
        name="place",
    )(where, *parts)
    return out if tail else out[0]


def make_body(dp, tn):
    def body(
        inputs, cotangent, picture_start, picture_length,
        qkvg_weight, forget_weight, forget_bias, out_weight, gate_up, down_weight,
        attn_gain, feed_gain,
        qkvg_first, qkvg_second, forget_first, forget_second, bias_first, bias_second,
        out_first, out_second, gateup_first, gateup_second, down_first, down_second,
        attngain_first, attngain_second, feedgain_first, feedgain_second,
    ):
        dims = inputs.shape[1]
        local, rank_rows, width = inputs.shape[0], qkvg_weight.shape[1], qkvg_weight.shape[2]
        hidden_size = gate_up.shape[2]
        heads = forget_weight.shape[1]
        seqs = picture_start.shape[0]
        rows_group = local * tn
        length = rows_group // seqs
        data = Ring("dp", dp)
        rank = lax.axis_index("tensor")
        paired = tn == 4 and local * 2 == length
        core, side = lax.rem(rank, 2), lax.div(rank, 2)
        rows_each = dims // dp

        def swap(x, bit):
            return lax.ppermute(x, "tensor", [(i, i ^ bit) for i in range(tn)])

        def rows_start(x):
            if not paired:
                return [lax.all_gather(x, "tensor", axis=0, tiled=True)], None
            return [x, swap(x, 1)], swap(x, 2)

        def far(moved, *done):
            there = after(moved[1], *done) if done else moved[1]
            return [there, swap(there, 1)]

        def spread_far(parts, count=1):
            if not paired:
                return parts[0], [lax.psum_scatter(parts[0], "tensor", scatter_dimension=0, tiled=True)]
            both = (parts[0].astype(F32) + swap(parts[1], 1).astype(F32)).astype(LOW)
            came, size = [], local // count
            for k in range(count):
                came.append(swap(after(both[k * size:(k + 1) * size], *came[-1:]), 2))
            return both, came

        def spread_own(parts, *done):
            return [parts[0], swap(after(parts[1], *done), 1)] if paired else []

        def spread_sum(back, own):
            total = jnp.concatenate(back).astype(F32)
            for p in own:
                total = total + p.astype(F32)
            return total

        if paired:
            pc = Pieces(jnp.stack([core, 1 - core]).astype(jnp.int32), 2, local)
        else:
            pc = Pieces(jnp.zeros((1,), jnp.int32), 1, rows_group)

        if paired:
            order = [side, 1 - side]
            starts = [index(picture_start.reshape(2, 1), o, 0) for o in order]
            sizes = [index(picture_length.reshape(2, 1), o, 0) for o in order]
            seqs_each = 1
        else:
            starts, sizes, seqs_each = [picture_start], [picture_length], seqs
        chunks = len(starts)
        hb, pairs, _ = head_shapes(width)

        def flat(w):
            return w.transpose(1, 0, 2).reshape(w.shape[1], -1).astype(LOW)

        now = [()]

        def at(x):
            return after(x, *now[0])

        def done(*xs):
            now[0] = tuple(x for x in xs if x is not None)

        inputs_f = inputs.astype(F32)
        tail = 16
        forget_row = forget_weight.T.astype(LOW)
        forget_row = jnp.pad(forget_row, ((0, tail - heads), (0, 5 * width - rows_each)))
        pack = jnp.concatenate([flat(qkvg_weight), out_weight.T.astype(LOW)], axis=1)
        pack = jnp.concatenate([pack, forget_row])
        ring_one = data.gather(pack, 1)
        ring_one.step()
        scale_one = rms_scale(inputs_f)
        normed_one = after((inputs_f * scale_one * attn_gain).astype(LOW), pack)
        low_feed = jnp.concatenate([flat(after(gate_up, normed_one)), down_weight.T.astype(LOW)], axis=1)
        if paired:
            near, came = [normed_one, swap(normed_one, 1)], []
            for k in range(2):
                part = normed_one[k * local // 2:(k + 1) * local // 2]
                if k:
                    ring_one.step()
                    part = after(part, came[-1])
                    ring_one.step(came[-1])
                came.append(swap(part, 2))
            move_one = (near, jnp.concatenate(came))
        else:
            move_one = rows_start(normed_one)
        while ring_one.k < dp // 2 - 1:
            ring_one.step()
        early = tuple(ring_one.ends)
        blocks = ring_one.all()
        w_one, w_tail = place([after(blocks[0], low_feed)] + blocks[1:], data.ahead, rows_each + tail, tail)
        w_out = w_one[:, 4 * width:]
        w_forget = w_tail.reshape(dp, tail, -1)[:, :heads, :rows_each].transpose(1, 0, 2)
        w_forget = jnp.pad(w_forget.reshape(pairs, hb, dims), ((0, 0), (0, 8 - hb), (0, 0))).reshape(-1, dims)
        bias_local = index(forget_bias.reshape(tn, heads), rank, 0)
        bias_local = jnp.pad(bias_local.reshape(pairs, hb), ((0, 0), (0, 8 - hb))).reshape(-1, 1)
        w_feed = lax.all_gather(after(low_feed, *early), "dp", axis=0, tiled=True)
        done(w_one)
        rows_one = [move_one[0]]
        if paired:
            rows_one.append(far(move_one))
        move_feed = rows_start(after(cotangent, rows_one[-1][0]))

        qkv, zf, attended, gate_sig, gated = ([None] * chunks for _ in range(5))
        for i in range(chunks):
            first = at(rows_one[i][0])
            qkv[i], gate_sig[i], zf[i] = project(pc, [first] + rows_one[i][1:], w_one, w_forget, bias_local, width)
            done(qkv[i])
        back, own = None, []
        feed_grad = [move_feed[0]]
        for i in reversed(range(chunks)):
            attended[i] = attend(starts[i], sizes[i], at(qkv[i]), zf[i], seqs_each)
            done(attended[i][0])
            gated[i], parts = close(pc, at(attended[i][0]), gate_sig[i], w_out)
            if back is None:
                sent, back = spread_far(parts)
                if paired:
                    feed_grad.append(far(move_feed))
                done(sent, feed_grad[-1][-1])
            else:
                own = spread_own(parts, back[0])
                done(gated[i], *own)
        middle = inputs_f + spread_sum(back, own)
        scale_two = rms_scale(middle)
        normed_two = (middle * scale_two * feed_gain).astype(LOW)
        move_two = rows_start(normed_two)

        hidden, grad_act, rows_two = ([None] * chunks for _ in range(3))
        done(w_feed)
        for i in range(chunks):
            rows_two[i] = far(move_two, *now[0]) if i else move_two[0]
            hidden[i], grad_act[i], parts = feed(
                pc, [at(rows_two[i][0])] + rows_two[i][1:], feed_grad[i], w_feed
            )
            done(hidden[i])
            if i == 0:
                own = spread_own(parts)
                done(hidden[i], *own)
            if i == chunks - 1:
                sent, back = spread_far(parts)
                done(sent)
        lefts = [[at(r[0])] + r[1:] for r in rows_two]
        groups = [
            [(r, (g, 2 * hidden_size, 0), False) for r, g in zip(lefts, grad_act)],
            [(y, (h, hidden_size, 0), False) for y, h in zip(feed_grad, hidden)],
        ]
        grad_feed = weight_grads(pc, groups, "grad_feed", 256)
        done(grad_feed)
        shard_feed = lax.psum_scatter(after(grad_feed, back[0]), "dp", scatter_dimension=0, tiled=True)
        grad_two = spread_sum([after(back[0], grad_feed)], own)
        grad_middle, gain_two_grad = norm_back(grad_two, middle, scale_two, feed_gain)
        grad_middle = grad_middle + cotangent.astype(F32)
        grad_low = grad_middle.astype(LOW)
        done(grad_low)
        move_back = rows_start(grad_low)
        out_parts = [None] * chunks
        out_parts[-1] = feed_out(pc, at(hidden[-1]), w_feed)
        done(out_parts[-1][0])

        grad_gatepre, grad_proj, grad_zf, attn_grad = ([None] * chunks for _ in range(4))
        for i in range(chunks):
            attn_grad[i] = far(move_back, grad_proj[i - 1][0]) if i else move_back[0]
            up_stream, grad_gatepre[i] = open_back(
                pc, [at(attn_grad[i][0])] + attn_grad[i][1:], w_out, attended[i][0], gate_sig[i]
            )
            done(up_stream)
            if i == chunks - 1:
                groups = [
                    [([at(r[0])] + r[1:], (g, width, 0), True) for r, g in zip(rows_one, grad_gatepre)],
                    [(y, (g, width, 0), False) for y, g in zip(attn_grad, gated)],
                ]
                grad_go = weight_grads(pc, groups, "grad_gate_out", 512)
                done(grad_go)
                ring_go = data.reduce(grad_go.reshape(dp, rows_each, -1), 1)
                ring_go.step()
                sent, out_back = spread_far([after(p, attn_grad[i][-1]) for p in out_parts[-1]])
                done(grad_go, sent)
            *grad_proj[i], grad_zf[i] = attend_back(
                starts[i], sizes[i], qkv[i], zf[i], attended[i][1], attended[i][0], at(up_stream), seqs_each, 0, pairs
            )
            grad_proj[i] = [[g] for g in grad_proj[i]]
            done(grad_proj[i][0][0])
            if i < chunks - 1:
                out_parts[i] = feed_out(pc, at(hidden[i]), w_feed)
                done(out_parts[i][0])

        def going():
            return [m for m in ring_go.moving if m is not None]

        bias_local_grad = sum(jnp.sum(z[:, :hb], axis=2).reshape(heads) for z in grad_zf)
        done(grad_proj[-1][0][0], *going(), *out_back)
        ring_go.step(grad_proj[-1][0][0])

        def rows_back(i):
            g = [x for group in grad_proj[i] for x in group]
            return project_back(pc, [at(g[0])] + g[1:] + [grad_gatepre[i]], grad_zf[i], w_one, w_forget, width)

        parts = rows_back(chunks - 1)
        sent, back = spread_far(parts, 2)
        done(sent)
        packed = project_grads(
            pc, [([at(r[0])] + r[1:], g, z) for r, g, z in zip(rows_one, grad_proj, grad_zf)], rows_each, tail, hb
        )
        packed = after(packed, back[0], *going())
        ring_go.step(packed)
        ring_qkv = data.reduce(packed, -1)
        ring_qkv.step()
        own = []
        if paired:
            done(packed)
            parts = rows_back(0)
            own = spread_own(parts, back[-1])
            outputs = after(middle, parts[0]) + spread_sum(out_back, spread_own(out_parts[0]))
            ring_qkv.step(parts[0], *going())
            ring_go.step(parts[0])
            shard_feed = after(shard_feed, outputs).astype(F32)
            square_feed = jnp.sum(shard_feed * shard_feed)
            ring_qkv.step(outputs, *going())
        else:
            outputs = middle + spread_sum(out_back, [])
            shard_feed = shard_feed.astype(F32)
            square_feed = jnp.sum(shard_feed * shard_feed)
        shard_up, shard_down = shard_feed[:, :2 * hidden_size], shard_feed[:, 2 * hidden_size:]
        grad_one = spread_sum(back, own)
        grad_inputs, gain_one_grad = norm_back(grad_one, inputs_f, scale_one, attn_gain)
        input_grad = grad_inputs + grad_middle
        while ring_go.k < dp // 2:
            ring_go.step()
        shard_go = ring_go.all()
        square_go = jnp.sum(shard_go * shard_go)
        ring_qkv.step(square_feed, gain_one_grad)
        shard_gate, shard_out = shard_go[:, :width], shard_go[:, width:]
        shard_qkv = ring_qkv.all()
        shard_forget = shard_qkv[rows_each:rows_each + heads, :rows_each].T
        shard_qkv = shard_qkv[:rows_each]
        bias_full = jnp.where(jnp.arange(tn)[:, None] == rank, bias_local_grad[None], 0.0).reshape(-1)
        square = square_feed + square_go + sum(jnp.sum(s * s) for s in (shard_qkv, shard_forget))
        pad = 128 - forget_bias.shape[0] - 1
        packed = jnp.concatenate([gain_one_grad, gain_two_grad, bias_full, square[None], jnp.zeros((pad,), F32)])
        packed = sum_all(sum_all(packed.reshape(-1, 128), "tensor", tn), "dp", dp).reshape(-1)
        gain_one_sum, gain_two_sum = packed[:dims], packed[dims:2 * dims]
        bias_sum = packed[2 * dims:2 * dims + forget_bias.shape[0]]
        total = (
            packed[2 * dims + forget_bias.shape[0]]
            + jnp.sum(gain_one_sum * gain_one_sum)
            + jnp.sum(gain_two_sum * gain_two_sum)
            + jnp.sum(bias_sum * bias_sum)
        )
        grad_norm = jnp.sqrt(total)
        clip_scale = jnp.minimum(1.0, MAX_NORM / (grad_norm + 1e-06))

        def unflat(s, parts):
            return s.reshape(s.shape[0], parts, -1).transpose(1, 0, 2)

        def adam(weight, gradient, first_old, second_old, decay):
            return adam_step(weight, gradient, first_old, second_old, clip_scale, decay, dims)

        grad_attn = unflat(jnp.concatenate([shard_qkv, shard_gate], axis=1), 4)
        return (
            (outputs, input_grad, grad_norm)
            + adam(qkvg_weight, grad_attn, qkvg_first, qkvg_second, WEIGHT_DECAY)
            + adam(forget_weight, shard_forget, forget_first, forget_second, WEIGHT_DECAY)
            + adam(forget_bias, bias_sum, bias_first, bias_second, 0.0)
            + adam(out_weight, shard_out.T, out_first, out_second, WEIGHT_DECAY)
            + adam(gate_up, unflat(shard_up, 2), gateup_first, gateup_second, WEIGHT_DECAY)
            + adam(down_weight, shard_down.T, down_first, down_second, WEIGHT_DECAY)
            + adam(attn_gain, gain_one_sum, attngain_first, attngain_second, 0.0)
            + adam(feed_gain, gain_two_sum, feedgain_first, feedgain_second, 0.0)
        )

    return body


def solution(mesh):
    tokens = P(("dp", "tensor"), None)
    stack, tall, wide = P(None, "dp", "tensor"), P("dp", "tensor"), P("tensor", "dp")
    return jax.shard_map(
        make_body(mesh.shape["dp"], mesh.shape["tensor"]),
        mesh=mesh,
        in_specs=(tokens, tokens, P("dp"), P("dp"), stack, tall, P(), wide, stack, wide, P(), P())
        + (stack, stack, tall, tall, P(), P(), wide, wide, stack, stack, wide, wide, P(), P(), P(), P()),
        out_specs=(tokens, tokens, P())
        + (stack,) * 3 + (tall,) * 3 + (P(),) * 3 + (wide,) * 3 + (stack,) * 3 + (wide,) * 3 + (P(),) * 6,
        check_vma=False,
    )
```

```python
import functools

import jax
import jax.numpy as jnp
from jax import lax
from jax.experimental import pallas as pl
from jax.experimental.pallas import tpu as pltpu

HEAD_DIM = 64
PIECE = 256
LOG2E = 1.4426950408889634
LOW = jnp.bfloat16
F32 = jnp.float32
HIDE = -1e30
NT = (((1,), (1,)), ((), ()))
TN = (((0,), (0,)), ((), ()))


def mm(a, b, dims=(((1,), (0,)), ((), ()))):
    return lax.dot_general(a, b, dims, preferred_element_type=F32)


COST_SHARE = 1.0


def cost(flops, moved):
    return pl.CostEstimate(flops=int(flops * COST_SHARE), bytes_accessed=int(moved * COST_SHARE), transcendentals=0)


def split_three(x):
    hi = x.astype(LOW)
    rest = x - hi.astype(F32)
    mid = rest.astype(LOW)
    return hi, mid, (rest - mid.astype(F32)).astype(LOW)


def scan_rows(x, reverse):
    length = x.shape[1]
    row = lax.broadcasted_iota(jnp.int32, (PIECE, PIECE), 0)
    col = lax.broadcasted_iota(jnp.int32, (PIECE, PIECE), 1)
    tri = jnp.where(row >= col if reverse else row <= col, 1.0, 0.0).astype(LOW)
    count = length // PIECE
    out = [None] * count
    carry = None
    for b in reversed(range(count)) if reverse else range(count):
        part = x[:, b * PIECE:(b + 1) * PIECE]
        done = sum(mm(t, tri) for t in split_three(part))
        if carry is not None:
            done = done + carry
        out[b] = done
        carry = done[:, :1] if reverse else done[:, PIECE - 1:]
    return jnp.concatenate(out, axis=1)


def log_gate(zf):
    return jnp.minimum(zf, 0.0) - jnp.log1p(jnp.exp(-jnp.abs(zf)))


def attn_fwd_kernel(start, size, q_ref, k_ref, v_ref, zf_ref, o_ref, lse_ref, *, hb):
    s_at = pl.program_id(0)
    length, width = q_ref.shape
    count = length // PIECE
    first, extent = start[s_at], size[s_at]
    c_rows = scan_rows(log_gate(zf_ref[...]), False) * LOG2E
    c_cols = c_rows.T
    row = lax.broadcasted_iota(jnp.int32, (PIECE, PIECE), 0)
    col = lax.broadcasted_iota(jnp.int32, (PIECE, PIECE), 1)
    causal = col <= row
    lane = lax.broadcasted_iota(jnp.int32, (1, width), 1)
    mine = [(lane >= h * HEAD_DIM) & (lane < (h + 1) * HEAD_DIM) for h in range(hb)]
    spare = [((h + 1) % hb) * HEAD_DIM for h in range(hb)]
    if lse_ref.shape[0] > hb:
        lse_ref[...] = jnp.zeros(lse_ref.shape, F32)

    def block(i, wide):
        lo, hi = i * PIECE, (i + 1) * PIECE
        in_pic = (lo >= first) & (lo < first + extent)
        out, lse = None, None
        for h in range(hb):
            q = jnp.where(mine[h], q_ref[lo:hi, :], jnp.zeros((), LOW))
            c_row = c_rows[h:h + 1, :]
            c_col = c_cols[lo:hi, h:h + 1]
            base = c_row[:, lo:lo + 1]
            parts, spans = [], []
            if i:
                parts.append(mm(q, k_ref[0:lo, :], NT) + (base - c_row[:, :lo]))
                spans.append((0, lo))
            back = base - 2.0 * c_col
            other = jnp.where(in_pic, back + c_row[:, lo:hi], HIDE)
            parts.append(mm(q, k_ref[lo:hi, :], NT) + jnp.where(causal, base - c_row[:, lo:hi], other))
            spans.append((lo, hi))
            if wide:
                parts.append(mm(q, k_ref[hi:hi + PIECE, :], NT) + (back + c_row[:, hi:hi + PIECE]))
                spans.append((hi, hi + PIECE))
            peak = functools.reduce(jnp.maximum, [jnp.max(p, axis=1, keepdims=True) for p in parts])
            acc = None
            for p, (a, b) in zip(parts, spans):
                v = jnp.where(mine[h], v_ref[a:b, :], jnp.ones((), LOW))
                t = mm(jnp.exp2(p - peak).astype(LOW), v)
                acc = t if acc is None else acc + t
            total = acc[:, spare[h]:spare[h] + 1]
            o_h = acc / total
            l_h = jnp.broadcast_to(peak + jnp.log2(total), o_h.shape)
            out = o_h if out is None else jnp.where(mine[h], o_h, out)
            lse = l_h if lse is None else jnp.where(mine[h], l_h, lse)
        o_ref[lo:hi, :] = out
        turned = lse.T
        for h in range(hb):
            lse_ref[h:h + 1, lo:hi] = turned[h * HEAD_DIM:h * HEAD_DIM + 1, :]

    for i in range(count):
        if i + 1 < count:
            wide = (first == i * PIECE) & (extent > PIECE)
            pl.when(wide)(functools.partial(block, i, True))
            pl.when(jnp.logical_not(wide))(functools.partial(block, i, False))
        else:
            block(i, False)


def attn_bwd_kernel(start, size, q_ref, k_ref, v_ref, zf_ref, lse_ref, o_ref, do_ref,
                    dq_ref, dk_ref, dv_ref, dzf_ref, dk_acc, dv_acc, dc_acc, *, hb):
    s_at = pl.program_id(0)
    length, width = q_ref.shape
    count = length // PIECE
    first, extent = start[s_at], size[s_at]
    zf = zf_ref[...]
    c_rows = scan_rows(log_gate(zf), False) * LOG2E
    c_cols = c_rows.T
    row = lax.broadcasted_iota(jnp.int32, (PIECE, PIECE), 0)
    col = lax.broadcasted_iota(jnp.int32, (PIECE, PIECE), 1)
    causal = row <= col
    lane = lax.broadcasted_iota(jnp.int32, (1, width), 1)
    mine = [(lane >= h * HEAD_DIM) & (lane < (h + 1) * HEAD_DIM) for h in range(hb)]
    spare = [((h + 1) % hb) * HEAD_DIM for h in range(hb)]
    zero, one = jnp.zeros((), LOW), jnp.ones((), LOW)
    dk_acc[...] = jnp.zeros(dk_acc.shape, F32)
    dv_acc[...] = jnp.zeros(dv_acc.shape, F32)
    prod = do_ref[...].astype(F32) * o_ref[...].astype(F32)
    head_row = lax.broadcasted_iota(jnp.int32, (8, width), 0)
    head_lane = lax.broadcasted_iota(jnp.int32, (8, width), 1)
    pick = jnp.where((head_lane >= head_row * HEAD_DIM) & (head_lane < (head_row + 1) * HEAD_DIM), 1.0, 0.0).astype(LOW)
    p_hi = prod.astype(LOW)
    p_lo = (prod - p_hi.astype(F32)).astype(LOW)
    delta = mm(pick, p_hi, NT) + mm(pick, p_lo, NT)

    heads = range(hb)
    parts_of = [slice(h * PIECE, (h + 1) * PIECE) for h in heads]
    causal_all = jnp.concatenate([causal] * hb, axis=1)

    def side(xs):
        return jnp.concatenate(xs, axis=1)

    def block(i, wide):
        lo, hi = i * PIECE, (i + 1) * PIECE
        in_pic = (lo >= first) & (lo < first + extent)
        q_all, do_all = q_ref[lo:hi, :], do_ref[lo:hi, :]
        q = jnp.concatenate([jnp.where(m, q_all, zero) for m in mine], axis=0)
        do = jnp.concatenate([jnp.where(m, do_all, zero) for m in mine], axis=0)
        c_row = [c_rows[h:h + 1, lo:hi] for h in heads]
        lse = side([lse_ref[h:h + 1, lo:hi] for h in heads])
        dl = side([delta[h:h + 1, lo:hi] for h in heads])
        base = side([jnp.broadcast_to(c[:, :1], (1, PIECE)) for c in c_row])
        ahead = base - lse
        back = ahead - 2.0 * side(c_row)
        acc = [None] * hb
        todo = ([(0, lo, 0)] if i else []) + [(lo, hi, 1)] + ([(hi, hi + PIECE, 2)] if wide else [])
        for a, b, kind in todo:
            c_col = side([jnp.broadcast_to(c_cols[a:b, h:h + 1], (b - a, PIECE)) for h in heads])
            st = mm(k_ref[a:b, :], q, NT)
            if kind == 0:
                st = st + (ahead - c_col)
            elif kind == 1:
                st = st + jnp.where(causal_all, ahead - c_col, jnp.where(in_pic, back + c_col, HIDE))
            else:
                st = st + (back + c_col)
            p = jnp.exp2(st)
            ds_all = (p * (mm(v_ref[a:b, :], do, NT) - dl)).astype(LOW)
            dv_acc[a:b, :] += mm(p.astype(LOW), do)
            mark = -one if kind == 2 else one
            for h in heads:
                ds = ds_all[:, parts_of[h]]
                dk_acc[h, a:b, :] += mm(ds, jnp.where(mine[h], q_all, mark))
                t = mm(ds, jnp.where(mine[h], k_ref[a:b, :], mark), TN)
                acc[h] = t if acc[h] is None else acc[h] + t
                if kind == 1:
                    def signs(ds=ds, h=h):
                        minus = jnp.where(causal, zero, ds)
                        m2 = jnp.where(mine[h], zero, jnp.full((), -2.0, LOW))
                        m2 = jnp.broadcast_to(m2, (PIECE, width))
                        dk_acc[h, lo:hi, :] += mm(minus, m2)
                        dc_acc[h] = mm(minus, m2, TN)
                    def none(h=h):
                        dc_acc[h] = jnp.zeros((PIECE, width), F32)
                    pl.when(in_pic)(signs)
                    pl.when(jnp.logical_not(in_pic))(none)
                    acc[h] = acc[h] + dc_acc[h]
        out = acc[0]
        for h in heads:
            out = jnp.where(mine[h], acc[h], out)
            dzf_ref[h:h + 1, lo:hi] = acc[h].T[spare[h]:spare[h] + 1, :]
        dq_ref[lo:hi, :] = (out * HEAD_DIM ** -0.5).astype(LOW)

    if dzf_ref.shape[0] > hb:
        dzf_ref[...] = jnp.zeros(dzf_ref.shape, F32)
    for i in range(count):
        if i + 1 < count:
            wide = (first == i * PIECE) & (extent > PIECE)
            pl.when(wide)(functools.partial(block, i, True))
            pl.when(jnp.logical_not(wide))(functools.partial(block, i, False))
        else:
            block(i, False)
    dv_ref[...] = dv_acc[...].astype(LOW)
    dk = dk_acc[0]
    for h in range(1, hb):
        dk = jnp.where(mine[h], dk_acc[h], dk)
    dk_ref[...] = (dk * (1.0 / LOG2E)).astype(LOW)
    for h in range(hb):
        turned = dk_acc[h].T
        dzf_ref[h:h + 1, :] -= turned[spare[h]:spare[h] + 1, :]
    dlog = scan_rows(dzf_ref[...], True)
    dzf_ref[...] = (dlog * jax.nn.sigmoid(-zf)).astype(LOW).astype(F32)


def head_shapes(width):
    heads = width // HEAD_DIM
    hb = 2 if heads % 2 == 0 else heads
    return hb, heads // hb, hb * HEAD_DIM


def head_specs(qkv, seqs, first=0):
    tokens, width = qkv.shape[0], qkv.shape[1] // 3
    hb, pairs, bw = head_shapes(width)
    length = tokens // seqs

    def col(off):
        return pl.BlockSpec((length, bw), lambda s, p, *_: (s, off + p))

    def rows(off):
        return pl.BlockSpec((None, 8, length), lambda s, p, *_: (off + p, 0, s))

    if bw % 128:
        three, cols = [qkv[:, j * width:(j + 1) * width] for j in range(3)], [col(first)] * 3
    else:
        three, cols = [qkv] * 3, [col(j * pairs + first) for j in range(3)]
    return three, cols, col, rows


def attend(start, size, qkv, zf, seqs):
    tokens, width = qkv.shape[0], qkv.shape[1] // 3
    hb, pairs, bw = head_shapes(width)
    three, cols, col, rows = head_specs(qkv, seqs)
    work = tokens * tokens // seqs * width // HEAD_DIM
    return pl.pallas_call(
        functools.partial(attn_fwd_kernel, hb=hb),
        grid_spec=pltpu.PrefetchScalarGridSpec(
            num_scalar_prefetch=2,
            grid=(seqs, pairs),
            in_specs=cols + [rows(0)],
            out_specs=[col(0), rows(0)],
        ),
        out_shape=[
            jax.ShapeDtypeStruct((tokens, width), F32),
            jax.ShapeDtypeStruct((pairs, 8, tokens), F32),
        ],
        compiler_params=pltpu.CompilerParams(vmem_limit_bytes=40 * 2**20),
        cost_estimate=cost(1600 * work, tokens * width * 10),
        name="attend",
    )(start, size, *three, zf)


def attend_back(start, size, qkv, zf, lse, core, up, seqs, first, count):
    tokens, width = qkv.shape[0], qkv.shape[1] // 3
    hb, pairs, bw = head_shapes(width)
    length = tokens // seqs
    three, cols, col, rows = head_specs(qkv, seqs, first)
    work = tokens * tokens // seqs * hb * count
    return pl.pallas_call(
        functools.partial(attn_bwd_kernel, hb=hb),
        grid_spec=pltpu.PrefetchScalarGridSpec(
            num_scalar_prefetch=2,
            grid=(seqs, count),
            in_specs=cols + [rows(first), rows(first), col(first), col(first)],
            out_specs=[col(0)] * 3 + [rows(0)],
            scratch_shapes=[
                pltpu.VMEM((hb, length, bw), F32),
                pltpu.VMEM((length, bw), F32),
                pltpu.VMEM((hb, PIECE, bw), F32),
            ],
        ),
        out_shape=[jax.ShapeDtypeStruct((tokens, count * bw), LOW)] * 3
        + [jax.ShapeDtypeStruct((count, 8, tokens), F32)],
        compiler_params=pltpu.CompilerParams(vmem_limit_bytes=40 * 2**20),
        cost_estimate=cost(2600 * work, tokens * count * bw * 20),
        name="attend_back",
    )(start, size, *three, zf, lse, core, up)


BLOCK = 256


class Pieces:
    def __init__(self, half, count, rows):
        self.half, self.count, self.rows = half, count, rows
        self.block = min(BLOCK, rows)
        self.each = rows // self.block
        self.steps = count * self.each

    def first(self, p):
        return (self.count - 1 - p) * self.each

    def inside(self, p, i):
        return jnp.clip(i - self.first(p), 0, self.each - 1)

    def active(self, p, i):
        return (i >= self.first(p)) & (i < self.first(p) + self.each)

    def own_spec(self, p, n):
        return pl.BlockSpec((self.block, n), lambda i, *_: (self.inside(p, i), 0))

    def own_specs(self, n):
        return [self.own_spec(p, n) for p in range(self.count)]

    def true_at(self, i, half):
        return half[self.count - 1 - lax.div(i, self.each)] * self.each + lax.rem(i, self.each)

    def true_spec(self, n):
        return pl.BlockSpec((self.block, n), lambda i, half: (self.true_at(i, half), 0))

    def lane_spec(self, lead):
        return pl.BlockSpec(lead + (self.block,), lambda i, half: (0,) * len(lead) + (self.true_at(i, half),))

    def flat_spec(self, n):
        return pl.BlockSpec(
            (self.block, n),
            lambda i, *_: ((self.count - 1 - lax.div(i, self.each)) * self.each + lax.rem(i, self.each), 0),
        )

    def pick(self, refs, i):
        x = refs[0][...]
        for p in range(1, self.count):
            x = jnp.where(self.active(p, i), refs[p][...], x)
        return x

    def put(self, refs, i, value):
        for p in range(self.count):
            def write(p=p):
                refs[p][...] = value
            pl.when(self.active(p, i))(write)

    def shapes(self, n, dtype=LOW):
        return [jax.ShapeDtypeStruct((self.rows, n), dtype)] * self.count

    def all_rows(self):
        return self.count * self.rows

    def call(self, kernel, name, ins, in_specs, out_shapes, out_specs, flops):
        moved = sum(x.size * x.dtype.itemsize for x in ins) + sum(s.size * s.dtype.itemsize for s in out_shapes)
        return pl.pallas_call(
            kernel,
            grid_spec=pltpu.PrefetchScalarGridSpec(
                num_scalar_prefetch=1, grid=(self.steps,), in_specs=in_specs, out_specs=out_specs
            ),
            out_shape=out_shapes,
            compiler_params=pltpu.CompilerParams(vmem_limit_bytes=48 * 2**20),
            cost_estimate=cost(flops * 3 // 2, moved),
            name=name,
        )(self.half, *ins)


def whole(rows, n, at=0):
    return pl.BlockSpec((rows, n), lambda *_: (0, at), pipeline_mode=pl.Buffered(1))


def project(pc, xs, w, wf, bias, width):
    dims = w.shape[0]
    pairs = wf.shape[0] // 8

    def kernel(half, *refs):
        i = pl.program_id(0)
        w_ref, wf_ref, bias_ref, qkv_ref, sig_ref, zf_ref = refs[pc.count:]
        x = pc.pick(refs[:pc.count], i)
        q = mm(x, w_ref[:, :width]) * (HEAD_DIM**-0.5 * LOG2E)
        qkv_ref[:, :width] = q.astype(LOW)
        qkv_ref[:, width:] = mm(x, w_ref[:, width:3 * width]).astype(LOW)
        sig_ref[...] = jax.nn.sigmoid(mm(x, w_ref[:, 3 * width:]))
        z = mm(wf_ref[...], x, NT) + bias_ref[...]
        for p in range(pairs):
            zf_ref[p] = z[8 * p:8 * p + 8, :]

    rows = pc.all_rows()
    return pc.call(
        kernel, "project",
        list(xs) + [w, wf, bias],
        pc.own_specs(dims) + [whole(dims, 4 * width), whole(8 * pairs, dims), whole(8 * pairs, 1)],
        [
            jax.ShapeDtypeStruct((rows, 3 * width), LOW),
            jax.ShapeDtypeStruct((rows, width), F32),
            jax.ShapeDtypeStruct((pairs, 8, rows), F32),
        ],
        [pc.true_spec(3 * width), pc.true_spec(width), pc.lane_spec((pairs, 8))],
        8 * rows * dims * width,
    )


def close(pc, core, sig, w_out):
    dims, width = w_out.shape

    def kernel(half, core_ref, sig_ref, w_ref, gated_ref, *parts):
        g = (core_ref[...] * sig_ref[...]).astype(LOW)
        gated_ref[...] = g
        pc.put(parts, pl.program_id(0), mm(g, w_ref[...], NT).astype(LOW))

    rows = pc.all_rows()
    out = pc.call(
        kernel, "close",
        [core, sig, w_out],
        [pc.true_spec(width), pc.true_spec(width), whole(dims, width)],
        [jax.ShapeDtypeStruct((rows, width), LOW)] + pc.shapes(dims),
        [pc.flat_spec(width)] + pc.own_specs(dims),
        2 * rows * dims * width,
    )
    return out[0], out[1:]


def feed(pc, xs, ys, w):
    dims, hidden = w.shape[0], w.shape[1] // 3
    n = pc.count

    def kernel(half, *refs):
        i = pl.program_id(0)
        w_ref, hidden_ref, grad_ref = refs[2 * n:2 * n + 3]
        x, y = pc.pick(refs[:n], i), pc.pick(refs[n:2 * n], i)
        a = mm(x, w_ref[:, :hidden])
        sig = jax.nn.sigmoid(a)
        silu = a * sig
        b = mm(x, w_ref[:, hidden:2 * hidden])
        hidden_ref[...] = (silu * b).astype(LOW)
        gh = mm(y, w_ref[:, 2 * hidden:])
        grad_ref[:, :hidden] = (gh * b * sig * (1.0 + a * (1.0 - sig))).astype(LOW)
        grad_ref[:, hidden:] = (gh * silu).astype(LOW)
        pc.put(refs[2 * n + 3:], i, mm(grad_ref[...], w_ref[:, :2 * hidden], NT).astype(LOW))

    rows = pc.all_rows()
    out = pc.call(
        kernel, "feed",
        list(xs) + list(ys) + [w],
        pc.own_specs(dims) * 2 + [whole(dims, 3 * hidden)],
        [jax.ShapeDtypeStruct((rows, hidden), LOW), jax.ShapeDtypeStruct((rows, 2 * hidden), LOW)] + pc.shapes(dims),
        [pc.flat_spec(hidden), pc.flat_spec(2 * hidden)] + pc.own_specs(dims),
        10 * rows * dims * hidden,
    )
    return out[0], out[1], out[2:]


def feed_out(pc, hidden, w):
    dims, n = w.shape[0], w.shape[1] // 3

    def kernel(half, hidden_ref, w_ref, *parts):
        pc.put(parts, pl.program_id(0), mm(hidden_ref[...], w_ref[...], NT).astype(LOW))

    return pc.call(
        kernel, "feed_out", [hidden, w], [pc.flat_spec(n), whole(dims, n, 2)],
        pc.shapes(dims), pc.own_specs(dims), 2 * pc.all_rows() * dims * n,
    )


def open_back(pc, ys, w_out, core, sig):
    dims, width = w_out.shape

    def kernel(half, *refs):
        w_ref, core_ref, sig_ref, up_ref, gate_ref = refs[pc.count:]
        g = mm(pc.pick(refs[:pc.count], pl.program_id(0)), w_ref[...])
        s = sig_ref[...]
        up_ref[...] = (g * s).astype(LOW)
        gate_ref[...] = (g * core_ref[...] * s * (1.0 - s)).astype(LOW)

    rows = pc.all_rows()
    return pc.call(
        kernel, "open_back",
        list(ys) + [w_out, core, sig],
        pc.own_specs(dims) + [whole(dims, width), pc.true_spec(width), pc.true_spec(width)],
        [jax.ShapeDtypeStruct((rows, width), LOW)] * 2,
        [pc.true_spec(width)] * 2,
        2 * rows * dims * width,
    )


def project_back(pc, grads, dz, w, wf, width):
    dims = w.shape[0]
    pairs = dz.shape[0]
    n = len(grads)

    def kernel(half, *refs):
        dz_ref, w_ref, wf_ref = refs[n:n + 3]
        g = jnp.concatenate([r[...] for r in refs[:n]], axis=1)
        total = mm(g, w_ref[...], NT)
        z = jnp.concatenate([dz_ref[p] for p in range(pairs)], axis=0).astype(LOW)
        total = total + mm(z, wf_ref[...], TN)
        pc.put(refs[n + 3:], pl.program_id(0), total.astype(LOW))

    return pc.call(
        kernel, "project_back",
        list(grads) + [dz, w, wf],
        [pc.true_spec(g.shape[1]) for g in grads]
        + [pc.lane_spec((pairs, 8)), whole(dims, 4 * width), whole(8 * pairs, dims)],
        pc.shapes(dims), pc.own_specs(dims), 8 * pc.all_rows() * dims * width,
    )


def weight_grads(pc, groups, name, step):
    dims = groups[0][0][0][0].shape[1]
    ins, specs, plan, at = [], [], [], 0
    flops = 0
    for group in groups:
        terms = []
        for lefts, (right, n, c), true in group:
            for p, left in enumerate(lefts):
                terms.append((len(ins), len(ins) + 1))
                ins += [left, right]
                specs.append(pl.BlockSpec((pc.rows, step), lambda i, *_: (0, i)))
                if true:
                    spec = pl.BlockSpec((pc.rows, n), lambda i, half, p=p, c=c: (half[p], c), pipeline_mode=pl.Buffered(1))
                else:
                    spec = pl.BlockSpec((pc.rows, n), lambda i, *_, p=p, c=c: (p, c), pipeline_mode=pl.Buffered(1))
                specs.append(spec)
                flops += 2 * pc.rows * dims * n
        plan.append((terms, at, n))
        at += n

    def kernel(half, *refs):
        out = refs[-1]
        for terms, at, n in plan:
            total = None
            for a, b in terms:
                t = mm(refs[a][...], refs[b][...], TN)
                total = t if total is None else total + t
            out[:, at:at + n] = total.astype(LOW)

    return pl.pallas_call(
        kernel,
        grid_spec=pltpu.PrefetchScalarGridSpec(
            num_scalar_prefetch=1, grid=(dims // step,), in_specs=specs,
            out_specs=pl.BlockSpec((step, at), lambda i, *_: (i, 0)),
        ),
        out_shape=jax.ShapeDtypeStruct((dims, at), LOW),
        compiler_params=pltpu.CompilerParams(vmem_limit_bytes=50 * 2**20),
        cost_estimate=cost(flops * 3 // 2, dims * at * 6),
        name=name,
    )(pc.half, *ins)


def project_grads(pc, chunks, size, tail, heads_each):
    dims = chunks[0][0][0].shape[1]
    step = 384
    per = step // size
    n = sum(g.shape[1] for g in chunks[0][1][0])
    cols = len(chunks[0][1])
    pairs = chunks[0][2].shape[0]
    ins, specs, plan = [], [], []
    for lefts, grads, dz in chunks:
        for p, left in enumerate(lefts):
            at, groups = len(ins), []
            ins.append(left)
            specs.append(pl.BlockSpec((pc.rows, step), lambda i, *_: (0, i)))
            for group in grads:
                groups.append(range(len(ins), len(ins) + len(group)))
                for g in group:
                    ins.append(g)
                    specs.append(
                        pl.BlockSpec(
                            (pc.rows, g.shape[1]), lambda i, half, p=p: (half[p], 0), pipeline_mode=pl.Buffered(1)
                        )
                    )
            plan.append((at, groups, len(ins)))
            ins.append(dz)
            specs.append(pl.BlockSpec((pairs, 8, pc.rows), lambda i, half, p=p: (0, 0, half[p])))

    def kernel(half, *refs):
        out = refs[-1]
        for c in range(cols):
            total = None
            for at, groups, _ in plan:
                right = [refs[j][...] for j in groups[c]]
                right = jnp.concatenate(right, axis=1) if len(right) > 1 else right[0]
                t = mm(refs[at][...], right, TN)
                total = t if total is None else total + t
            total = total.astype(LOW)
            for b in range(per):
                out[b, :size, c * n:(c + 1) * n] = total[b * size:(b + 1) * size]
        total = None
        for at, _, z_at in plan:
            z = jnp.concatenate([refs[z_at][p] for p in range(pairs)], axis=0).astype(LOW)
            t = mm(z, refs[at][...])
            total = t if total is None else total + t
        heads = [total[8 * p:8 * p + heads_each] for p in range(pairs)]
        heads.append(jnp.zeros((tail - heads_each * pairs, step), F32))
        total = jnp.concatenate(heads, axis=0)
        for b in range(per):
            row = total[:, b * size:(b + 1) * size]
            row = jnp.concatenate([row, jnp.zeros((tail, cols * n - size), F32)], axis=1)
            out[b, size:, :] = row.astype(LOW)

    return pl.pallas_call(
        kernel,
        grid_spec=pltpu.PrefetchScalarGridSpec(
            num_scalar_prefetch=1, grid=(dims // step,), in_specs=specs,
            out_specs=pl.BlockSpec((per, size + tail, cols * n), lambda i, *_: (i, 0, 0)),
        ),
        out_shape=jax.ShapeDtypeStruct((dims // size, size + tail, cols * n), LOW),
        compiler_params=pltpu.CompilerParams(vmem_limit_bytes=50 * 2**20),
        cost_estimate=cost(12 * pc.rows * dims * cols * n, dims * cols * n * 6),
        name="project_grads",
    )(pc.half, *ins)


def norm_grads(backs, own, values, gain, base, low):
    rows, dims = values.shape
    block = rows // 4
    per = rows // len(backs) // block
    n, m = len(backs), len(own)

    def kernel(*refs):
        i = pl.program_id(0)
        values_ref, gain_ref, base_ref = refs[n + m:n + m + 3]
        outs = refs[n + m + 3:]
        g = refs[0][...]
        for p in range(1, n):
            g = jnp.where(i >= p * per, refs[p][...], g)
        g = g.astype(F32)
        for r in refs[n:n + m]:
            g = g + r[...].astype(F32)
        v = values_ref[...].astype(F32)
        s = lax.rsqrt(jnp.mean(v * v, axis=1, keepdims=True) + 1e-05)
        normed = v * s
        scaled = g * gain_ref[...]
        total = base_ref[...].astype(F32) + s * (scaled - normed * jnp.mean(scaled * normed, axis=1, keepdims=True))
        outs[0][...] = total
        if low:
            outs[1][...] = total.astype(LOW)
        part = jnp.sum(g * normed, axis=0, keepdims=True)

        def start():
            outs[-1][...] = part

        def more():
            outs[-1][...] += part

        pl.when(i == 0)(start)
        pl.when(i > 0)(more)

    wide = pl.BlockSpec((block, dims), lambda i: (i, 0))
    row = pl.BlockSpec((1, dims), lambda i: (0, 0))
    parts = [pl.BlockSpec((block, dims), lambda i, p=p: (jnp.clip(i - p * per, 0, per - 1), 0)) for p in range(n)]
    return pl.pallas_call(
        kernel,
        grid=(4,),
        in_specs=parts + [wide] * (m + 1) + [row, wide],
        out_specs=[wide] * (2 if low else 1) + [row],
        out_shape=[jax.ShapeDtypeStruct((rows, dims), F32)]
        + ([jax.ShapeDtypeStruct((rows, dims), LOW)] if low else [])
        + [jax.ShapeDtypeStruct((1, dims), F32)],
        compiler_params=pltpu.CompilerParams(vmem_limit_bytes=32 * 2**20),
        cost_estimate=cost(0, rows * dims * 20),
        name="norm_grads",
    )(*backs, *own, values, gain.reshape(1, dims), base)


from jax.sharding import PartitionSpec as P

NORM_EPS = 1e-05
BETA_ONE = 0.9
BETA_TWO = 0.95
WEIGHT_DECAY = 0.1
ADAM_EPS = 1e-08
MAX_NORM = 1.0
STEP_COUNT = 10.0


def rms_scale(values):
    return lax.rsqrt(jnp.mean(values * values, axis=-1, keepdims=True) + NORM_EPS)


def adam_step(weight, gradient, first_old, second_old, clip_scale, decay_rate, width):
    learn_rate = 0.4 / width**0.5
    scaled = gradient * clip_scale
    first_new = BETA_ONE * first_old + (1.0 - BETA_ONE) * scaled
    second_new = BETA_TWO * second_old + (1.0 - BETA_TWO) * scaled * scaled
    update = (
        first_new
        / (1.0 - BETA_ONE**STEP_COUNT)
        / (jnp.sqrt(second_new / (1.0 - BETA_TWO**STEP_COUNT)) + ADAM_EPS)
    )
    return (-learn_rate * (update + decay_rate * weight), first_new, second_new)


def after(x, *done):
    return lax.optimization_barrier((x,) + done)[0]


def index(x, i, axis):
    return lax.dynamic_index_in_dim(x, i, axis, keepdims=False, allow_negative_indices=False)


class Ring:
    def __init__(self, axis, size):
        self.axis, self.size = axis, size
        if size == 8:
            self.table = list(range(0, size, 2)) + list(range(size - 1, 0, -2))
        else:
            self.table = list(range(size))
        spot = [self.table.index(i) for i in range(size)]
        ahead = [[self.table[(spot[i] + k) % size] for k in range(size)] for i in range(size)]
        self.ahead = index(jnp.asarray(ahead, jnp.int32), lax.axis_index(axis), 0)

    def step(self, x, way):
        n = self.size
        return lax.ppermute(x, self.axis, [(self.table[r], self.table[(r + way) % n]) for r in range(n)])

    def gather(self, x, way):
        return Gather(self, x, way)

    def reduce(self, x, way):
        return Reduce(self, x, way)


class Gather:
    def __init__(self, ring, x, way):
        self.ring, self.way, self.k = ring, way, 0
        self.blocks = {0: x}
        self.ends = [x, x]

    def step(self, *done):
        ring, n = self.ring, self.ring.size
        self.k += 1
        if self.k > 1 or done:
            self.ends = list(lax.optimization_barrier(tuple(self.ends) + done)[:2])
        self.ends[0] = ring.step(self.ends[0], self.way)
        self.blocks[-self.k * self.way % n] = self.ends[0]
        if self.k <= (n - 1) // 2:
            self.ends[1] = ring.step(self.ends[1], -self.way)
            self.blocks[self.k * self.way % n] = self.ends[1]
        return self.ends

    def all(self):
        while self.k < self.ring.size // 2:
            self.step()
        return [self.blocks[k] for k in range(self.ring.size)]


class Reduce:
    def __init__(self, ring, x, way):
        self.ring, self.x, self.k = ring, x, 0
        n = ring.size
        self.ways = ((way, n // 2), (-way, (n - 1) // 2))
        self.moving = [None, None]

    def block(self, k):
        return index(self.x, index(self.ring.ahead, k % self.ring.size, 0), 0)

    def step(self, *done):
        self.k += 1
        if self.k > 1:
            tied = lax.optimization_barrier(tuple(self.moving) + done)
            self.moving = list(tied[:2])
        for j, (way, far) in enumerate(self.ways):
            left = far - self.k + 1
            if left < 1:
                continue
            own = self.block(way * left)
            if self.k > 1:
                own = (self.moving[j].astype(F32) + own.astype(F32)).astype(LOW)
            self.moving[j] = self.ring.step(own, way)
        return self.moving

    def all(self):
        while self.k < self.ring.size // 2:
            self.step()
        return sum(m.astype(F32) for m in self.moving if m is not None) + self.block(0).astype(F32)


def sum_all(x, axis, size):
    bit = 1
    while bit < size:
        x = x + lax.ppermute(x, axis, [(i, i ^ bit) for i in range(size)])
        bit *= 2
    return x


def place_kernel(where, *refs, arrays, size, rows, tail):
    out, sem = refs[arrays], refs[-1]
    copies = []
    block = 0
    for ref in refs[:arrays]:
        for j in range(ref.shape[0] // size):
            spans = [(out, rows, j * size)] + ([(refs[arrays + 1], tail, j * size + rows)] if tail else [])
            for to, count, at in spans:
                to_at = pl.multiple_of(where[block] * count, count)
                copies.append(
                    pltpu.make_async_copy(
                        ref.at[pl.ds(at, count), :], to.at[pl.ds(to_at, count), :], sem.at[len(copies)]
                    )
                )
            block += 1
    for copy in copies:
        copy.start()
    for copy in copies:
        copy.wait()


def place(parts, where, size, tail=0):
    n = parts[0].shape[1]
    count = sum(p.shape[0] for p in parts) // size
    shapes = [jax.ShapeDtypeStruct((count * r, n), LOW) for r in (size - tail, tail) if r]
    out = pl.pallas_call(
        functools.partial(place_kernel, arrays=len(parts), size=size, rows=size - tail, tail=tail),
        in_specs=[pl.BlockSpec(memory_space=pltpu.SMEM)] + [pl.BlockSpec(memory_space=pl.ANY)] * len(parts),
        out_specs=[pl.BlockSpec(memory_space=pltpu.VMEM)] * len(shapes),
        out_shape=shapes,
        scratch_shapes=[pltpu.SemaphoreType.DMA((2 * count,))],
        compiler_params=pltpu.CompilerParams(vmem_limit_bytes=40 * 2**20),
        cost_estimate=cost(0, 4 * count * size * n),
        name="place",
    )(where, *parts)
    return out if tail else out[0]


def make_body(dp, tn):
    def body(
        inputs, cotangent, picture_start, picture_length,
        qkvg_weight, forget_weight, forget_bias, out_weight, gate_up, down_weight,
        attn_gain, feed_gain,
        qkvg_first, qkvg_second, forget_first, forget_second, bias_first, bias_second,
        out_first, out_second, gateup_first, gateup_second, down_first, down_second,
        attngain_first, attngain_second, feedgain_first, feedgain_second,
    ):
        dims = inputs.shape[1]
        local, rank_rows, width = inputs.shape[0], qkvg_weight.shape[1], qkvg_weight.shape[2]
        hidden_size = gate_up.shape[2]
        heads = forget_weight.shape[1]
        seqs = picture_start.shape[0]
        rows_group = local * tn
        length = rows_group // seqs
        data = Ring("dp", dp)
        rank = lax.axis_index("tensor")
        paired = tn == 4 and local * 2 == length
        core, side = lax.rem(rank, 2), lax.div(rank, 2)
        rows_each = dims // dp

        def swap(x, bit):
            return lax.ppermute(x, "tensor", [(i, i ^ bit) for i in range(tn)])

        def rows_start(x):
            if not paired:
                return [lax.all_gather(x, "tensor", axis=0, tiled=True)], None
            return [x, swap(x, 1)], swap(x, 2)

        def far(moved, *done):
            there = after(moved[1], *done) if done else moved[1]
            return [there, swap(there, 1)]

        def spread_far(parts, count=1):
            if not paired:
                return parts[0], [lax.psum_scatter(parts[0], "tensor", scatter_dimension=0, tiled=True)]
            both = (parts[0].astype(F32) + swap(parts[1], 1).astype(F32)).astype(LOW)
            came, size = [], local // count
            for k in range(count):
                came.append(swap(after(both[k * size:(k + 1) * size], *came[-1:]), 2))
            return both, came

        def spread_own(parts, *done):
            return [parts[0], swap(after(parts[1], *done), 1)] if paired else []

        def spread_sum(back, own):
            total = jnp.concatenate(back).astype(F32)
            for p in own:
                total = total + p.astype(F32)
            return total

        if paired:
            pc = Pieces(jnp.stack([core, 1 - core]).astype(jnp.int32), 2, local)
        else:
            pc = Pieces(jnp.zeros((1,), jnp.int32), 1, rows_group)

        if paired:
            order = [side, 1 - side]
            starts = [index(picture_start.reshape(2, 1), o, 0) for o in order]
            sizes = [index(picture_length.reshape(2, 1), o, 0) for o in order]
            seqs_each = 1
        else:
            starts, sizes, seqs_each = [picture_start], [picture_length], seqs
        chunks = len(starts)
        hb, pairs, _ = head_shapes(width)

        def flat(w):
            return w.transpose(1, 0, 2).reshape(w.shape[1], -1).astype(LOW)

        now = [()]

        def at(x):
            return after(x, *now[0])

        def done(*xs):
            now[0] = tuple(x for x in xs if x is not None)

        inputs_f = inputs.astype(F32)
        tail = 16
        forget_row = forget_weight.T.astype(LOW)
        forget_row = jnp.pad(forget_row, ((0, tail - heads), (0, 5 * width - rows_each)))
        pack = jnp.concatenate([flat(qkvg_weight), out_weight.T.astype(LOW)], axis=1)
        pack = jnp.concatenate([pack, forget_row])
        ring_one = data.gather(pack, 1)
        ring_one.step()
        scale_one = rms_scale(inputs_f)
        normed_one = after((inputs_f * scale_one * attn_gain).astype(LOW), pack)
        low_feed = jnp.concatenate([flat(after(gate_up, normed_one)), down_weight.T.astype(LOW)], axis=1)
        if paired:
            near, came = [normed_one, swap(normed_one, 1)], []
            for k in range(2):
                part = normed_one[k * local // 2:(k + 1) * local // 2]
                if k:
                    ring_one.step()
                    part = after(part, came[-1])
                    ring_one.step(came[-1])
                came.append(swap(part, 2))
            move_one = (near, jnp.concatenate(came))
        else:
            move_one = rows_start(normed_one)
        while ring_one.k < dp // 2 - 1:
            ring_one.step()
        early = tuple(ring_one.ends)
        blocks = ring_one.all()
        w_one, w_tail = place([after(blocks[0], low_feed)] + blocks[1:], data.ahead, rows_each + tail, tail)
        w_out = w_one[:, 4 * width:]
        w_forget = w_tail.reshape(dp, tail, -1)[:, :heads, :rows_each].transpose(1, 0, 2)
        w_forget = jnp.pad(w_forget.reshape(pairs, hb, dims), ((0, 0), (0, 8 - hb), (0, 0))).reshape(-1, dims)
        bias_local = index(forget_bias.reshape(tn, heads), rank, 0)
        bias_local = jnp.pad(bias_local.reshape(pairs, hb), ((0, 0), (0, 8 - hb))).reshape(-1, 1)
        w_feed = lax.all_gather(after(low_feed, *early), "dp", axis=0, tiled=True)
        done(w_one)
        rows_one = [move_one[0]]
        if paired:
            rows_one.append(far(move_one))
        move_feed = rows_start(after(cotangent, rows_one[-1][0]))

        qkv, zf, attended, gate_sig, gated = ([None] * chunks for _ in range(5))
        for i in range(chunks):
            first = at(rows_one[i][0])
            qkv[i], gate_sig[i], zf[i] = project(pc, [first] + rows_one[i][1:], w_one, w_forget, bias_local, width)
            done(qkv[i])
        back, own = None, []
        feed_grad = [move_feed[0]]
        for i in reversed(range(chunks)):
            attended[i] = attend(starts[i], sizes[i], at(qkv[i]), zf[i], seqs_each)
            done(attended[i][0])
            gated[i], parts = close(pc, at(attended[i][0]), gate_sig[i], w_out)
            if back is None:
                sent, back = spread_far(parts)
                if paired:
                    feed_grad.append(far(move_feed))
                done(sent, feed_grad[-1][-1])
            else:
                own = spread_own(parts, back[0])
                done(gated[i], *own)
        middle = inputs_f + spread_sum(back, own)
        scale_two = rms_scale(middle)
        normed_two = (middle * scale_two * feed_gain).astype(LOW)
        move_two = rows_start(normed_two)

        hidden, grad_act, rows_two = ([None] * chunks for _ in range(3))
        done(w_feed)
        for i in range(chunks):
            rows_two[i] = far(move_two, *now[0]) if i else move_two[0]
            hidden[i], grad_act[i], parts = feed(
                pc, [at(rows_two[i][0])] + rows_two[i][1:], feed_grad[i], w_feed
            )
            done(hidden[i])
            if i == 0:
                own = spread_own(parts)
                done(hidden[i], *own)
            if i == chunks - 1:
                sent, back = spread_far(parts)
                done(sent)
        lefts = [[at(r[0])] + r[1:] for r in rows_two]
        groups = [
            [(r, (g, 2 * hidden_size, 0), False) for r, g in zip(lefts, grad_act)],
            [(y, (h, hidden_size, 0), False) for y, h in zip(feed_grad, hidden)],
        ]
        grad_feed = weight_grads(pc, groups, "grad_feed", 256)
        done(grad_feed)
        shard_feed = lax.psum_scatter(after(grad_feed, back[0]), "dp", scatter_dimension=0, tiled=True)
        grad_middle, grad_low, gain_two_grad = norm_grads(
            [after(back[0], grad_feed)], own, middle, feed_gain, cotangent, True
        )
        done(grad_low)
        move_back = rows_start(grad_low)
        out_parts = [None] * chunks
        out_parts[-1] = feed_out(pc, at(hidden[-1]), w_feed)
        done(out_parts[-1][0])

        grad_gatepre, grad_proj, grad_zf, attn_grad = ([None] * chunks for _ in range(4))
        for i in range(chunks):
            attn_grad[i] = far(move_back, grad_proj[i - 1][0]) if i else move_back[0]
            up_stream, grad_gatepre[i] = open_back(
                pc, [at(attn_grad[i][0])] + attn_grad[i][1:], w_out, attended[i][0], gate_sig[i]
            )
            done(up_stream)
            if i == chunks - 1:
                groups = [
                    [([at(r[0])] + r[1:], (g, width, 0), True) for r, g in zip(rows_one, grad_gatepre)],
                    [(y, (g, width, 0), False) for y, g in zip(attn_grad, gated)],
                ]
                grad_go = weight_grads(pc, groups, "grad_gate_out", 512)
                done(grad_go)
                ring_go = data.reduce(grad_go.reshape(dp, rows_each, -1), 1)
                ring_go.step()
                sent, out_back = spread_far([after(p, attn_grad[i][-1]) for p in out_parts[-1]])
                done(grad_go, sent)
            *grad_proj[i], grad_zf[i] = attend_back(
                starts[i], sizes[i], qkv[i], zf[i], attended[i][1], attended[i][0], at(up_stream), seqs_each, 0, pairs
            )
            grad_proj[i] = [[g] for g in grad_proj[i]]
            done(grad_proj[i][0][0])
            if i < chunks - 1:
                out_parts[i] = feed_out(pc, at(hidden[i]), w_feed)
                done(out_parts[i][0])

        def going():
            return [m for m in ring_go.moving if m is not None]

        bias_local_grad = sum(jnp.sum(z[:, :hb], axis=2).reshape(heads) for z in grad_zf)
        done(grad_proj[-1][0][0], *going(), *out_back)
        ring_go.step(grad_proj[-1][0][0])

        def rows_back(i):
            g = [x for group in grad_proj[i] for x in group]
            return project_back(pc, [at(g[0])] + g[1:] + [grad_gatepre[i]], grad_zf[i], w_one, w_forget, width)

        parts = rows_back(chunks - 1)
        sent, back = spread_far(parts, 2)
        done(sent)
        packed = project_grads(
            pc, [([at(r[0])] + r[1:], g, z) for r, g, z in zip(rows_one, grad_proj, grad_zf)], rows_each, tail, hb
        )
        packed = after(packed, back[0], *going())
        ring_go.step(packed)
        ring_qkv = data.reduce(packed, -1)
        ring_qkv.step()
        own = []
        if paired:
            done(packed)
            parts = rows_back(0)
            own = spread_own(parts, back[-1])
            outputs = after(middle, parts[0]) + spread_sum(out_back, spread_own(out_parts[0]))
            ring_qkv.step(parts[0], *going())
            ring_go.step(parts[0])
            shard_feed = after(shard_feed, outputs).astype(F32)
            square_feed = jnp.sum(shard_feed * shard_feed)
            ring_qkv.step(outputs, *going())
        else:
            outputs = middle + spread_sum(out_back, [])
            shard_feed = shard_feed.astype(F32)
            square_feed = jnp.sum(shard_feed * shard_feed)
        shard_up, shard_down = shard_feed[:, :2 * hidden_size], shard_feed[:, 2 * hidden_size:]
        input_grad, gain_one_grad = norm_grads(back, own, inputs, attn_gain, grad_middle, False)
        while ring_go.k < dp // 2:
            ring_go.step()
        shard_go = ring_go.all()
        square_go = jnp.sum(shard_go * shard_go)
        ring_qkv.step(square_feed, gain_one_grad)
        shard_gate, shard_out = shard_go[:, :width], shard_go[:, width:]
        shard_qkv = ring_qkv.all()
        shard_forget = shard_qkv[rows_each:rows_each + heads, :rows_each].T
        shard_qkv = shard_qkv[:rows_each]
        bias_full = jnp.where(jnp.arange(tn)[:, None] == rank, bias_local_grad[None], 0.0).reshape(-1)
        square = square_feed + square_go + sum(jnp.sum(s * s) for s in (shard_qkv, shard_forget))
        pad = 128 - forget_bias.shape[0] - 1
        packed = jnp.concatenate([gain_one_grad[0], gain_two_grad[0], bias_full, square[None], jnp.zeros((pad,), F32)])
        packed = sum_all(sum_all(packed.reshape(-1, 128), "tensor", tn), "dp", dp).reshape(-1)
        gain_one_sum, gain_two_sum = packed[:dims], packed[dims:2 * dims]
        bias_sum = packed[2 * dims:2 * dims + forget_bias.shape[0]]
        total = (
            packed[2 * dims + forget_bias.shape[0]]
            + jnp.sum(gain_one_sum * gain_one_sum)
            + jnp.sum(gain_two_sum * gain_two_sum)
            + jnp.sum(bias_sum * bias_sum)
        )
        grad_norm = jnp.sqrt(total)
        clip_scale = jnp.minimum(1.0, MAX_NORM / (grad_norm + 1e-06))

        def unflat(s, parts):
            return s.reshape(s.shape[0], parts, -1).transpose(1, 0, 2)

        def adam(weight, gradient, first_old, second_old, decay):
            return adam_step(weight, gradient, first_old, second_old, clip_scale, decay, dims)

        grad_attn = unflat(jnp.concatenate([shard_qkv, shard_gate], axis=1), 4)
        return (
            (outputs, input_grad, grad_norm)
            + adam(qkvg_weight, grad_attn, qkvg_first, qkvg_second, WEIGHT_DECAY)
            + adam(forget_weight, shard_forget, forget_first, forget_second, WEIGHT_DECAY)
            + adam(forget_bias, bias_sum, bias_first, bias_second, 0.0)
            + adam(out_weight, shard_out.T, out_first, out_second, WEIGHT_DECAY)
            + adam(gate_up, unflat(shard_up, 2), gateup_first, gateup_second, WEIGHT_DECAY)
            + adam(down_weight, shard_down.T, down_first, down_second, WEIGHT_DECAY)
            + adam(attn_gain, gain_one_sum, attngain_first, attngain_second, 0.0)
            + adam(feed_gain, gain_two_sum, feedgain_first, feedgain_second, 0.0)
        )

    return body


def solution(mesh):
    tokens = P(("dp", "tensor"), None)
    stack, tall, wide = P(None, "dp", "tensor"), P("dp", "tensor"), P("tensor", "dp")
    return jax.shard_map(
        make_body(mesh.shape["dp"], mesh.shape["tensor"]),
        mesh=mesh,
        in_specs=(tokens, tokens, P("dp"), P("dp"), stack, tall, P(), wide, stack, wide, P(), P())
        + (stack, stack, tall, tall, P(), P(), wide, wide, stack, stack, wide, wide, P(), P(), P(), P()),
        out_specs=(tokens, tokens, P())
        + (stack,) * 3 + (tall,) * 3 + (P(),) * 3 + (wide,) * 3 + (stack,) * 3 + (wide,) * 3 + (P(),) * 6,
        check_vma=False,
    )
```
